512 devices in a mesh: dp: 2 (over x_hi), context: 32 (over x_lo, z, core), embodime: 8 (over y).
Axes of the slice: x: 4 (x_hi: 2, x_lo: 2; x = x_hi * 2 + x_lo), y: 8, z: 8, core: 2. Of those that a mesh axis runs over, the one named last changes fastest.
Arguments:
- query_tokens: bfloat16 [2, 8, 4096, 2560], P('dp', 'embodime', 'context'), may hold values from -40 to 40
- key_tokens: bfloat16 [2, 8, 4096, 2560], P('dp', 'embodime', 'context'), may hold values from -8 to 8
- value_tokens: bfloat16 [2, 8, 4096, 2560], P('dp', 'embodime', 'context'), may hold values from -6 to 6
- out_grad: bfloat16 [2, 8, 4096, 2560], P('dp', 'embodime', 'context'), may hold values from -6 to 6
- actions: bfloat16 [2, 8, 4096, 128], P('dp', 'embodime', 'context'), may hold values from -6 to 6
- clip_lengths: int32 [2, 8, 16], P('dp', 'embodime'), may hold values from 1 to 3, 32 in all within a row
- clip_robots: int32 [2, 8, 16], P('dp', 'embodime'), may hold values from 0 to 3
- adapters: bfloat16 [8, 4, 128, 64], P('embodime'), may hold values from -0.5 to 0.5
- up_proj: bfloat16 [64, 2560], replicated, may hold values from -0.75 to 0.75
Outputs:
- key_grad: bfloat16 [2, 8, 4096, 2560], P('dp', 'embodime', 'context')
- value_grad: bfloat16 [2, 8, 4096, 2560], P('dp', 'embodime', 'context')
- adapter_grad: float32 [8, 4, 128, 64], P('embodime')
- up_grad: float32 [64, 2560], replicated
The draws below stay inside these ranges and needn't reach their ends.
Inputs may be any that keep to these rules, and one draw needn't show every extreme that they name: `clip_lengths`: each row sums to 32 and its largest entry is exactly 3.
All inputs are finite; a program needn't handle non-finite values.
Results may differ from the reference program's by a relative error of at most 0.0076.
Values may be sent and summed in bfloat16 or wider, within the bound.
No kernel may reach another device: no remote copies, remote signals or barrier semaphores. Data moves between devices by JAX's collectives and lax.ppermute only.
A program may use at most 64 MiB of HBM per device.

```python
import math
import jax
import jax.numpy as jnp
import numpy as np
from jax import lax

HEADS = 20
HEAD_DIM = 128
FRAME_TOK = 128
ACT = 128
RANK = 64
ROBOTS = 4
FRAMES = 32
TOKENS = 4096
MAXCLIP = 3
CLIPS = 16
N_DP = 2
N_EMBODIME = 8


def key_field(key):
    base = jax.random.truncated_normal(jax.random.fold_in(key, 11), -6.0, 6.0, (N_DP, N_EMBODIME, TOKENS, HEADS * HEAD_DIM), jnp.float32)
    position = jnp.arange(TOKENS)[None, None, :, None]
    paired = (position % 37 == 1) & (position >= 37)
    return jnp.where(paired, base, base)


def draw_key_tokens(key, part):
    return key_field(key).astype(jnp.bfloat16)


def draw_query_tokens(key, part):
    key = jax.random.fold_in(key, 3)
    return jax.random.truncated_normal(key, -6.0, 6.0, (N_DP, N_EMBODIME, TOKENS, HEADS * HEAD_DIM), jnp.float32).astype(jnp.bfloat16)


def touch_ends(result, stream_key, least, largest):
    longest = result.shape.index(max(result.shape))
    spots = []
    for shift in (0, 1):
        where = [jax.random.randint(jax.random.fold_in(stream_key, axis), (), 0, length) for axis, length in enumerate(result.shape)]
        where[longest] = (where[longest] + shift) % result.shape[longest]
        spots.append(tuple(where))
    return result.at[spots[0]].set(least).at[spots[1]].set(largest)


def steps_of(stream_key, shape, cuts, low, high):
    loudness = 1.0
    for axis_at, blocks in cuts:
        heights = jax.random.uniform(jax.random.fold_in(jax.random.fold_in(stream_key, 6), axis_at), (blocks,), jnp.float32, low / len(cuts), high / len(cuts))
        loudness = loudness * jnp.repeat(jnp.exp(heights), shape[axis_at] // blocks).reshape((-1,) + (1,) * (len(shape) - 1 - axis_at))
    return loudness


def profile(count, total, reach, skew):
    portions = [(1 << 20) // math.isqrt(rank ** skew) + 1 for rank in range(2, count + 1)]
    rest, holding = total - reach - (count - 1), [1] * (count - 1)
    while rest > 0:
        movable = [i for i in range(count - 1) if holding[i] < reach]
        pool, left = sum([portions[i] for i in movable]), rest
        for i in movable:
            more = min(reach - holding[i], max(1, left * portions[i] // pool), rest)
            holding[i] = holding[i] + more
            rest = rest - more
    return np.array([reach] + holding)


def ragged(rng, count, total, bound, skew):
    if count == 2:
        one = jax.random.randint(rng, (), max(1, total - bound), min(bound, total - 1) + 1)
        return jnp.stack([one, total - one])
    lengths = jnp.asarray(profile(count, total, bound, skew), jnp.int32)
    pairs = (count - 1) // 2
    donor, taker = lengths[1:1 + 2 * pairs:2], lengths[2:2 + 2 * pairs:2]
    slack = jnp.minimum(donor - 1, bound - taker)
    moved = jax.random.randint(jax.random.fold_in(rng, 1), (pairs,), 0, 1 << 20) % (slack + 1)
    lengths = lengths.at[1:1 + 2 * pairs:2].set(donor - moved).at[2:2 + 2 * pairs:2].set(taker + moved)
    return lengths[jax.random.permutation(jax.random.fold_in(rng, 2), count)]


def normal_values(own_key, shape, scale, limit, shards=(), kind=jnp.bfloat16):
    entries = jax.random.normal(own_key, shape, jnp.float32) * scale
    if len(shards) > 0:
        entries = steps_of(own_key, shape, shards, -0.22, 0.18) * entries
    return jnp.clip(entries, min=-limit, max=limit).astype(kind)


def setup_inputs(seed: int = 0) -> dict:
    key_of = jax.random.split(jax.random.key(seed), 10)
    query_tokens = draw_query_tokens(jax.random.fold_in(key_of[9], 71), 0)
    key_tokens = draw_key_tokens(jax.random.fold_in(key_of[9], 71), 0)
    value_tokens = normal_values(key_of[2], (N_DP, N_EMBODIME, TOKENS, HEADS * HEAD_DIM), 1.0, 6.0, ((0, 2), (1, 8), (2, 32)))
    out_grad = normal_values(key_of[3], (N_DP, N_EMBODIME, TOKENS, HEADS * HEAD_DIM), 1.0, 6.0, ((0, 2), (1, 8), (2, 32)))
    actions = normal_values(key_of[4], (N_DP, N_EMBODIME, TOKENS, ACT), 1.0, 6.0, ((0, 2), (1, 8), (2, 32)))
    clip_lengths = jax.vmap(lambda own: ragged(own, CLIPS, FRAMES, MAXCLIP, 2))(jax.random.split(key_of[5], N_DP * N_EMBODIME)).reshape((N_DP, N_EMBODIME, CLIPS)).astype(jnp.int32)
    clip_robots = touch_ends(jax.random.randint(key_of[6], (N_DP, N_EMBODIME, CLIPS), 0, ROBOTS), jax.random.fold_in(key_of[6], 1), 0, ROBOTS - 1).astype(jnp.int32)
    adapters = normal_values(key_of[7], (N_EMBODIME, ROBOTS, ACT, RANK), ACT ** -0.5, 0.5, ((0, 8),))
    up_proj = normal_values(key_of[8], (RANK, HEADS * HEAD_DIM), RANK ** -0.5, 0.75)
    return dict(query_tokens=query_tokens, key_tokens=key_tokens, value_tokens=value_tokens, out_grad=out_grad, actions=actions, clip_lengths=clip_lengths, clip_robots=clip_robots, adapters=adapters, up_proj=up_proj)


HIGH = lax.Precision.HIGHEST


def rounded(values):
    return lax.optimization_barrier(values.astype(jnp.bfloat16)).astype(jnp.float32)


def shift_frames(values, offset):
    if offset == 0:
        return values
    filler = jnp.zeros((offset,) + values.shape[1:], values.dtype)
    return jnp.concatenate([filler, values[:-offset]], 0)


def back_frames(values, offset):
    filler = jnp.zeros((offset,) + values.shape[1:], values.dtype)
    return jnp.concatenate([values[offset:], filler], 0)


def one_batch(query_in, key_in, value_in, grad_in, action_in, length_row, robot_row, group_table, up_proj):
    width = HEADS * HEAD_DIM
    frame_ids = jnp.arange(FRAMES, dtype=jnp.int32)
    clip_ends = jnp.cumsum(length_row).astype(jnp.int32)
    clip_index = jnp.sum((clip_ends[None, :] <= frame_ids[:, None]).astype(jnp.int32), 1)
    clip_hot = clip_index[:, None] == jnp.arange(CLIPS, dtype=jnp.int32)[None, :]
    clip_start = jnp.sum(jnp.where(clip_hot, (clip_ends - length_row)[None, :], 0), 1)
    robot_index = jnp.sum(jnp.where(clip_hot, robot_row[None, :], 0), 1)
    robot_hot = (robot_index[:, None] == jnp.arange(ROBOTS, dtype=jnp.int32)[None, :]).astype(jnp.float32)
    robot_table = jnp.einsum("fr,rak->fak", robot_hot, group_table.astype(jnp.float32), precision=HIGH)
    action_rows = action_in.reshape(FRAMES, FRAME_TOK, ACT).astype(jnp.float32)
    adapted = jnp.einsum("fta,fak->ftk", action_rows, robot_table, precision=HIGH).astype(jnp.bfloat16)
    adapted_flat = adapted.reshape(TOKENS, RANK)
    query = (query_in + jnp.dot(adapted_flat, up_proj, preferred_element_type=jnp.float32)).astype(jnp.bfloat16)
    shape4 = (FRAMES, FRAME_TOK, HEADS, HEAD_DIM)
    query4 = query.reshape(shape4).astype(jnp.float32)
    keys4 = key_in.reshape(shape4).astype(jnp.float32)
    values4 = value_in.reshape(shape4).astype(jnp.float32)
    grads4 = grad_in.reshape(shape4).astype(jnp.float32)
    score_scale = HEAD_DIM ** -0.5
    scores = []
    products = []
    for offset in range(MAXCLIP):
        keys_d = shift_frames(keys4, offset)
        values_d = shift_frames(values4, offset)
        valid = (frame_ids - offset) >= clip_start
        raw = jnp.einsum("fqhe,fkhe->fhqk", query4, keys_d) * score_scale
        scores.append(jnp.where(valid[:, None, None, None], raw, -jnp.inf))
        products.append(jnp.einsum("fqhe,fkhe->fhqk", grads4, values_d))
    row_max = jnp.max(jnp.stack([jnp.max(block, -1) for block in scores]), 0)
    row_sum = sum(jnp.sum(jnp.exp(block - row_max[..., None]), -1) for block in scores)
    probs = [jnp.exp(block - row_max[..., None]) / row_sum[..., None] for block in scores]
    row_delta = sum(jnp.sum(prob * prod, -1) for prob, prod in zip(probs, products))
    query_grad = jnp.zeros(shape4, jnp.float32)
    key_total = jnp.zeros(shape4, jnp.float32)
    value_total = jnp.zeros(shape4, jnp.float32)
    for offset in range(MAXCLIP):
        keys_d = shift_frames(keys4, offset)
        dscore = rounded(probs[offset] * (products[offset] - row_delta[..., None]) * score_scale)
        prob_b = rounded(probs[offset])
        query_grad = query_grad + jnp.einsum("fhqk,fkhe->fqhe", dscore, keys_d)
        key_part = jnp.einsum("fhqk,fqhe->fkhe", dscore, query4)
        value_part = jnp.einsum("fhqk,fqhe->fkhe", prob_b, grads4)
        if offset == 0:
            key_total = key_total + key_part
            value_total = value_total + value_part
        else:
            key_total = key_total + back_frames(rounded(key_part), offset)
            value_total = value_total + back_frames(rounded(value_part), offset)
    query_flat = query_grad.reshape(TOKENS, width)
    adapted_grad = jnp.dot(query_flat, up_proj.astype(jnp.float32).T, precision=HIGH)
    up_term = jnp.dot(adapted_flat.astype(jnp.float32).T, query_flat, precision=HIGH)
    action_terms = jnp.einsum("fta,ftk->fak", action_rows, adapted_grad.reshape(FRAMES, FRAME_TOK, RANK), precision=HIGH)
    adapter_term = jnp.einsum("fr,fak->rak", robot_hot, action_terms, precision=HIGH)
    key_grad = key_total.reshape(TOKENS, width).astype(jnp.bfloat16)
    value_grad = value_total.reshape(TOKENS, width).astype(jnp.bfloat16)
    return key_grad, value_grad, up_term, adapter_term


def reference(query_tokens, key_tokens, value_tokens, out_grad, actions, clip_lengths, clip_robots, adapters, up_proj):
    batches = N_DP * N_EMBODIME
    width = HEADS * HEAD_DIM

    def flatten(array):
        return array.reshape((batches,) + array.shape[2:])

    groups = jnp.tile(jnp.arange(N_EMBODIME, dtype=jnp.int32), N_DP)

    def per_batch(items):
        query_in, key_in, value_in, grad_in, action_in, length_row, robot_row, group_id = items
        return one_batch(query_in, key_in, value_in, grad_in, action_in, length_row, robot_row, adapters[group_id], up_proj)

    key_all, value_all, up_all, adapter_all = lax.map(per_batch, (flatten(query_tokens), flatten(key_tokens), flatten(value_tokens), flatten(out_grad), flatten(actions), flatten(clip_lengths), flatten(clip_robots), groups))
    key_grad = key_all.reshape(N_DP, N_EMBODIME, TOKENS, width)
    value_grad = value_all.reshape(N_DP, N_EMBODIME, TOKENS, width)
    up_grad = jnp.sum(up_all, 0)
    adapter_grad = jnp.sum(adapter_all.reshape(N_DP, N_EMBODIME, ROBOTS, ACT, RANK), 0)
    return key_grad, value_grad, adapter_grad, up_grad
```

```python
import functools
import math

import jax
import jax.numpy as jnp
from jax import lax
from jax.experimental import pallas as pl
from jax.experimental.pallas import tpu as pltpu
from jax.sharding import Mesh, PartitionSpec as P

HEAD = 128
TOK = 128
RANK = 64
STEP_HEADS = 2
LOW = -1e30
SCALE = HEAD**-0.5
SCALE2 = SCALE * math.log2(math.e)
F32 = jnp.float32
BF16 = jnp.bfloat16
GROUP = ("dp", "x", "z")


def dot(a, b, ca, cb):
    return lax.dot_general(a, b, (((ca,), (cb,)), ((), ())), preferred_element_type=F32)


def clip_of(frame, lengths, robots, clips):
    begin = jnp.int32(0)
    start = jnp.int32(0)
    robot = jnp.int32(0)
    for i in range(clips):
        size = lengths[i]
        inside = jnp.logical_and(frame >= begin, frame < begin + size)
        start = jnp.where(inside, begin, start)
        robot = jnp.where(inside, robots[i], robot)
        begin = begin + size
    return start, robot


def attend_kernel(
    clips, steps, place, lengths, robots,
    act_own, act_oth, adapters, up,
    q_own, g_own, k_own, v_own,
    q_oth, g_oth, k_oth, v_oth,
    k_str, v_str, k_crs, v_crs,
    mine, other, back_str, back_crs, payload,
    adapted, adapted_t, agrad_t,
):
    step = pl.program_id(0)
    core = place[0]
    first = core == 0
    frame_a = 2 * place[1]
    frame_b = frame_a + 1
    start_a, robot_a = clip_of(frame_a, lengths, robots, clips)
    start_b, robot_b = clip_of(frame_b, lengths, robots, clips)

    def bias(valid):
        return jnp.where(valid, jnp.float32(0), jnp.float32(LOW))

    bias_a = (bias(frame_a - 2 >= start_a), bias(frame_a - 1 >= start_a), jnp.float32(0))
    bias_b = (bias(frame_b - 2 >= start_b), bias(frame_b - 1 >= start_b), jnp.float32(0))

    def pick(one, two):
        return jnp.where(first, one, two)

    @pl.when(step == 0)
    def _():
        for n, robot in enumerate((robot_a, robot_b)):
            act = pick(act_own[...], act_oth[...]) if n == 0 else pick(act_oth[...], act_own[...])
            table = adapters[robot]
            adapted[n * TOK:(n + 1) * TOK, :] = dot(act, table, 1, 0).astype(BF16)
            adapted_t[:, n * TOK:(n + 1) * TOK] = dot(table, act, 0, 1).astype(BF16)
        agrad_t[...] = jnp.zeros_like(agrad_t)

    def soften(raw, prod, biases):
        scores = [raw[n * TOK:(n + 1) * TOK] * SCALE2 + b for n, b in enumerate(biases)]
        top = functools.reduce(jnp.maximum, scores)
        top = jnp.max(top, 0, keepdims=True)
        weights = [jnp.exp2(s - top) for s in scores]
        prods = [prod[n * TOK:(n + 1) * TOK] for n in range(len(biases))]
        total = jnp.sum(functools.reduce(jnp.add, weights), 0, keepdims=True)
        mixed = [w * p for w, p in zip(weights, prods)]
        moment = jnp.sum(functools.reduce(jnp.add, mixed), 0, keepdims=True)
        inverse = 1.0 / total
        delta = moment * inverse
        scaled = inverse * SCALE
        prob = [(w * inverse).astype(BF16) for w in weights]
        dscore = [((w * scaled) * (p - delta)).astype(BF16) for w, p in zip(weights, prods)]
        return prob, dscore

    none = jnp.zeros((TOK, TOK), BF16)
    for h in range(STEP_HEADS):
        cols = slice(h * HEAD, (h + 1) * HEAD)
        up_h = up[:, cols]
        shift = dot(adapted[...], up_h, 1, 0)
        q_tok = jnp.concatenate(
            [pick(q_own[:, cols], q_oth[:, cols]), pick(q_oth[:, cols], q_own[:, cols])], 0
        )
        query = (q_tok.astype(F32) + shift).astype(BF16)
        grad = jnp.concatenate(
            [pick(g_own[:, cols], g_oth[:, cols]), pick(g_oth[:, cols], g_own[:, cols])], 0
        )
        keys = jnp.concatenate(
            [
                pick(k_str[:, cols], k_crs[:, cols]), pick(k_crs[:, cols], k_str[:, cols]),
                pick(k_own[:, cols], k_oth[:, cols]), pick(k_oth[:, cols], k_own[:, cols]),
            ],
            0,
        )
        values = jnp.concatenate(
            [
                pick(v_str[:, cols], v_crs[:, cols]), pick(v_crs[:, cols], v_str[:, cols]),
                pick(v_own[:, cols], v_oth[:, cols]), pick(v_oth[:, cols], v_own[:, cols]),
            ],
            0,
        )
        raw = dot(keys, query, 1, 1)
        prod = dot(values, grad, 1, 1)
        prob_a, dscore_a = soften(raw[: 3 * TOK, :TOK], prod[: 3 * TOK, :TOK], bias_a)
        prob_b, dscore_b = soften(raw[TOK:, TOK:], prod[TOK:, TOK:], bias_b)
        prob = jnp.concatenate(
            [jnp.concatenate(prob_a + [none], 0), jnp.concatenate([none] + prob_b, 0)], 1
        )
        dscore = jnp.concatenate(
            [jnp.concatenate(dscore_a + [none], 0), jnp.concatenate([none] + dscore_b, 0)], 1
        )
        query_grad = dot(keys, dscore, 0, 0)
        high = query_grad.astype(BF16)
        low = (query_grad - high.astype(F32)).astype(BF16)
        agrad_t[...] += dot(up_h, high, 1, 0) + dot(up_h, low, 1, 0)
        up_term = dot(adapted_t[...], high, 1, 1) + dot(adapted_t[...], low, 1, 1)
        payload[pl.ds(2 * (step * STEP_HEADS + h), 2)] = up_term.reshape(2, 32, HEAD).astype(BF16)
        for n, part in enumerate((dot(dscore, query, 1, 0), dot(prob, grad, 1, 0))):
            p0, p1 = part[:TOK].astype(BF16), part[TOK:2 * TOK].astype(BF16)
            a, b = part[2 * TOK:3 * TOK], part[3 * TOK:]
            back_str[n, :, cols] = pick(p0, p1)
            back_crs[n, :, cols] = pick(p1, p0)
            mine[n, :, cols] = pick(a, b)
            other[n, :, cols] = pick(b, a).astype(BF16)

    @pl.when(step == steps - 1)
    def _():
        terms = []
        for n in range(2):
            act = pick(act_own[...], act_oth[...]) if n == 0 else pick(act_oth[...], act_own[...])
            whole = agrad_t[:, n * TOK:(n + 1) * TOK]
            high = whole.astype(BF16)
            low = (whole - high.astype(F32)).astype(BF16)
            terms.append(dot(high, act, 1, 0) + dot(low, act, 1, 0))
        zero = jnp.zeros((RANK, HEAD), F32)
        base = 2 * steps * STEP_HEADS
        for s in range(4):
            term = jnp.where(robot_a == s, terms[0], zero) + jnp.where(robot_b == s, terms[1], zero)
            payload[base + 2 * s:base + 2 * s + 2] = term.reshape(2, 32, HEAD).astype(BF16)
        rest = payload.shape[0] - base - 8
        payload[base + 8:] = jnp.zeros((rest, 32, HEAD), BF16)


def attend(place, lengths, robots, act_own, act_oth, adapters, up, own, oth, straight, cross):
    half = straight.shape[2]
    width = STEP_HEADS * HEAD
    steps = half // width
    own_spec = pl.BlockSpec((TOK, width), lambda j, place, *_: (0, place[0] * steps + j))

    def layer(n):
        return pl.BlockSpec((None, TOK, width), lambda j, *_: (n, 0, j))

    def whole(shape):
        return pl.BlockSpec(shape, lambda j, *_: (0,) * len(shape))

    pair = pl.BlockSpec((2, TOK, width), lambda j, *_: (0, 0, j))
    grid_spec = pltpu.PrefetchScalarGridSpec(
        num_scalar_prefetch=3,
        grid=(steps,),
        in_specs=[whole((TOK, HEAD)), whole((TOK, HEAD)), whole(adapters.shape)]
        + [pl.BlockSpec((RANK, width), lambda j, place, *_: (0, place[0] * steps + j))]
        + [own_spec] * 4
        + [layer(n) for n in range(4)]
        + [layer(0), layer(1), layer(0), layer(1)],
        out_specs=[pair, pair, pair, pair, whole((32, 32, HEAD))],
        scratch_shapes=[
            pltpu.VMEM((2 * TOK, RANK), BF16),
            pltpu.VMEM((RANK, 2 * TOK), BF16),
            pltpu.VMEM((RANK, 2 * TOK), F32),
        ],
    )
    shape = (2, TOK, half)
    return pl.pallas_call(
        functools.partial(attend_kernel, lengths.shape[0], steps),
        grid_spec=grid_spec,
        out_shape=[
            jax.ShapeDtypeStruct(shape, F32),
            jax.ShapeDtypeStruct(shape, BF16),
            jax.ShapeDtypeStruct(shape, BF16),
            jax.ShapeDtypeStruct(shape, BF16),
            jax.ShapeDtypeStruct((32, 32, HEAD), BF16),
        ],
        compiler_params=pltpu.CompilerParams(
            dimension_semantics=("arbitrary",), vmem_limit_bytes=32 * 1024 * 1024
        ),
        cost_estimate=pl.CostEstimate(
            flops=2 * 10 * 5 * 512 * 256 * 128, bytes_accessed=12 * 1024 * 1024, transcendentals=10 * 512 * 256
        ),
        name="attend",
    )(place, lengths, robots, act_own, act_oth, adapters, up, *own, oth, oth, oth, oth, straight, straight, cross, cross)


def finish_kernel(heads, gathered, up_grad, adapter_grad):
    per_core = heads // 2
    for core in range(2):
        for h in range(per_core):
            at = (core * per_core + h) * HEAD
            for part in range(2):
                up_grad[part * 32:(part + 1) * 32, at:at + HEAD] = gathered[2 * (2 * h + part) + core].astype(F32)
    for s in range(4):
        chunk = 2 * per_core + 2 * s
        term = jnp.concatenate([gathered[2 * chunk], gathered[2 * chunk + 2]], 0).astype(F32)
        adapter_grad[s] = term.T


def finish(gathered, heads, adapters_shape):
    return pl.pallas_call(
        functools.partial(finish_kernel, heads),
        out_shape=[
            jax.ShapeDtypeStruct((RANK, heads * HEAD), F32),
            jax.ShapeDtypeStruct(adapters_shape, F32),
        ],
        name="finish",
    )(gathered)


def local(
    query_tokens, key_tokens, value_tokens, out_grad, actions, clip_lengths, clip_robots, adapters, up_proj,
):
    q, k, v, g = (t[0, 0] for t in (query_tokens, key_tokens, value_tokens, out_grad))
    act = actions[0, 0]
    width = q.shape[1]
    half = width // 2
    core = lax.axis_index("core")
    nz = lax.axis_size("z")
    chips = lax.axis_size("x") * nz
    chip = lax.axis_index("x") * nz + lax.axis_index("z")
    chain = ("x", "z", "core")

    def near(array):
        return lax.dynamic_slice_in_dim(array, core * half, half, 1)

    def far(array):
        return lax.dynamic_slice_in_dim(array, (1 - core) * half, half, 1)

    def chip_step(by, flip):
        return [
            (2 * c + i, 2 * (c + by) + ((1 - i) if flip else i))
            for c in range(chips)
            for i in range(2)
            if 0 <= c + by < chips
        ]

    swap = [(0, 1), (1, 0)]
    near_pair = jnp.stack([near(k), near(v)])
    far_all = jnp.stack([far(q), far(g), far(k), far(v)])
    straight = lax.ppermute(near_pair, chain, chip_step(1, False))
    cross = lax.ppermute(far_all[2:], chain, chip_step(1, True))
    oth = lax.ppermute(far_all, "core", swap)
    act_oth = lax.ppermute(act, "core", swap)
    place = jnp.stack([core, chip]).astype(jnp.int32)
    mine, other, back_str, back_crs, payload = attend(
        place, clip_lengths[0, 0], clip_robots[0, 0], act, act_oth, adapters[0], up_proj,
        (q, g, k, v), oth, straight, cross,
    )

    pieces = lax.all_to_all(payload, GROUP, 0, 0, tiled=True)
    chunk = jnp.sum(pieces.astype(F32), 0)
    index = (lax.axis_index("dp") * lax.axis_size("x") + lax.axis_index("x")) * nz + lax.axis_index("z")
    is_up = index < 2 * (half // HEAD)
    ny = lax.axis_size("y")
    spread = jnp.broadcast_to(chunk.astype(BF16)[None], (2 * ny, 32, HEAD))
    shared = lax.all_to_all(spread, ("core", "y"), 0, 0, tiled=True)
    from_core = jnp.arange(2 * ny, dtype=jnp.int32) // ny
    from_y = jnp.arange(2 * ny, dtype=jnp.int32) % ny
    keep = jnp.where(is_up, from_core == core, from_y == lax.axis_index("y"))
    total = jnp.sum(jnp.where(keep[:, None, None], shared.astype(F32), 0.0), 0)
    spread = jnp.broadcast_to(total.astype(BF16)[None], (64, 32, HEAD))
    gathered = lax.all_to_all(spread, GROUP + ("core",), 0, 0, tiled=True)
    up_total, adapter_total = finish(gathered, width // HEAD, adapters.shape[1:])

    ret_str = lax.ppermute(back_str, chain, chip_step(-1, False))
    ret_crs = lax.ppermute(back_crs, chain, chip_step(-1, True))
    other_in = lax.ppermute(other, "core", swap)
    near_out = (mine + ret_str.astype(F32)).astype(BF16)
    far_out = (other_in.astype(F32) + ret_crs.astype(F32)).astype(BF16)
    first = core == 0
    out = jnp.concatenate([jnp.where(first, near_out, far_out), jnp.where(first, far_out, near_out)], 2)
    return out[0][None, None], out[1][None, None], adapter_total[None], up_total


def solution(mesh):
    sizes = dict(mesh.shape)
    wide = Mesh(
        mesh.devices.reshape(sizes["dp"], 2, sizes["context"] // 4, 2, sizes["embodime"]),
        ("dp", "x", "z", "core", "y"),
    )
    frames = P("dp", "y", ("x", "z", "core"), None)
    rows = P("dp", "y", None)
    return jax.shard_map(
        local,
        mesh=wide,
        in_specs=(frames,) * 5 + (rows, rows, P("y", None, None, None), P()),
        out_specs=(frames, frames, P("y", None, None, None), P()),
        check_vma=False,
    )
```

```python
import functools
import math

import jax
import jax.numpy as jnp
from jax import lax
from jax.experimental import pallas as pl
from jax.experimental.pallas import tpu as pltpu
from jax.sharding import Mesh, PartitionSpec as P

HEAD = 128
TOK = 128
RANK = 64
FIRST = 8
LOW = -1e30
SCALE = HEAD**-0.5
SCALE2 = SCALE * math.log2(math.e)
F32 = jnp.float32
BF16 = jnp.bfloat16
GROUP = ("dp", "x", "z")


def dot(a, b, ca, cb):
    return lax.dot_general(a, b, (((ca,), (cb,)), ((), ())), preferred_element_type=F32)


def clip_of(frame, lengths, robots, clips):
    begin = jnp.int32(0)
    start = jnp.int32(0)
    robot = jnp.int32(0)
    for i in range(clips):
        size = lengths[i]
        inside = jnp.logical_and(frame >= begin, frame < begin + size)
        start = jnp.where(inside, begin, start)
        robot = jnp.where(inside, robots[i], robot)
        begin = begin + size
    return start, robot


def attend_kernel(
    clips, heads, offset, chunks, place, lengths, robots,
    act_own, adapters, oth, straight, cross, early, agrad_in,
    q_hbm, g_hbm, k_hbm, v_hbm, up_hbm, *refs,
):
    last = early is not None
    refs = refs[4:] if last else refs
    mine_hbm, other_hbm, str_hbm, crs_hbm, payload, agrad_out = refs[:6]
    own, up, mine, other, back_str, back_crs, adapted, adapted_t, agrad_t, sem_in, sem_out = refs[6:]
    core = place[0]
    first = core == 0
    half = oth.shape[1] // 4 // HEAD * HEAD
    width = heads * HEAD
    far = pl.ds(pl.multiple_of(core * half + offset * HEAD, HEAD), width)
    loads = [
        pltpu.make_async_copy(x.at[:, far], own.at[n], sem_in.at[n])
        for n, x in enumerate((q_hbm, g_hbm, k_hbm, v_hbm))
    ]
    loads.append(pltpu.make_async_copy(up_hbm.at[:, far], up, sem_in.at[4]))
    for load in loads:
        load.start()
    frame_a = 2 * place[1]
    frame_b = frame_a + 1
    start_a, robot_a = clip_of(frame_a, lengths, robots, clips)
    start_b, robot_b = clip_of(frame_b, lengths, robots, clips)

    def bias(valid):
        return jnp.where(valid, jnp.float32(0), jnp.float32(LOW))

    bias_a = (bias(frame_a - 2 >= start_a), bias(frame_a - 1 >= start_a), jnp.float32(0))
    bias_b = (bias(frame_b - 2 >= start_b), bias(frame_b - 1 >= start_b), jnp.float32(0))

    def pick(one, two):
        return jnp.where(first, one, two)

    def pair(one, two):
        return [pick(one, two), pick(two, one)]

    acts = pair(act_own[...], oth[:, 4 * half:])
    for n, (act, robot) in enumerate(zip(acts, (robot_a, robot_b))):
        table = adapters[robot]
        adapted[n * TOK:(n + 1) * TOK, :] = dot(act, table, 1, 1).astype(BF16)
        adapted_t[:, n * TOK:(n + 1) * TOK] = dot(table, act, 1, 1).astype(BF16)
    agrad_t[...] = agrad_in[...] if last else jnp.zeros_like(agrad_t)
    for load in loads:
        load.wait()

    def soften(raw, prod, biases):
        scores = [raw[n * TOK:(n + 1) * TOK] * SCALE2 + b for n, b in enumerate(biases)]
        top = functools.reduce(jnp.maximum, scores)
        top = jnp.max(top, 0, keepdims=True)
        weights = [jnp.exp2(s - top) for s in scores]
        prods = [prod[n * TOK:(n + 1) * TOK] for n in range(len(biases))]
        total = jnp.sum(functools.reduce(jnp.add, weights), 0, keepdims=True)
        mixed = [w * p for w, p in zip(weights, prods)]
        moment = jnp.sum(functools.reduce(jnp.add, mixed), 0, keepdims=True)
        inverse = 1.0 / total
        delta = moment * inverse
        scaled = inverse * SCALE
        prob = [(w * inverse).astype(BF16) for w in weights]
        dscore = [((w * scaled) * (p - delta)).astype(BF16) for w, p in zip(weights, prods)]
        return prob, dscore

    none = jnp.zeros((TOK, TOK), BF16)

    def one_head(h):
        at = pl.multiple_of(h * HEAD, HEAD)
        cols = pl.ds(at, HEAD)

        def theirs(n):
            return oth[:, pl.ds(pl.multiple_of(n * half + offset * HEAD + at, HEAD), HEAD)]

        up_h = up[:, cols]
        shift = dot(adapted[...], up_h, 1, 0)
        q_tok = jnp.concatenate(pair(own[0, :, cols], theirs(0)), 0)
        query = (q_tok.astype(F32) + shift).astype(BF16)
        grad = jnp.concatenate(pair(own[1, :, cols], theirs(1)), 0)
        keys = jnp.concatenate(pair(straight[0, :, cols], cross[0, :, cols]) + pair(own[2, :, cols], theirs(2)), 0)
        values = jnp.concatenate(pair(straight[1, :, cols], cross[1, :, cols]) + pair(own[3, :, cols], theirs(3)), 0)
        raw = dot(keys, query, 1, 1)
        prod = dot(values, grad, 1, 1)
        prob_a, dscore_a = soften(raw[: 3 * TOK, :TOK], prod[: 3 * TOK, :TOK], bias_a)
        prob_b, dscore_b = soften(raw[TOK:, TOK:], prod[TOK:, TOK:], bias_b)
        prob = jnp.concatenate(
            [jnp.concatenate(prob_a + [none], 0), jnp.concatenate([none] + prob_b, 0)], 1
        )
        dscore = jnp.concatenate(
            [jnp.concatenate(dscore_a + [none], 0), jnp.concatenate([none] + dscore_b, 0)], 1
        )
        query_grad = dot(keys, dscore, 0, 0)
        high = query_grad.astype(BF16)
        low = (query_grad - high.astype(F32)).astype(BF16)
        agrad_t[...] += dot(up_h, high, 1, 0) + dot(up_h, low, 1, 0)
        up_term = dot(adapted_t[...], high, 1, 1) + dot(adapted_t[...], low, 1, 1)
        chunk = 2 * h + (2 * offset if last else 0)
        payload[pl.ds(chunk, 2)] = up_term.reshape(2, 32, HEAD).astype(BF16)
        for n, part in enumerate((dot(dscore, query, 1, 0), dot(prob, grad, 1, 0))):
            p0, p1 = part[:TOK].astype(BF16), part[TOK:2 * TOK].astype(BF16)
            a, b = part[2 * TOK:3 * TOK], part[3 * TOK:]
            back_str[n, :, cols] = pick(p0, p1)
            back_crs[n, :, cols] = pick(p1, p0)
            mine[n, :, cols] = pick(a, b)
            other[n, :, cols] = pick(b, a).astype(BF16)

    if heads <= 2:
        for h in range(heads):
            one_head(h)
    else:
        @pl.loop(0, heads // 2)
        def _(j):
            one_head(2 * j)
            one_head(2 * j + 1)

    span = pl.ds(offset * HEAD, width)
    stores = [
        pltpu.make_async_copy(x, y.at[:, :, span], sem_out.at[n])
        for n, (x, y) in enumerate(
            ((back_str, str_hbm), (back_crs, crs_hbm), (other, other_hbm), (mine, mine_hbm))
        )
    ]
    for store in stores:
        store.start()
    if last:
        payload[: early.shape[0]] = early[...]
        terms = []
        for n, act in enumerate(acts):
            whole = agrad_t[:, n * TOK:(n + 1) * TOK]
            high = whole.astype(BF16)
            low = (whole - high.astype(F32)).astype(BF16)
            terms.append(dot(high, act, 1, 0) + dot(low, act, 1, 0))
        zero = jnp.zeros((RANK, HEAD), F32)
        base = 2 * (offset + heads)
        for s in range(4):
            term = jnp.where(robot_a == s, terms[0], zero) + jnp.where(robot_b == s, terms[1], zero)
            payload[base + 2 * s:base + 2 * s + 2] = term.reshape(2, 32, HEAD).astype(BF16)
        payload[base + 8:] = jnp.zeros((chunks - base - 8, 32, HEAD), BF16)
    else:
        agrad_out[...] = agrad_t[...]
    for store in stores:
        store.wait()


def attend(scalars, act_own, adapters, oth, straight, cross, own, up, offset, before=None):
    heads = straight.shape[2] // HEAD
    half = own[0].shape[1] // 2
    last = before is not None
    chunks = 32 if last else 2 * heads
    smem = pl.BlockSpec(memory_space=pltpu.SMEM)
    vmem = pl.BlockSpec(memory_space=pltpu.VMEM)
    hbm = pl.BlockSpec(memory_space=pl.ANY)
    shape = (2, TOK, half)
    part = (2, TOK, heads * HEAD)

    def fixed(x):
        return pltpu.with_memory_space_constraint(x, pltpu.HBM)

    inputs = [*scalars, act_own, adapters, oth, straight, cross]
    specs = [smem] * 3 + [vmem] * 5
    aliases = {}
    if last:
        inputs += [before[4], before[5]]
        specs += [vmem] * 2
    inputs += [fixed(x) for x in (*own, up)]
    specs += [hbm] * 5
    if last:
        aliases = {len(inputs) + n: n for n in range(4)}
        inputs += [fixed(x) for x in before[:4]]
        specs += [hbm] * 4
    body = functools.partial(attend_kernel, scalars[1].shape[0], heads, offset, chunks)

    def kernel(*refs):
        refs = list(refs)
        if not last:
            refs[8:8] = [None, None]
        if last:
            refs.insert(len(inputs) + 5, None)
        body(*refs)

    out_shape = [
        pltpu.HBM(shape, F32), pltpu.HBM(shape, BF16), pltpu.HBM(shape, BF16), pltpu.HBM(shape, BF16),
        jax.ShapeDtypeStruct((chunks, 32, HEAD), BF16),
    ]
    out_specs = [hbm] * 4 + [vmem]
    if not last:
        out_shape.append(jax.ShapeDtypeStruct((RANK, 2 * TOK), F32))
        out_specs.append(vmem)
    return pl.pallas_call(
        kernel,
        in_specs=specs,
        out_specs=out_specs,
        out_shape=out_shape,
        input_output_aliases=aliases,
        scratch_shapes=[
            pltpu.VMEM((4, TOK, heads * HEAD), BF16),
            pltpu.VMEM((RANK, heads * HEAD), BF16),
            pltpu.VMEM(part, F32),
            pltpu.VMEM(part, BF16),
            pltpu.VMEM(part, BF16),
            pltpu.VMEM(part, BF16),
            pltpu.VMEM((2 * TOK, RANK), BF16),
            pltpu.VMEM((RANK, 2 * TOK), BF16),
            pltpu.VMEM((RANK, 2 * TOK), F32),
            pltpu.SemaphoreType.DMA((5,)),
            pltpu.SemaphoreType.DMA((4,)),
        ],
        compiler_params=pltpu.CompilerParams(vmem_limit_bytes=24 * 1024 * 1024),
        cost_estimate=pl.CostEstimate(
            flops=2 * heads * 5 * 512 * 256 * 128, bytes_accessed=heads * 1024 * 1024, transcendentals=heads * 512 * 256
        ),
        name="attend_last" if last else "attend_first",
    )(*inputs)


def finish_kernel(heads, place, gathered, swapped, up_grad, adapter_grad):
    per_core = heads // 2
    for n, part in enumerate((gathered, swapped)):
        side = place[0] if n == 0 else 1 - place[0]
        for h in range(per_core):
            cols = pl.ds(pl.multiple_of((side * per_core + h) * HEAD, HEAD), HEAD)
            up_grad[:32, cols] = part[2 * h].astype(F32)
            up_grad[32:, cols] = part[2 * h + 1].astype(F32)
    for s in range(4):
        for n in range(2):
            at = 2 * per_core + 2 * s + n
            adapter_grad[s, n * 32:(n + 1) * 32] = gathered[at].astype(F32) + swapped[at].astype(F32)


def finish(place, gathered, swapped, heads):
    vmem = pl.BlockSpec(memory_space=pltpu.VMEM)
    return pl.pallas_call(
        functools.partial(finish_kernel, heads),
        in_specs=[pl.BlockSpec(memory_space=pltpu.SMEM), vmem, vmem],
        out_specs=[vmem, vmem],
        out_shape=[
            jax.ShapeDtypeStruct((RANK, heads * HEAD), F32),
            jax.ShapeDtypeStruct((4, RANK, HEAD), F32),
        ],
        compiler_params=pltpu.CompilerParams(vmem_limit_bytes=4 * 1024 * 1024),
        name="finish",
    )(place, gathered, swapped)


def local(
    query_tokens, key_tokens, value_tokens, out_grad, actions, clip_lengths, clip_robots, adapters, up_proj,
):
    q, k, v, g = (t[0, 0] for t in (query_tokens, key_tokens, value_tokens, out_grad))
    act = actions[0, 0]
    width = q.shape[1]
    half = width // 2
    core = lax.axis_index("core")
    nz = lax.axis_size("z")
    chips = lax.axis_size("x") * nz
    chip = lax.axis_index("x") * nz + lax.axis_index("z")
    chain = ("x", "z", "core")

    def cut(array, side, begin, size):
        return lax.dynamic_slice_in_dim(array, side * half + begin, size, 1)

    def chip_step(by, flip):
        return [
            (2 * c + i, 2 * (c + by) + ((1 - i) if flip else i))
            for c in range(chips)
            for i in range(2)
            if 0 <= c + by < chips
        ]

    swap = [(0, 1), (1, 0)]
    split = FIRST * HEAD
    moved = []
    for begin, size in ((0, split), (split, half - split)):
        for side, flip in ((core, False), (1 - core, True)):
            both = jnp.stack([cut(k, side, begin, size), cut(v, side, begin, size)])
            moved.append(lax.ppermute(both, chain, chip_step(1, flip)))
    oth = lax.ppermute(
        jnp.concatenate([cut(t, 1 - core, 0, half) for t in (q, g, k, v)] + [act], 1), "core", swap
    )
    place = jnp.stack([core, chip]).astype(jnp.int32)
    scalars = (place, clip_lengths[0, 0], clip_robots[0, 0])
    table = jnp.swapaxes(adapters[0], 1, 2)
    own = (q, g, k, v)
    before = attend(scalars, act, table, oth, moved[0], moved[1], own, up_proj, 0)
    mine, other, back_str, back_crs, payload = attend(
        scalars, act, table, oth, moved[2], moved[3], own, up_proj, FIRST, before
    )

    pieces = lax.all_to_all(payload, GROUP, 0, 0, tiled=True)
    chunk = jnp.sum(pieces.astype(F32), 0)
    index = (lax.axis_index("dp") * lax.axis_size("x") + lax.axis_index("x")) * nz + lax.axis_index("z")
    is_up = index < 2 * (half // HEAD)
    ny = lax.axis_size("y")
    shared = lax.all_to_all(jnp.broadcast_to(chunk.astype(BF16)[None], (ny, 32, HEAD)), "y", 0, 0, tiled=True)
    keep = jnp.logical_or(is_up, jnp.arange(ny, dtype=jnp.int32) == lax.axis_index("y"))
    total = jnp.sum(jnp.where(keep[:, None, None], shared.astype(F32), 0.0), 0)
    gathered = lax.all_to_all(jnp.broadcast_to(total.astype(BF16)[None], (32, 32, HEAD)), GROUP, 0, 0, tiled=True)
    swapped = lax.ppermute(gathered, "core", swap)
    up_total, adapter_total = finish(place, gathered, swapped, width // HEAD)
    adapter_total = jnp.swapaxes(adapter_total, 1, 2)

    ret_str = lax.ppermute(back_str, chain, chip_step(-1, False))
    ret_crs = lax.ppermute(back_crs, chain, chip_step(-1, True))
    other_in = lax.ppermute(other, "core", swap)
    near_out = (mine + ret_str.astype(F32)).astype(BF16)
    far_out = (other_in.astype(F32) + ret_crs.astype(F32)).astype(BF16)
    first = core == 0
    out = jnp.concatenate([jnp.where(first, near_out, far_out), jnp.where(first, far_out, near_out)], 2)
    return out[0][None, None], out[1][None, None], adapter_total[None], up_total


def solution(mesh):
    sizes = dict(mesh.shape)
    wide = Mesh(
        mesh.devices.reshape(sizes["dp"], 2, sizes["context"] // 4, 2, sizes["embodime"]),
        ("dp", "x", "z", "core", "y"),
    )
    frames = P("dp", "y", ("x", "z", "core"), None)
    rows = P("dp", "y", None)
    return jax.shard_map(
        local,
        mesh=wide,
        in_specs=(frames,) * 5 + (rows, rows, P("y", None, None, None), P()),
        out_specs=(frames, frames, P("y", None, None, None), P()),
        check_vma=False,
    )
```

```python
import functools
import math

import jax
import jax.numpy as jnp
from jax import lax
from jax.experimental import pallas as pl
from jax.experimental.pallas import tpu as pltpu
from jax.sharding import Mesh, PartitionSpec as P

HEAD = 128
TOK = 128
RANK = 64
SPLIT = 3
LOW = -1e30
SCALE = HEAD**-0.5
SCALE2 = SCALE * math.log2(math.e)
F32 = jnp.float32
BF16 = jnp.bfloat16
GROUP = ("dp", "x", "z")
MIB = 1024 * 1024


def dot(a, b, ca, cb):
    return lax.dot_general(a, b, (((ca,), (cb,)), ((), ())), preferred_element_type=F32)


def clip_of(frame, lengths, robots, clips):
    begin = jnp.int32(0)
    start = jnp.int32(0)
    robot = jnp.int32(0)
    for i in range(clips):
        size = lengths[i]
        inside = jnp.logical_and(frame >= begin, frame < begin + size)
        start = jnp.where(inside, begin, start)
        robot = jnp.where(inside, robots[i], robot)
        begin = begin + size
    return start, robot


def smem():
    return pl.BlockSpec(memory_space=pltpu.SMEM)


def vmem():
    return pl.BlockSpec(memory_space=pltpu.VMEM)


def hbm():
    return pl.BlockSpec(memory_space=pl.ANY)


def fixed(x):
    return pltpu.with_memory_space_constraint(x, pltpu.HBM)


def take_kernel(far, place, q, g, k, v, act, out, sems):
    half = q.shape[1] // 2
    side = 1 - place[0] if far else place[0]
    copies = [
        pltpu.make_async_copy(
            x.at[:, pl.ds(pl.multiple_of(side * half, HEAD), half)], out.at[:, pl.ds(n * half, half)], sems.at[n]
        )
        for n, x in enumerate((q, g, k, v))
    ]
    copies.append(pltpu.make_async_copy(act, out.at[:, pl.ds(4 * half, HEAD)], sems.at[4]))
    for copy in copies:
        copy.start()
    for copy in copies:
        copy.wait()


def take_half(place, own, act, far):
    half = own[0].shape[1] // 2
    return pl.pallas_call(
        functools.partial(take_kernel, far),
        in_specs=[smem()] + [hbm()] * 5,
        out_specs=vmem(),
        out_shape=pltpu.VMEM((TOK, 4 * half + HEAD), BF16),
        scratch_shapes=[pltpu.SemaphoreType.DMA((5,))],
        compiler_params=pltpu.CompilerParams(vmem_limit_bytes=8 * MIB),
        cost_estimate=pl.CostEstimate(flops=0, bytes_accessed=4 * MIB, transcendentals=0),
        name="take_far" if far else "take_near",
    )(place, *(fixed(x) for x in own), fixed(act))


def pack_kernel(clips, begin, heads, place, lengths, robots, near, oth, up, down):
    half = near.shape[1] // 4 // HEAD * HEAD
    quarter = half // 2
    first = place[0] == 0
    frame_a = 2 * place[1]
    start_n, _ = clip_of(frame_a + 2, lengths, robots, clips)
    wide = start_n == frame_a
    width = heads * HEAD

    def frame(is_a, array, group):
        at = array * half + group * quarter + begin * HEAD
        one, two = near[:, at:at + width], oth[:, at:at + width]
        return jnp.where(first, one, two) if is_a else jnp.where(first, two, one)

    for n, array in enumerate((2, 3)):
        up[:, n * width:(n + 1) * width] = frame(False, array, 0)
        up[:, (2 + n) * width:(3 + n) * width] = jnp.where(wide, frame(True, array, 0), frame(False, array, 1))
    for n in range(4):
        down[:, n * width:(n + 1) * width] = frame(True, n, 1)
    one, two = near[:, 4 * half:], oth[:, 4 * half:]
    down[:, 4 * width:] = jnp.where(first, one, two)


def pack(scalars, near, oth, begin, heads):
    width = heads * HEAD
    return pl.pallas_call(
        functools.partial(pack_kernel, scalars[1].shape[0], begin, heads),
        in_specs=[smem()] * 3 + [vmem()] * 2,
        out_specs=[vmem()] * 2,
        out_shape=[
            jax.ShapeDtypeStruct((TOK, 4 * width), BF16),
            jax.ShapeDtypeStruct((TOK, 4 * width + HEAD), BF16),
        ],
        compiler_params=pltpu.CompilerParams(vmem_limit_bytes=8 * MIB),
        cost_estimate=pl.CostEstimate(flops=0, bytes_accessed=4 * MIB, transcendentals=0),
        name="pack",
    )(*scalars, near, oth)


def attend_kernel(
    clips, begin, heads, place, lengths, robots,
    adapters, near, oth, below, above, early, agrad_in, up_hbm, *refs,
):
    last = early is not None
    refs = refs[4:] if last else refs
    sum_a, sum_b, ret_down, ret_up, payload, agrad_out = refs[:6]
    up, keep_a, keep_b, keep_down, keep_up, adapted, adapted_t, agrad_t, sem_in, sem_out = refs[6:]
    core = place[0]
    first = core == 0
    half = near.shape[1] // 4 // HEAD * HEAD
    quarter = half // 2
    five = quarter // HEAD
    width = heads * HEAD
    loads = [
        pltpu.make_async_copy(
            up_hbm.at[:, pl.ds(pl.multiple_of(core * half + n * quarter + begin * HEAD, HEAD), width)],
            up.at[n], sem_in.at[n],
        )
        for n in range(2)
    ]
    for load in loads:
        load.start()
    frame_a = 2 * place[1]
    start_a, robot_a = clip_of(frame_a, lengths, robots, clips)
    start_b, robot_b = clip_of(frame_a + 1, lengths, robots, clips)
    start_n, robot_n = clip_of(frame_a + 2, lengths, robots, clips)
    wide_below = start_a == frame_a - 2
    wide_above = start_n == frame_a

    def bias(valid):
        return jnp.where(valid, jnp.float32(0), jnp.float32(LOW))

    zero = jnp.float32(0)
    bias_a = (bias(wide_below), bias(start_a <= frame_a - 1), zero)
    bias_b = (bias(start_b <= frame_a - 1), bias(start_b <= frame_a), zero)
    scale_a = jnp.where(wide_below, 0.0, 1.0).astype(F32)
    scale_n = jnp.where(wide_above, 1.0, 0.0).astype(F32)

    def pick(one, two):
        return jnp.where(first, one, two)

    def pair(one, two):
        return [pick(one, two), pick(two, one)]

    acts = pair(near[:, 4 * half:], oth[:, 4 * half:]) + [above[:, 4 * width:]]
    for n, (act, robot) in enumerate(zip(acts, (robot_a, robot_b, robot_n))):
        table = adapters[robot]
        adapted[n * TOK:(n + 1) * TOK, :] = dot(act, table, 1, 1).astype(BF16)
        adapted_t[:, n * TOK:(n + 1) * TOK] = dot(table, act, 1, 1).astype(BF16)
    agrad_t[...] = agrad_in[...] if last else jnp.zeros_like(agrad_t)
    for load in loads:
        load.wait()

    def soften(raw, prods, biases, keep=None):
        scores = [r * SCALE2 + b for r, b in zip(raw, biases)]
        top = jnp.max(functools.reduce(jnp.maximum, scores), 0, keepdims=True)
        weights = [jnp.exp2(s - top) for s in scores]
        total = jnp.sum(functools.reduce(jnp.add, weights), 0, keepdims=True)
        mixed = [w * p for w, p in zip(weights, prods)]
        moment = jnp.sum(functools.reduce(jnp.add, mixed), 0, keepdims=True)
        inverse = 1.0 / total
        if keep is not None:
            inverse = inverse * keep
        delta = moment * inverse
        scaled = inverse * SCALE
        prob = [(w * inverse).astype(BF16) for w in weights]
        dscore = [((w * scaled) * (p - delta)).astype(BF16) for w, p in zip(weights, prods)]
        return prob, dscore

    def block(x, i, j):
        return x[i * TOK:(i + 1) * TOK, j * TOK:(j + 1) * TOK]

    def column(blocks):
        return jnp.concatenate(blocks, 0)

    none = jnp.zeros((TOK, TOK), BF16)

    def sums(keys, dscore, up_h, rows, where):
        query_grad = dot(keys, dscore, 0, 0)
        high = query_grad.astype(BF16)
        low = (query_grad - high.astype(F32)).astype(BF16)
        agrad_t[:, :rows] += dot(up_h, high, 1, 0) + dot(up_h, low, 1, 0)
        term = dot(adapted_t[:, :rows], high, 1, 1) + dot(adapted_t[:, :rows], low, 1, 1)
        payload[pl.ds(where, 2)] = term.reshape(2, 32, HEAD).astype(BF16)

    def one_pair(j):
        at = pl.multiple_of(j * HEAD, HEAD)
        cols = pl.ds(at, HEAD)

        def there(n, group):
            return pl.ds(pl.multiple_of(n * half + group * quarter + begin * HEAD + at, HEAD), HEAD)

        def both(n, group):
            return pair(near[:, there(n, group)], oth[:, there(n, group)])

        def lower(n):
            return below[:, pl.ds(pl.multiple_of(n * width + at, HEAD), HEAD)]

        def upper(n):
            return above[:, pl.ds(pl.multiple_of(n * width + at, HEAD), HEAD)]

        up_h = up[0, :, cols]
        shift = dot(adapted[: 2 * TOK], up_h, 1, 0)
        query = (column(both(0, 0)).astype(F32) + shift).astype(BF16)
        grad = column(both(1, 0))
        keys = column([lower(2), lower(0)] + both(2, 0))
        values = column([lower(3), lower(1)] + both(3, 0))
        raw = dot(keys, query, 1, 1)
        prod = dot(values, grad, 1, 1)
        prob_a, dscore_a = soften([block(raw, i, 0) for i in range(3)], [block(prod, i, 0) for i in range(3)], bias_a)
        prob_b, dscore_b = soften(
            [block(raw, i, 1) for i in range(1, 4)], [block(prod, i, 1) for i in range(1, 4)], bias_b
        )
        prob = jnp.concatenate([column(prob_a + [none]), column([none] + prob_b)], 1)
        dscore = jnp.concatenate([column(dscore_a + [none]), column([none] + dscore_b)], 1)
        sums(keys, dscore, up_h, 2 * TOK, 2 * j + (2 * begin if last else 0))
        wide_parts = []
        for n, part in enumerate((dot(dscore, query, 1, 0), dot(prob, grad, 1, 0))):
            wide_parts.append(part[:TOK])
            keep_down[n, :, cols] = part[TOK:2 * TOK].astype(BF16)
            keep_a[n, 0, :, cols] = part[2 * TOK:3 * TOK]
            keep_b[n, 0, :, cols] = part[3 * TOK:]

        up_h = up[1, :, cols]
        shift = dot(adapted[...], up_h, 1, 0)
        query = (column(both(0, 1) + [upper(0)]).astype(F32) + shift).astype(BF16)
        grad = column(both(1, 1) + [upper(1)])
        keys = column([lower(2)] + both(2, 1) + [upper(2)])
        values = column([lower(3)] + both(3, 1) + [upper(3)])
        raw = dot(keys[: 3 * TOK], query[: 2 * TOK], 1, 1)
        prod = dot(values[: 3 * TOK], grad[: 2 * TOK], 1, 1)
        raw_n = dot(keys[TOK:], query[2 * TOK:], 1, 1)
        prod_n = dot(values[TOK:], grad[2 * TOK:], 1, 1)
        prob_a, dscore_a = soften(
            [block(raw, i, 0) for i in range(2)], [block(prod, i, 0) for i in range(2)], bias_a[1:], scale_a
        )
        prob_b, dscore_b = soften([block(raw, i, 1) for i in range(3)], [block(prod, i, 1) for i in range(3)], bias_b)
        prob_n, dscore_n = soften(
            [block(raw_n, i, 0) for i in range(3)], [block(prod_n, i, 0) for i in range(3)], (zero, zero, zero), scale_n
        )
        prob = jnp.concatenate([column(prob_a + [none, none]), column(prob_b + [none]), column([none] + prob_n)], 1)
        dscore = jnp.concatenate(
            [column(dscore_a + [none, none]), column(dscore_b + [none]), column([none] + dscore_n)], 1
        )
        sums(keys, dscore, up_h, 3 * TOK, 2 * j + (2 * (five + begin) if last else 2 * heads))
        for n, part in enumerate((dot(dscore, query, 1, 0), dot(prob, grad, 1, 0))):
            keep_down[2 + n, :, cols] = jnp.where(wide_below, wide_parts[n], part[:TOK]).astype(BF16)
            keep_a[n, 1, :, cols] = part[TOK:2 * TOK]
            keep_b[n, 1, :, cols] = part[2 * TOK:3 * TOK]
            keep_up[n, :, cols] = part[3 * TOK:].astype(BF16)

    for j in range(heads):
        one_pair(j)

    span = pl.ds(begin * HEAD, width)
    stores = [
        pltpu.make_async_copy(x, y, sem_out.at[n])
        for n, (x, y) in enumerate(
            (
                (keep_down, ret_down.at[:, :, span]), (keep_up, ret_up.at[:, :, span]),
                (keep_a, sum_a.at[:, :, :, span]), (keep_b, sum_b.at[:, :, :, span]),
            )
        )
    ]
    for store in stores:
        store.start()
    if last:
        payload[: 2 * begin] = early[: 2 * begin]
        payload[2 * five:2 * (five + begin)] = early[2 * begin:]
        terms = []
        for n, act in enumerate(acts):
            whole = agrad_t[:, n * TOK:(n + 1) * TOK]
            high = whole.astype(BF16)
            low = (whole - high.astype(F32)).astype(BF16)
            terms.append(dot(high, act, 1, 0) + dot(low, act, 1, 0))
        blank = jnp.zeros((RANK, HEAD), F32)
        base = 4 * five
        for s in range(4):
            term = jnp.where(robot_a == s, terms[0], blank) + jnp.where(robot_b == s, terms[1], blank)
            term = term + jnp.where(robot_n == s, terms[2], blank)
            payload[base + 2 * s:base + 2 * s + 2] = term.reshape(2, 32, HEAD).astype(BF16)
        payload[base + 8:] = jnp.zeros((payload.shape[0] - base - 8, 32, HEAD), BF16)
    else:
        agrad_out[...] = agrad_t[...]
    for store in stores:
        store.wait()


def attend(scalars, adapters, near, oth, below, above, up, begin, before=None):
    width = below.shape[1] // 4
    heads = width // HEAD
    quarter = up.shape[1] // 4
    last = before is not None
    chunks = 32 if last else 4 * heads
    inputs = [*scalars, adapters, near, oth, below, above]
    specs = [smem()] * 3 + [vmem()] * 5
    if last:
        inputs += [before[4], before[5]]
        specs += [vmem()] * 2
    inputs.append(fixed(up))
    specs.append(hbm())
    plain = len(inputs)
    aliases = {}
    if last:
        aliases = {plain + n: n for n in range(4)}
        inputs += [fixed(x) for x in before[:4]]
        specs += [hbm()] * 4
    body = functools.partial(attend_kernel, scalars[1].shape[0], begin, heads)

    def kernel(*refs):
        refs = list(refs)
        if last:
            refs.insert(plain + 9, None)
        else:
            refs[8:8] = [None, None]
        body(*refs)

    out_shape = [
        pltpu.HBM((2, 2, TOK, quarter), F32), pltpu.HBM((2, 2, TOK, quarter), F32),
        pltpu.HBM((4, TOK, quarter), BF16), pltpu.HBM((2, TOK, quarter), BF16),
        jax.ShapeDtypeStruct((chunks, 32, HEAD), BF16),
    ]
    out_specs = [hbm()] * 4 + [vmem()]
    if not last:
        out_shape.append(jax.ShapeDtypeStruct((RANK, 3 * TOK), F32))
        out_specs.append(vmem())
    return pl.pallas_call(
        kernel,
        in_specs=specs,
        out_specs=out_specs,
        out_shape=out_shape,
        input_output_aliases=aliases,
        scratch_shapes=[
            pltpu.VMEM((2, RANK, width), BF16),
            pltpu.VMEM((2, 2, TOK, width), F32),
            pltpu.VMEM((2, 2, TOK, width), F32),
            pltpu.VMEM((4, TOK, width), BF16),
            pltpu.VMEM((2, TOK, width), BF16),
            pltpu.VMEM((3 * TOK, RANK), BF16),
            pltpu.VMEM((RANK, 3 * TOK), BF16),
            pltpu.VMEM((RANK, 3 * TOK), F32),
            pltpu.SemaphoreType.DMA((2,)),
            pltpu.SemaphoreType.DMA((4,)),
        ],
        compiler_params=pltpu.CompilerParams(vmem_limit_bytes=24 * MIB),
        cost_estimate=pl.CostEstimate(
            flops=2 * heads * 12 * 512 * 256 * 128, bytes_accessed=heads * 2 * MIB, transcendentals=heads * 1024 * 256
        ),
        name="attend_last" if last else "attend_first",
    )(*inputs)


def finish_kernel(heads, place, gathered, swapped, up_grad, adapter_grad):
    per_core = heads // 2
    for n, part in enumerate((gathered, swapped)):
        side = place[0] if n == 0 else 1 - place[0]
        for h in range(per_core):
            cols = pl.ds(pl.multiple_of((side * per_core + h) * HEAD, HEAD), HEAD)
            up_grad[:32, cols] = part[2 * h].astype(F32)
            up_grad[32:, cols] = part[2 * h + 1].astype(F32)
    for s in range(4):
        for n in range(2):
            at = 2 * per_core + 2 * s + n
            adapter_grad[s, n * 32:(n + 1) * 32] = gathered[at].astype(F32) + swapped[at].astype(F32)


def finish(place, gathered, swapped, heads):
    return pl.pallas_call(
        functools.partial(finish_kernel, heads),
        in_specs=[smem(), vmem(), vmem()],
        out_specs=[vmem(), vmem()],
        out_shape=[
            jax.ShapeDtypeStruct((RANK, heads * HEAD), F32),
            jax.ShapeDtypeStruct((4, RANK, HEAD), F32),
        ],
        compiler_params=pltpu.CompilerParams(vmem_limit_bytes=4 * MIB),
        name="finish",
    )(place, gathered, swapped)


def local(
    query_tokens, key_tokens, value_tokens, out_grad, actions, clip_lengths, clip_robots, adapters, up_proj,
):
    q, k, v, g = (t[0, 0] for t in (query_tokens, key_tokens, value_tokens, out_grad))
    act = actions[0, 0]
    width = q.shape[1]
    half = width // 2
    quarter = half // 2
    core = lax.axis_index("core")
    nz = lax.axis_size("z")
    chips = lax.axis_size("x") * nz
    chip = lax.axis_index("x") * nz + lax.axis_index("z")
    column = ("x", "z")
    swap = [(0, 1), (1, 0)]
    upward = [(c, c + 1) for c in range(chips - 1)]
    downward = [(c + 1, c) for c in range(chips - 1)]
    place = jnp.stack([core, chip]).astype(jnp.int32)
    lengths = clip_lengths[0, 0]
    scalars = (place, lengths, clip_robots[0, 0])
    own = (q, g, k, v)
    oth = lax.ppermute(take_half(place, own, act, True), "core", swap)
    near = take_half(place, own, act, False)
    five = quarter // HEAD
    table = jnp.swapaxes(adapters[0], 1, 2)
    moved = []
    for begin, heads in ((0, SPLIT), (SPLIT, five - SPLIT)):
        up_msg, down_msg = pack(scalars, near, oth, begin, heads)
        moved.append((lax.ppermute(up_msg, column, upward), lax.ppermute(down_msg, column, downward)))
    before = attend(scalars, table, near, oth, *moved[0], up_proj, 0)
    sum_a, sum_b, ret_down, ret_up, payload = attend(
        scalars, table, near, oth, *moved[1], up_proj, SPLIT, before
    )

    pieces = lax.all_to_all(payload, GROUP, 0, 0, tiled=True)
    chunk = jnp.sum(pieces.astype(F32), 0)
    index = (lax.axis_index("dp") * lax.axis_size("x") + lax.axis_index("x")) * nz + lax.axis_index("z")
    is_up = index < 2 * (half // HEAD)
    ny = lax.axis_size("y")
    shared = lax.all_to_all(jnp.broadcast_to(chunk.astype(BF16)[None], (ny, 32, HEAD)), "y", 0, 0, tiled=True)
    keep = jnp.logical_or(is_up, jnp.arange(ny, dtype=jnp.int32) == lax.axis_index("y"))
    total = jnp.sum(jnp.where(keep[:, None, None], shared.astype(F32), 0.0), 0)
    gathered = lax.all_to_all(jnp.broadcast_to(total.astype(BF16)[None], (32, 32, HEAD)), GROUP, 0, 0, tiled=True)
    swapped = lax.ppermute(gathered, "core", swap)
    up_total, adapter_total = finish(place, gathered, swapped, width // HEAD)
    adapter_total = jnp.swapaxes(adapter_total, 1, 2)

    ends = jnp.cumsum(lengths)
    after = 2 * chip + 2
    wide_above = jnp.sum(jnp.where((ends - lengths <= after) & (after < ends), ends - lengths, 0)) == 2 * chip
    wide_above = jnp.logical_and(wide_above, after < ends[-1])
    from_above = lax.ppermute(ret_down, column, downward).astype(F32)
    from_below = lax.ppermute(ret_up, column, upward).astype(F32)
    second = from_above[2:]
    a1 = sum_a[:, 0] + jnp.where(wide_above, second, 0.0)
    a2 = sum_a[:, 1] + from_below
    b1 = sum_b[:, 0] + from_above[:2]
    b2 = sum_b[:, 1] + jnp.where(wide_above, 0.0, second)
    first = core == 0
    mine = [jnp.where(first, x, y).astype(BF16) for x, y in ((a1, b1), (a2, b2))]
    theirs = jnp.stack([jnp.where(first, y, x).astype(BF16) for x, y in ((a1, b1), (a2, b2))])
    other = lax.ppermute(theirs, "core", swap)
    out = jnp.concatenate(
        [jnp.where(first, mine[0], other[0]), jnp.where(first, mine[1], other[1])]
        + [jnp.where(first, other[0], mine[0]), jnp.where(first, other[1], mine[1])],
        2,
    )
    return out[0][None, None], out[1][None, None], adapter_total[None], up_total


def solution(mesh):
    sizes = dict(mesh.shape)
    wide = Mesh(
        mesh.devices.reshape(sizes["dp"], 2, sizes["context"] // 4, 2, sizes["embodime"]),
        ("dp", "x", "z", "core", "y"),
    )
    frames = P("dp", "y", ("x", "z", "core"), None)
    rows = P("dp", "y", None)
    return jax.shard_map(
        local,
        mesh=wide,
        in_specs=(frames,) * 5 + (rows, rows, P("y", None, None, None), P()),
        out_specs=(frames, frames, P("y", None, None, None), P()),
        check_vma=False,
    )
```

```python
import functools
import math

import jax
import jax.numpy as jnp
from jax import lax
from jax.experimental import pallas as pl
from jax.experimental.pallas import tpu as pltpu
from jax.sharding import Mesh, PartitionSpec as P

HEAD = 128
TOK = 128
RANK = 64
LOW = -1e30
SCALE = HEAD**-0.5
SCALE2 = SCALE * math.log2(math.e)
F32 = jnp.float32
BF16 = jnp.bfloat16
ROWS = 16
MIB = 1024 * 1024


def dot(a, b, ca, cb):
    return lax.dot_general(a, b, (((ca,), (cb,)), ((), ())), preferred_element_type=F32)


def clip_of(frame, lengths, robots, clips):
    begin = jnp.int32(0)
    start = jnp.int32(0)
    robot = jnp.int32(0)
    for i in range(clips):
        size = lengths[i]
        inside = jnp.logical_and(frame >= begin, frame < begin + size)
        start = jnp.where(inside, begin, start)
        robot = jnp.where(inside, robots[i], robot)
        begin = begin + size
    return start, robot


def smem():
    return pl.BlockSpec(memory_space=pltpu.SMEM)


def vmem():
    return pl.BlockSpec(memory_space=pltpu.VMEM)


def hbm():
    return pl.BlockSpec(memory_space=pl.ANY)


def fixed(x):
    return pltpu.with_memory_space_constraint(x, pltpu.HBM)


def take_kernel(far, place, q, g, k, v, act, out, sems):
    half = q.shape[1] // 2
    side = 1 - place[0] if far else place[0]
    copies = [
        pltpu.make_async_copy(
            x.at[:, pl.ds(pl.multiple_of(side * half, HEAD), half)], out.at[:, pl.ds(n * half, half)], sems.at[n]
        )
        for n, x in enumerate((q, g, k, v))
    ]
    copies.append(pltpu.make_async_copy(act, out.at[:, pl.ds(4 * half, HEAD)], sems.at[4]))
    for copy in copies:
        copy.start()
    for copy in copies:
        copy.wait()


def take_half(place, own, act, far):
    half = own[0].shape[1] // 2
    return pl.pallas_call(
        functools.partial(take_kernel, far),
        in_specs=[smem()] + [hbm()] * 5,
        out_specs=vmem(),
        out_shape=pltpu.VMEM((TOK, 4 * half + HEAD), BF16),
        scratch_shapes=[pltpu.SemaphoreType.DMA((5,))],
        compiler_params=pltpu.CompilerParams(vmem_limit_bytes=8 * MIB),
        cost_estimate=pl.CostEstimate(flops=0, bytes_accessed=4 * MIB, transcendentals=0),
        name="take_far" if far else "take_near",
    )(place, *(fixed(x) for x in own), fixed(act))


def pack_kernel(clips, place, lengths, robots, near, oth, up, down):
    half = near.shape[1] // 4 // HEAD * HEAD
    quarter = half // 2
    first = place[0] == 0
    frame_a = 2 * place[1]
    start_n, _ = clip_of(frame_a + 2, lengths, robots, clips)
    wide = start_n == frame_a

    def frame(is_a, array, group):
        at = array * half + group * quarter
        one, two = near[:, at:at + quarter], oth[:, at:at + quarter]
        return jnp.where(first, one, two) if is_a else jnp.where(first, two, one)

    for n, array in enumerate((2, 3)):
        up[:, n * quarter:(n + 1) * quarter] = frame(False, array, 0)
        up[:, (2 + n) * quarter:(3 + n) * quarter] = jnp.where(wide, frame(True, array, 0), frame(False, array, 1))
    for n in range(4):
        down[:, n * quarter:(n + 1) * quarter] = frame(True, n, 1)
    one, two = near[:, 4 * half:], oth[:, 4 * half:]
    down[:, 4 * quarter:] = jnp.where(first, one, two)


def pack(scalars, near, oth):
    quarter = near.shape[1] // 4 // HEAD * HEAD // 2
    return pl.pallas_call(
        functools.partial(pack_kernel, scalars[1].shape[0]),
        in_specs=[smem()] * 3 + [vmem()] * 2,
        out_specs=[vmem()] * 2,
        out_shape=[pltpu.VMEM((TOK, 4 * quarter), BF16), pltpu.VMEM((TOK, 4 * quarter + HEAD), BF16)],
        compiler_params=pltpu.CompilerParams(vmem_limit_bytes=8 * MIB),
        cost_estimate=pl.CostEstimate(flops=0, bytes_accessed=4 * MIB, transcendentals=0),
        name="pack",
    )(*scalars, near, oth)


class Views:
    def __init__(self, place, near, oth, below, above):
        self.first = place[0] == 0
        self.near, self.oth, self.below, self.above = near, oth, below, above
        self.half = near.shape[1] // 4 // HEAD * HEAD
        self.quarter = self.half // 2

    def pick(self, one, two):
        return jnp.where(self.first, one, two)

    def pair(self, one, two):
        return [self.pick(one, two), self.pick(two, one)]

    def both(self, n, group, j):
        at = n * self.half + group * self.quarter + j * HEAD
        return self.pair(self.near[:, at:at + HEAD], self.oth[:, at:at + HEAD])

    def lower(self, n, j):
        at = n * self.quarter + j * HEAD
        return self.below[:, at:at + HEAD]

    def upper(self, n, j):
        at = n * self.quarter + j * HEAD
        return self.above[:, at:at + HEAD]

    def actions(self):
        return self.pair(self.near[:, 4 * self.half:], self.oth[:, 4 * self.half:]) + [self.above[:, 4 * self.quarter:]]


def block(x, i, j):
    return x[i * TOK:(i + 1) * TOK, j * TOK:(j + 1) * TOK]


def column(blocks):
    return jnp.concatenate(blocks, 0)


def soften(raw, prods, biases, keep=None):
    scores = [r * SCALE2 + b for r, b in zip(raw, biases)]
    top = jnp.max(functools.reduce(jnp.maximum, scores), 0, keepdims=True)
    weights = [jnp.exp2(s - top) for s in scores]
    total = jnp.sum(functools.reduce(jnp.add, weights), 0, keepdims=True)
    mixed = [w * p for w, p in zip(weights, prods)]
    moment = jnp.sum(functools.reduce(jnp.add, mixed), 0, keepdims=True)
    inverse = 1.0 / total
    if keep is not None:
        inverse = inverse * keep
    delta = moment * inverse
    scaled = inverse * SCALE
    prob = [(w * inverse).astype(BF16) for w in weights]
    dscore = [((w * scaled) * (p - delta)).astype(BF16) for w, p in zip(weights, prods)]
    return prob, dscore


class Masks:
    def __init__(self, clips, place, lengths, robots):
        frame_a = 2 * place[1]
        start_a, robot_a = clip_of(frame_a, lengths, robots, clips)
        start_b, robot_b = clip_of(frame_a + 1, lengths, robots, clips)
        start_n, robot_n = clip_of(frame_a + 2, lengths, robots, clips)
        self.wide_below = start_a == frame_a - 2
        self.wide_above = start_n == frame_a
        self.robots = (robot_a, robot_b, robot_n)

        def bias(valid):
            return jnp.where(valid, jnp.float32(0), jnp.float32(LOW))

        zero = jnp.float32(0)
        self.a = (bias(self.wide_below), bias(start_a <= frame_a - 1), zero)
        self.b = (bias(start_b <= frame_a - 1), bias(start_b <= frame_a), zero)
        self.n = (zero, zero, zero)
        self.scale_a = jnp.where(self.wide_below, 0.0, 1.0).astype(F32)
        self.scale_n = jnp.where(self.wide_above, 1.0, 0.0).astype(F32)


def shifts(view, masks, adapters, adapted, adapted_t):
    for n, (act, robot) in enumerate(zip(view.actions(), masks.robots)):
        table = adapters[robot]
        adapted[n * TOK:(n + 1) * TOK, :] = dot(act, table, 1, 1).astype(BF16)
        if adapted_t is not None:
            adapted_t[:, n * TOK:(n + 1) * TOK] = dot(table, act, 1, 1).astype(BF16)


def narrow_head(view, masks, adapted, up_h, j):
    none = jnp.zeros((TOK, TOK), BF16)
    shift = dot(adapted[: 2 * TOK], up_h, 1, 0)
    query = (column(view.both(0, 0, j)).astype(F32) + shift).astype(BF16)
    grad = column(view.both(1, 0, j))
    keys = column([view.lower(2, j), view.lower(0, j)] + view.both(2, 0, j))
    values = column([view.lower(3, j), view.lower(1, j)] + view.both(3, 0, j))
    raw = dot(keys, query, 1, 1)
    prod = dot(values, grad, 1, 1)
    prob_a, dscore_a = soften([block(raw, i, 0) for i in range(3)], [block(prod, i, 0) for i in range(3)], masks.a)
    prob_b, dscore_b = soften([block(raw, i, 1) for i in range(1, 4)], [block(prod, i, 1) for i in range(1, 4)], masks.b)
    prob = jnp.concatenate([column(prob_a + [none]), column([none] + prob_b)], 1)
    dscore = jnp.concatenate([column(dscore_a + [none]), column([none] + dscore_b)], 1)
    return query, grad, keys, prob, dscore


def wide_head(view, masks, adapted, up_h, j):
    none = jnp.zeros((TOK, TOK), BF16)
    shift = dot(adapted[...], up_h, 1, 0)
    query = (column(view.both(0, 1, j) + [view.upper(0, j)]).astype(F32) + shift).astype(BF16)
    grad = column(view.both(1, 1, j) + [view.upper(1, j)])
    keys = column([view.lower(2, j)] + view.both(2, 1, j) + [view.upper(2, j)])
    values = column([view.lower(3, j)] + view.both(3, 1, j) + [view.upper(3, j)])
    raw = dot(keys[: 3 * TOK], query[: 2 * TOK], 1, 1)
    prod = dot(values[: 3 * TOK], grad[: 2 * TOK], 1, 1)
    raw_n = dot(keys[TOK:], query[2 * TOK:], 1, 1)
    prod_n = dot(values[TOK:], grad[2 * TOK:], 1, 1)
    prob_a, dscore_a = soften(
        [block(raw, i, 0) for i in range(2)], [block(prod, i, 0) for i in range(2)], masks.a[1:], masks.scale_a
    )
    prob_b, dscore_b = soften([block(raw, i, 1) for i in range(3)], [block(prod, i, 1) for i in range(3)], masks.b)
    prob_n, dscore_n = soften(
        [block(raw_n, i, 0) for i in range(3)], [block(prod_n, i, 0) for i in range(3)], masks.n, masks.scale_n
    )
    prob = jnp.concatenate([column(prob_a + [none, none]), column(prob_b + [none]), column([none] + prob_n)], 1)
    dscore = jnp.concatenate([column(dscore_a + [none, none]), column(dscore_b + [none]), column([none] + dscore_n)], 1)
    return query, grad, keys, prob, dscore


def rows_kernel(
    clips, place, lengths, robots, adapters, near, oth, below, above, up_hbm, payload,
    up, adapted, adapted_t, agrad_t, pay, sem,
):
    view = Views(place, near, oth, below, above)
    half, quarter = view.half, view.quarter
    five = quarter // HEAD
    load = pltpu.make_async_copy(
        up_hbm.at[:, pl.ds(pl.multiple_of(place[0] * half, HEAD), half)], up, sem.at[0]
    )
    load.start()
    masks = Masks(clips, place, lengths, robots)
    shifts(view, masks, adapters, adapted, adapted_t)
    agrad_t[...] = jnp.zeros_like(agrad_t)
    pay[:, 2 * five:, :] = jnp.zeros((RANK, ROWS - 2 * five, HEAD), F32)
    load.wait()

    def sums(keys, dscore, up_h, rows, head):
        query_grad = dot(keys, dscore, 0, 0)
        high = query_grad.astype(BF16)
        low = (query_grad - high.astype(F32)).astype(BF16)
        agrad_t[:, :rows] += dot(up_h, high, 1, 0) + dot(up_h, low, 1, 0)
        term = dot(adapted_t[:, :rows], high, 1, 1) + dot(adapted_t[:, :rows], low, 1, 1)
        pay[:, head, :] = term

    for j in range(five):
        up_h = up[:, j * HEAD:(j + 1) * HEAD]
        _, _, keys, _, dscore = narrow_head(view, masks, adapted, up_h, j)
        sums(keys, dscore, up_h, 2 * TOK, j)
        up_h = up[:, quarter + j * HEAD:quarter + (j + 1) * HEAD]
        _, _, keys, _, dscore = wide_head(view, masks, adapted, up_h, j)
        sums(keys, dscore, up_h, 3 * TOK, five + j)

    terms = []
    for n, act in enumerate(view.actions()):
        whole = agrad_t[:, n * TOK:(n + 1) * TOK]
        high = whole.astype(BF16)
        low = (whole - high.astype(F32)).astype(BF16)
        terms.append(dot(high, act, 1, 0) + dot(low, act, 1, 0))
    blank = jnp.zeros((RANK, HEAD), F32)
    for s in range(4):
        pay[:, 2 * five + s, :] = functools.reduce(
            jnp.add, [jnp.where(robot == s, term, blank) for robot, term in zip(masks.robots, terms)]
        )
    payload[...] = pay[...].astype(BF16)


def rows_call(scalars, adapters, near, oth, below, above, up):
    half = up.shape[1] // 2
    five = half // 2 // HEAD
    return pl.pallas_call(
        functools.partial(rows_kernel, scalars[1].shape[0]),
        in_specs=[smem()] * 3 + [vmem()] * 5 + [hbm()],
        out_specs=vmem(),
        out_shape=jax.ShapeDtypeStruct((RANK, ROWS, HEAD), BF16),
        scratch_shapes=[
            pltpu.VMEM((RANK, half), BF16),
            pltpu.VMEM((3 * TOK, RANK), BF16),
            pltpu.VMEM((RANK, 3 * TOK), BF16),
            pltpu.VMEM((RANK, 3 * TOK), F32),
            pltpu.VMEM((RANK, ROWS, HEAD), F32),
            pltpu.SemaphoreType.DMA((1,)),
        ],
        compiler_params=pltpu.CompilerParams(vmem_limit_bytes=16 * MIB),
        cost_estimate=pl.CostEstimate(
            flops=2 * five * 7 * 512 * 256 * 128, bytes_accessed=12 * MIB, transcendentals=five * 1024 * 256
        ),
        name="attend_rows",
    )(*scalars, adapters, near, oth, below, above, fixed(up))


def keys_kernel(
    clips, place, lengths, robots, adapters, oth, below, above, q, g, k, v, act, up_hbm,
    sum_a, sum_b, ret_down, ret_up,
    near, up, adapted, keep_a, keep_b, keep_down, keep_up, sem_in, sem_out,
):
    view = Views(place, near, oth, below, above)
    half, quarter = view.half, view.quarter
    five = quarter // HEAD
    side = pl.ds(pl.multiple_of(place[0] * half, HEAD), half)
    pairs = [(x.at[:, side], near.at[:, pl.ds(n * half, half)]) for n, x in enumerate((q, g, k, v))]
    pairs += [(act, near.at[:, pl.ds(4 * half, HEAD)]), (up_hbm.at[:, side], up)]
    loads = [pltpu.make_async_copy(x, y, sem_in.at[n]) for n, (x, y) in enumerate(pairs)]
    for load in loads:
        load.start()
    masks = Masks(clips, place, lengths, robots)
    for load in loads:
        load.wait()
    shifts(view, masks, adapters, adapted, None)
    stores = []
    for j in range(five):
        cols = slice(j * HEAD, (j + 1) * HEAD)
        query, grad, _, prob, dscore = narrow_head(view, masks, adapted, up[:, cols], j)
        wide_parts = []
        for n, part in enumerate((dot(dscore, query, 1, 0), dot(prob, grad, 1, 0))):
            wide_parts.append(part[:TOK])
            keep_down[n, :, cols] = part[TOK:2 * TOK].astype(BF16)
            keep_a[n, 0, :, cols] = part[2 * TOK:3 * TOK]
            keep_b[n, 0, :, cols] = part[3 * TOK:]
        up_h = up[:, quarter + j * HEAD:quarter + (j + 1) * HEAD]
        query, grad, _, prob, dscore = wide_head(view, masks, adapted, up_h, j)
        for n, part in enumerate((dot(dscore, query, 1, 0), dot(prob, grad, 1, 0))):
            keep_down[2 + n, :, cols] = jnp.where(masks.wide_below, wide_parts[n], part[:TOK]).astype(BF16)
            keep_a[n, 1, :, cols] = part[TOK:2 * TOK]
            keep_b[n, 1, :, cols] = part[2 * TOK:3 * TOK]
            keep_up[n, :, cols] = part[3 * TOK:].astype(BF16)
        span = pl.ds(j * HEAD, HEAD)
        for n, (x, y) in enumerate(((keep_down, ret_down), (keep_up, ret_up), (keep_a, sum_a), (keep_b, sum_b))):
            at = (slice(None),) * (len(x.shape) - 1) + (span,)
            stores.append(pltpu.make_async_copy(x.at[at], y.at[at], sem_out.at[j, n]))
            stores[-1].start()
    for store in stores:
        store.wait()


def keys_call(scalars, adapters, oth, below, above, own, act, up):
    half = up.shape[1] // 2
    quarter = half // 2
    five = quarter // HEAD
    shapes = [((4, TOK, quarter), BF16), ((2, TOK, quarter), BF16)]
    sums = ((2, 2, TOK, quarter), F32)
    return pl.pallas_call(
        functools.partial(keys_kernel, scalars[1].shape[0]),
        in_specs=[smem()] * 3 + [vmem()] * 4 + [hbm()] * 6,
        out_specs=[hbm()] * 4,
        out_shape=[pltpu.HBM(*x) for x in (sums, sums, *shapes)],
        scratch_shapes=[
            pltpu.VMEM((TOK, 4 * half + HEAD), BF16),
            pltpu.VMEM((RANK, half), BF16),
            pltpu.VMEM((3 * TOK, RANK), BF16),
            pltpu.VMEM(*sums),
            pltpu.VMEM(*sums),
            pltpu.VMEM(*shapes[0]),
            pltpu.VMEM(*shapes[1]),
            pltpu.SemaphoreType.DMA((6,)),
            pltpu.SemaphoreType.DMA((five, 4)),
        ],
        compiler_params=pltpu.CompilerParams(vmem_limit_bytes=24 * MIB),
        cost_estimate=pl.CostEstimate(
            flops=2 * five * 9 * 512 * 256 * 128, bytes_accessed=10 * MIB, transcendentals=five * 1024 * 256
        ),
        name="attend_keys",
    )(*scalars, adapters, oth, below, above, *(fixed(x) for x in (*own, act, up)))


def join_kernel(
    clips, place, lengths, robots, sum_a_hbm, sum_b_hbm, above, below, mine, theirs, sum_a, sum_b, sems
):
    loads = [
        pltpu.make_async_copy(x.at[n], y.at[n], sems.at[2 * m + n])
        for m, (x, y) in enumerate(((sum_a_hbm, sum_a), (sum_b_hbm, sum_b)))
        for n in range(2)
    ]
    for load in loads:
        load.start()
    first = place[0] == 0
    frame_a = 2 * place[1]
    start_n, _ = clip_of(frame_a + 2, lengths, robots, clips)
    wide = start_n == frame_a
    quarter = above.shape[2]
    for n in range(2):
        loads[n].wait()
        loads[2 + n].wait()
        for group in range(2):
            second = above[2 + n].astype(F32)
            if group == 0:
                a = sum_a[n, 0] + jnp.where(wide, second, 0.0)
                b = sum_b[n, 0] + above[n].astype(F32)
            else:
                a = sum_a[n, 1] + below[n].astype(F32)
                b = sum_b[n, 1] + jnp.where(wide, 0.0, second)
            cols = slice(group * quarter, (group + 1) * quarter)
            mine[n, :, cols] = jnp.where(first, a, b).astype(BF16)
            theirs[n, :, cols] = jnp.where(first, b, a).astype(BF16)


def join(scalars, sum_a, sum_b, above, below):
    shape = (2, TOK, 2 * above.shape[2])
    return pl.pallas_call(
        functools.partial(join_kernel, scalars[1].shape[0]),
        in_specs=[smem()] * 3 + [hbm()] * 2 + [vmem()] * 2,
        out_specs=[vmem()] * 2,
        out_shape=[pltpu.VMEM(shape, BF16), pltpu.VMEM(shape, BF16)],
        scratch_shapes=[
            pltpu.VMEM(sum_a.shape, F32), pltpu.VMEM(sum_b.shape, F32), pltpu.SemaphoreType.DMA((4,))
        ],
        compiler_params=pltpu.CompilerParams(vmem_limit_bytes=8 * MIB),
        cost_estimate=pl.CostEstimate(flops=MIB, bytes_accessed=6 * MIB, transcendentals=0),
        name="join",
    )(*scalars, fixed(sum_a), fixed(sum_b), above, below)


def place_kernel(place, mine, other, key_grad, value_grad, sems):
    half = mine.shape[2]
    copies = []
    for n, out in enumerate((key_grad, value_grad)):
        for side, source in ((place[0], mine), (1 - place[0], other)):
            cols = pl.ds(pl.multiple_of(side * half, HEAD), half)
            copies.append(pltpu.make_async_copy(source.at[n], out.at[:, cols], sems.at[len(copies)]))
    for copy in copies:
        copy.start()
    for copy in copies:
        copy.wait()


def place_halves(place, mine, other):
    shape = (TOK, 2 * mine.shape[2])
    return pl.pallas_call(
        place_kernel,
        in_specs=[smem()] + [vmem()] * 2,
        out_specs=[hbm()] * 2,
        out_shape=[pltpu.HBM(shape, BF16), pltpu.HBM(shape, BF16)],
        scratch_shapes=[pltpu.SemaphoreType.DMA((4,))],
        compiler_params=pltpu.CompilerParams(vmem_limit_bytes=4 * MIB),
        cost_estimate=pl.CostEstimate(flops=0, bytes_accessed=4 * MIB, transcendentals=0),
        name="place_halves",
    )(place, mine, other)


def first_sum_kernel(nz, ny, pieces, out):
    for y in range(ny):
        total = functools.reduce(jnp.add, [pieces[z * ny + y].astype(F32) for z in range(nz)]).astype(BF16)
        for n in range(out.shape[0]):
            out[n, y] = total


def first_sum(pieces, nz, ny, peers):
    return pl.pallas_call(
        functools.partial(first_sum_kernel, nz, ny),
        in_specs=[vmem()],
        out_specs=vmem(),
        out_shape=pltpu.VMEM((peers, ny, ROWS, HEAD), BF16),
        compiler_params=pltpu.CompilerParams(vmem_limit_bytes=2 * MIB),
        name="first_sum",
    )(pieces)


def second_sum_kernel(nz, ny, up_rows, pieces, out):
    totals = [functools.reduce(jnp.add, [pieces[n, y].astype(F32) for n in range(pieces.shape[0])]) for y in range(ny)]
    everything = functools.reduce(jnp.add, totals)
    is_up = lax.broadcasted_iota(jnp.int32, (ROWS, HEAD), 0) < up_rows
    for y in range(ny):
        message = jnp.where(is_up, everything, totals[y]).astype(BF16)
        for z in range(nz):
            out[z * ny + y] = message


def second_sum(pieces, nz, ny, up_rows):
    return pl.pallas_call(
        functools.partial(second_sum_kernel, nz, ny, up_rows),
        in_specs=[vmem()],
        out_specs=vmem(),
        out_shape=pltpu.VMEM((nz * ny, ROWS, HEAD), BF16),
        compiler_params=pltpu.CompilerParams(vmem_limit_bytes=2 * MIB),
        name="second_sum",
    )(pieces)


def finish_kernel(heads, place, gathered, swapped, up_grad, adapter_grad, one, two):
    per_core = heads // 2
    one[...] = gathered[...].astype(F32)
    two[...] = swapped[...].astype(F32)
    for n, part in enumerate((one, two)):
        side = place[0] if n == 0 else 1 - place[0]
        for h in range(per_core):
            cols = pl.ds(pl.multiple_of((side * per_core + h) * HEAD, HEAD), HEAD)
            up_grad[:, cols] = part[:, h, :]
    for s in range(4):
        adapter_grad[s] = one[:, per_core + s, :] + two[:, per_core + s, :]


def finish(place, gathered, swapped, heads):
    return pl.pallas_call(
        functools.partial(finish_kernel, heads),
        in_specs=[smem(), vmem(), vmem()],
        out_specs=[vmem(), vmem()],
        out_shape=[
            jax.ShapeDtypeStruct((RANK, heads * HEAD), F32),
            jax.ShapeDtypeStruct((4, RANK, HEAD), F32),
        ],
        scratch_shapes=[pltpu.VMEM((RANK, ROWS, HEAD), F32), pltpu.VMEM((RANK, ROWS, HEAD), F32)],
        compiler_params=pltpu.CompilerParams(vmem_limit_bytes=6 * MIB),
        name="finish",
    )(place, gathered, swapped)


def local(
    query_tokens, key_tokens, value_tokens, out_grad, actions, clip_lengths, clip_robots, adapters, up_proj,
):
    q, k, v, g = (t[0, 0] for t in (query_tokens, key_tokens, value_tokens, out_grad))
    act = actions[0, 0]
    heads = q.shape[1] // HEAD
    core = lax.axis_index("core")
    nz, ny = lax.axis_size("z"), lax.axis_size("y")
    chips = lax.axis_size("x") * nz
    chip = lax.axis_index("x") * nz + lax.axis_index("z")
    chain = ("x", "z")
    swap = [(0, 1), (1, 0)]
    upward = [(c, c + 1) for c in range(chips - 1)]
    downward = [(c + 1, c) for c in range(chips - 1)]
    place = jnp.stack([core, chip]).astype(jnp.int32)
    scalars = (place, clip_lengths[0, 0], clip_robots[0, 0])
    own = (q, g, k, v)
    oth = lax.ppermute(take_half(place, own, act, True), "core", swap)
    near = take_half(place, own, act, False)
    up_msg, down_msg = pack(scalars, near, oth)
    below = lax.ppermute(up_msg, chain, upward)
    above = lax.ppermute(down_msg, chain, downward)
    table = jnp.swapaxes(adapters[0], 1, 2)
    payload = rows_call(scalars, table, near, oth, below, above, up_proj)

    plane, line = ("z", "y"), ("dp", "x")
    peers = lax.axis_size("dp") * lax.axis_size("x")
    pieces = lax.all_to_all(payload, plane, 0, 0, tiled=True)
    pieces = lax.all_to_all(first_sum(pieces, nz, ny, peers), line, 0, 0, tiled=True)
    gathered = lax.all_to_all(second_sum(pieces, nz, ny, heads // 2), plane, 0, 0, tiled=True)
    swapped = lax.ppermute(gathered, "core", swap)
    up_total, adapter_total = finish(place, gathered, swapped, heads)
    adapter_total = jnp.swapaxes(adapter_total, 1, 2)

    sum_a, sum_b, ret_down, ret_up = keys_call(scalars, table, oth, below, above, own, act, up_proj)
    from_above = lax.ppermute(ret_down, chain, downward)
    from_below = lax.ppermute(ret_up, chain, upward)
    mine, theirs = join(scalars, sum_a, sum_b, from_above, from_below)
    key_grad, value_grad = place_halves(place, mine, lax.ppermute(theirs, "core", swap))
    return key_grad[None, None], value_grad[None, None], adapter_total[None], up_total


def solution(mesh):
    sizes = dict(mesh.shape)
    wide = Mesh(
        mesh.devices.reshape(sizes["dp"], 2, sizes["context"] // 4, 2, sizes["embodime"]),
        ("dp", "x", "z", "core", "y"),
    )
    frames = P("dp", "y", ("x", "z", "core"), None)
    rows = P("dp", "y", None)
    return jax.shard_map(
        local,
        mesh=wide,
        in_specs=(frames,) * 5 + (rows, rows, P("y", None, None, None), P()),
        out_specs=(frames, frames, P("y", None, None, None), P()),
        check_vma=False,
    )
```

```python
import functools
import math

import jax
import jax.numpy as jnp
from jax import lax
from jax.experimental import pallas as pl
from jax.experimental.pallas import tpu as pltpu
from jax.sharding import Mesh, PartitionSpec as P

HEAD = 128
TOK = 128
RANK = 64
LOW = -1e30
SCALE = HEAD**-0.5
SCALE2 = SCALE * math.log2(math.e)
F32 = jnp.float32
BF16 = jnp.bfloat16
ROWS = 16
MIB = 1024 * 1024


def dot(a, b, ca, cb):
    return lax.dot_general(a, b, (((ca,), (cb,)), ((), ())), preferred_element_type=F32)


def clip_of(frame, lengths, robots, clips):
    begin = jnp.int32(0)
    start = jnp.int32(0)
    robot = jnp.int32(0)
    for i in range(clips):
        size = lengths[i]
        inside = jnp.logical_and(frame >= begin, frame < begin + size)
        start = jnp.where(inside, begin, start)
        robot = jnp.where(inside, robots[i], robot)
        begin = begin + size
    return start, robot


def smem():
    return pl.BlockSpec(memory_space=pltpu.SMEM)


def vmem():
    return pl.BlockSpec(memory_space=pltpu.VMEM)


def hbm():
    return pl.BlockSpec(memory_space=pl.ANY)


def fixed(x):
    return pltpu.with_memory_space_constraint(x, pltpu.HBM)


def take_kernel(far, place, q, g, k, v, act, out, sems):
    half = q.shape[1] // 2
    side = 1 - place[0] if far else place[0]
    copies = [
        pltpu.make_async_copy(
            x.at[:, pl.ds(pl.multiple_of(side * half, HEAD), half)], out.at[:, pl.ds(n * half, half)], sems.at[n]
        )
        for n, x in enumerate((q, g, k, v))
    ]
    copies.append(pltpu.make_async_copy(act, out.at[:, pl.ds(4 * half, HEAD)], sems.at[4]))
    for copy in copies:
        copy.start()
    for copy in copies:
        copy.wait()


def take_half(place, own, act, far):
    half = own[0].shape[1] // 2
    return pl.pallas_call(
        functools.partial(take_kernel, far),
        in_specs=[smem()] + [hbm()] * 5,
        out_specs=vmem(),
        out_shape=pltpu.VMEM((TOK, 4 * half + HEAD), BF16),
        scratch_shapes=[pltpu.SemaphoreType.DMA((5,))],
        compiler_params=pltpu.CompilerParams(vmem_limit_bytes=8 * MIB),
        cost_estimate=pl.CostEstimate(flops=0, bytes_accessed=4 * MIB, transcendentals=0),
        name="take_far" if far else "take_near",
    )(place, *(fixed(x) for x in own), fixed(act))


def pack_kernel(clips, place, lengths, robots, near, oth, up, down):
    half = near.shape[1] // 4 // HEAD * HEAD
    quarter = half // 2
    first = place[0] == 0
    frame_a = 2 * place[1]
    start_n, _ = clip_of(frame_a + 2, lengths, robots, clips)
    wide = start_n == frame_a

    def frame(is_a, array, group):
        at = array * half + group * quarter
        one, two = near[:, at:at + quarter], oth[:, at:at + quarter]
        return jnp.where(first, one, two) if is_a else jnp.where(first, two, one)

    for n, array in enumerate((2, 3)):
        up[:, n * quarter:(n + 1) * quarter] = frame(False, array, 0)
        up[:, (2 + n) * quarter:(3 + n) * quarter] = jnp.where(wide, frame(True, array, 0), frame(False, array, 1))
    for n in range(4):
        down[:, n * quarter:(n + 1) * quarter] = frame(True, n, 1)
    one, two = near[:, 4 * half:], oth[:, 4 * half:]
    down[:, 4 * quarter:] = jnp.where(first, one, two)


def pack(scalars, near, oth):
    quarter = near.shape[1] // 4 // HEAD * HEAD // 2
    return pl.pallas_call(
        functools.partial(pack_kernel, scalars[1].shape[0]),
        in_specs=[smem()] * 3 + [vmem()] * 2,
        out_specs=[vmem()] * 2,
        out_shape=[pltpu.VMEM((TOK, 4 * quarter), BF16), pltpu.VMEM((TOK, 4 * quarter + HEAD), BF16)],
        compiler_params=pltpu.CompilerParams(vmem_limit_bytes=8 * MIB),
        cost_estimate=pl.CostEstimate(flops=0, bytes_accessed=4 * MIB, transcendentals=0),
        name="pack",
    )(*scalars, near, oth)


class Views:
    def __init__(self, place, near, oth, below, above):
        self.first = place[0] == 0
        self.near, self.oth, self.below, self.above = near, oth, below, above
        self.half = near.shape[1] // 4 // HEAD * HEAD
        self.quarter = self.half // 2

    def pick(self, one, two):
        return jnp.where(self.first, one, two)

    def pair(self, one, two):
        return [self.pick(one, two), self.pick(two, one)]

    def both(self, n, group, j):
        at = n * self.half + group * self.quarter + j * HEAD
        return self.pair(self.near[:, at:at + HEAD], self.oth[:, at:at + HEAD])

    def lower(self, n, j):
        at = n * self.quarter + j * HEAD
        return self.below[:, at:at + HEAD]

    def upper(self, n, j):
        at = n * self.quarter + j * HEAD
        return self.above[:, at:at + HEAD]

    def actions(self):
        return self.pair(self.near[:, 4 * self.half:], self.oth[:, 4 * self.half:]) + [self.above[:, 4 * self.quarter:]]


def block(x, i, j):
    return x[i * TOK:(i + 1) * TOK, j * TOK:(j + 1) * TOK]


def column(blocks):
    return jnp.concatenate(blocks, 0)


def soften(raw, prods, biases, keep=None):
    tops = [jnp.max(r, 0, keepdims=True) + b for r, b in zip(raw, biases)]
    top = functools.reduce(jnp.maximum, tops)
    weights = [jnp.exp2(r * SCALE2 + (b - top) * SCALE2) for r, b in zip(raw, biases)]
    total = jnp.sum(functools.reduce(jnp.add, weights), 0, keepdims=True)
    mixed = [w * p for w, p in zip(weights, prods)]
    moment = jnp.sum(functools.reduce(jnp.add, mixed), 0, keepdims=True)
    inverse = 1.0 / total
    if keep is not None:
        inverse = inverse * keep
    delta = moment * inverse
    scaled = inverse * SCALE
    prob = [(w * inverse).astype(BF16) for w in weights]
    dscore = [((w * scaled) * (p - delta)).astype(BF16) for w, p in zip(weights, prods)]
    return prob, dscore


class Masks:
    def __init__(self, clips, place, lengths, robots):
        frame_a = 2 * place[1]
        start_a, robot_a = clip_of(frame_a, lengths, robots, clips)
        start_b, robot_b = clip_of(frame_a + 1, lengths, robots, clips)
        start_n, robot_n = clip_of(frame_a + 2, lengths, robots, clips)
        self.wide_below = start_a == frame_a - 2
        self.wide_above = start_n == frame_a
        self.robots = (robot_a, robot_b, robot_n)

        def bias(valid):
            return jnp.where(valid, jnp.float32(0), jnp.float32(LOW))

        zero = jnp.float32(0)
        self.a = (bias(self.wide_below), bias(start_a <= frame_a - 1), zero)
        self.b = (bias(start_b <= frame_a - 1), bias(start_b <= frame_a), zero)
        self.n = (zero, zero, zero)
        self.scale_a = jnp.where(self.wide_below, 0.0, 1.0).astype(F32)
        self.scale_n = jnp.where(self.wide_above, 1.0, 0.0).astype(F32)


def shifts(view, masks, adapters, adapted, adapted_t):
    for n, (act, robot) in enumerate(zip(view.actions(), masks.robots)):
        table = adapters[robot]
        adapted[n * TOK:(n + 1) * TOK, :] = dot(act, table, 1, 1).astype(BF16)
        if adapted_t is not None:
            adapted_t[:, n * TOK:(n + 1) * TOK] = dot(table, act, 1, 1).astype(BF16)


def narrow_head(view, masks, adapted, up_h, j):
    none = jnp.zeros((TOK, TOK), BF16)
    shift = dot(adapted[: 2 * TOK], up_h, 1, 0)
    query = (column(view.both(0, 0, j)).astype(F32) + shift).astype(BF16)
    grad = column(view.both(1, 0, j))
    keys = column([view.lower(2, j), view.lower(0, j)] + view.both(2, 0, j))
    values = column([view.lower(3, j), view.lower(1, j)] + view.both(3, 0, j))
    raw = dot(keys, query, 1, 1)
    prod = dot(values, grad, 1, 1)
    prob_a, dscore_a = soften([block(raw, i, 0) for i in range(3)], [block(prod, i, 0) for i in range(3)], masks.a)
    prob_b, dscore_b = soften([block(raw, i, 1) for i in range(1, 4)], [block(prod, i, 1) for i in range(1, 4)], masks.b)
    prob = jnp.concatenate([column(prob_a + [none]), column([none] + prob_b)], 1)
    dscore = jnp.concatenate([column(dscore_a + [none]), column([none] + dscore_b)], 1)
    return query, grad, keys, prob, dscore


def wide_head(view, masks, adapted, up_h, j):
    none = jnp.zeros((TOK, TOK), BF16)
    shift = dot(adapted[...], up_h, 1, 0)
    query = (column(view.both(0, 1, j) + [view.upper(0, j)]).astype(F32) + shift).astype(BF16)
    grad = column(view.both(1, 1, j) + [view.upper(1, j)])
    keys = column([view.lower(2, j)] + view.both(2, 1, j) + [view.upper(2, j)])
    values = column([view.lower(3, j)] + view.both(3, 1, j) + [view.upper(3, j)])
    raw = dot(keys[: 3 * TOK], query[: 2 * TOK], 1, 1)
    prod = dot(values[: 3 * TOK], grad[: 2 * TOK], 1, 1)
    raw_n = dot(keys[TOK:], query[2 * TOK:], 1, 1)
    prod_n = dot(values[TOK:], grad[2 * TOK:], 1, 1)
    prob_a, dscore_a = soften(
        [block(raw, i, 0) for i in range(2)], [block(prod, i, 0) for i in range(2)], masks.a[1:], masks.scale_a
    )
    prob_b, dscore_b = soften([block(raw, i, 1) for i in range(3)], [block(prod, i, 1) for i in range(3)], masks.b)
    prob_n, dscore_n = soften(
        [block(raw_n, i, 0) for i in range(3)], [block(prod_n, i, 0) for i in range(3)], masks.n, masks.scale_n
    )
    prob = jnp.concatenate([column(prob_a + [none, none]), column(prob_b + [none]), column([none] + prob_n)], 1)
    dscore = jnp.concatenate([column(dscore_a + [none, none]), column(dscore_b + [none]), column([none] + dscore_n)], 1)
    return query, grad, keys, prob, dscore


def attend_kernel(
    clips, place, lengths, robots, adapters, near, oth, below, above, up_hbm,
    payload, sum_a, sum_b, ret_down, ret_up,
    up, adapted, adapted_t, agrad_t, pay, keep_a, keep_b, keep_down, keep_up, sem_in, sem_out,
):
    view = Views(place, near, oth, below, above)
    half, quarter = view.half, view.quarter
    five = quarter // HEAD
    load = pltpu.make_async_copy(
        up_hbm.at[:, pl.ds(pl.multiple_of(place[0] * half, HEAD), half)], up, sem_in.at[0]
    )
    load.start()
    masks = Masks(clips, place, lengths, robots)
    shifts(view, masks, adapters, adapted, adapted_t)
    agrad_t[...] = jnp.zeros_like(agrad_t)
    pay[:, 2 * five:, :] = jnp.zeros((RANK, ROWS - 2 * five, HEAD), F32)
    load.wait()

    def sums(keys, dscore, up_h, rows, head):
        query_grad = dot(keys, dscore, 0, 0)
        high = query_grad.astype(BF16)
        low = (query_grad - high.astype(F32)).astype(BF16)
        agrad_t[:, :rows] += dot(up_h, high, 1, 0) + dot(up_h, low, 1, 0)
        term = dot(adapted_t[:, :rows], high, 1, 1) + dot(adapted_t[:, :rows], low, 1, 1)
        pay[:, head, :] = term

    stores = []
    for j in range(five):
        cols = slice(j * HEAD, (j + 1) * HEAD)
        up_h = up[:, cols]
        query, grad, keys, prob, dscore = narrow_head(view, masks, adapted, up_h, j)
        sums(keys, dscore, up_h, 2 * TOK, j)
        wide_parts = []
        for n, part in enumerate((dot(dscore, query, 1, 0), dot(prob, grad, 1, 0))):
            wide_parts.append(part[:TOK])
            keep_down[n, :, cols] = part[TOK:2 * TOK].astype(BF16)
            keep_a[n, 0, :, cols] = part[2 * TOK:3 * TOK]
            keep_b[n, 0, :, cols] = part[3 * TOK:]
        up_h = up[:, quarter + j * HEAD:quarter + (j + 1) * HEAD]
        query, grad, keys, prob, dscore = wide_head(view, masks, adapted, up_h, j)
        sums(keys, dscore, up_h, 3 * TOK, five + j)
        for n, part in enumerate((dot(dscore, query, 1, 0), dot(prob, grad, 1, 0))):
            keep_down[2 + n, :, cols] = jnp.where(masks.wide_below, wide_parts[n], part[:TOK]).astype(BF16)
            keep_a[n, 1, :, cols] = part[TOK:2 * TOK]
            keep_b[n, 1, :, cols] = part[2 * TOK:3 * TOK]
            keep_up[n, :, cols] = part[3 * TOK:].astype(BF16)
        span = pl.ds(j * HEAD, HEAD)
        for n, (x, y) in enumerate(((keep_down, ret_down), (keep_up, ret_up), (keep_a, sum_a), (keep_b, sum_b))):
            at = (slice(None),) * (len(x.shape) - 1) + (span,)
            stores.append(pltpu.make_async_copy(x.at[at], y.at[at], sem_out.at[j, n]))
            stores[-1].start()

    terms = []
    for n, act in enumerate(view.actions()):
        whole = agrad_t[:, n * TOK:(n + 1) * TOK]
        high = whole.astype(BF16)
        low = (whole - high.astype(F32)).astype(BF16)
        terms.append(dot(high, act, 1, 0) + dot(low, act, 1, 0))
    blank = jnp.zeros((RANK, HEAD), F32)
    for s in range(4):
        pay[:, 2 * five + s, :] = functools.reduce(
            jnp.add, [jnp.where(robot == s, term, blank) for robot, term in zip(masks.robots, terms)]
        )
    payload[...] = pay[...].astype(BF16)
    for store in stores:
        store.wait()


def attend(scalars, adapters, near, oth, below, above, up):
    half = up.shape[1] // 2
    quarter = half // 2
    five = quarter // HEAD
    shapes = [((4, TOK, quarter), BF16), ((2, TOK, quarter), BF16)]
    sums = ((2, 2, TOK, quarter), F32)
    return pl.pallas_call(
        functools.partial(attend_kernel, scalars[1].shape[0]),
        in_specs=[smem()] * 3 + [vmem()] * 5 + [hbm()],
        out_specs=[vmem()] + [hbm()] * 4,
        out_shape=[jax.ShapeDtypeStruct((RANK, ROWS, HEAD), BF16)] + [pltpu.HBM(*x) for x in (sums, sums, *shapes)],
        scratch_shapes=[
            pltpu.VMEM((RANK, half), BF16),
            pltpu.VMEM((3 * TOK, RANK), BF16),
            pltpu.VMEM((RANK, 3 * TOK), BF16),
            pltpu.VMEM((RANK, 3 * TOK), F32),
            pltpu.VMEM((RANK, ROWS, HEAD), F32),
            pltpu.VMEM(*sums),
            pltpu.VMEM(*sums),
            pltpu.VMEM(*shapes[0]),
            pltpu.VMEM(*shapes[1]),
            pltpu.SemaphoreType.DMA((1,)),
            pltpu.SemaphoreType.DMA((five, 4)),
        ],
        compiler_params=pltpu.CompilerParams(vmem_limit_bytes=24 * MIB),
        cost_estimate=pl.CostEstimate(
            flops=2 * five * 12 * 512 * 256 * 128, bytes_accessed=12 * MIB, transcendentals=five * 1024 * 256
        ),
        name="attend",
    )(*scalars, adapters, near, oth, below, above, fixed(up))


def hold_kernel(down_in, up_in, down_out, up_out):
    pass


def hold(ret_down, ret_up):
    return pl.pallas_call(
        hold_kernel,
        in_specs=[hbm()] * 2,
        out_specs=[hbm()] * 2,
        out_shape=[pltpu.HBM(x.shape, x.dtype) for x in (ret_down, ret_up)],
        input_output_aliases={0: 0, 1: 1},
        compiler_params=pltpu.CompilerParams(vmem_limit_bytes=MIB),
        cost_estimate=pl.CostEstimate(flops=MIB, bytes_accessed=MIB, transcendentals=0),
        name="hold",
    )(fixed(ret_down), fixed(ret_up))


def join_kernel(
    clips, place, lengths, robots, sum_a_hbm, sum_b_hbm, above, below, mine, theirs, sum_a, sum_b, sems
):
    loads = [
        pltpu.make_async_copy(x.at[n], y.at[n], sems.at[2 * m + n])
        for m, (x, y) in enumerate(((sum_a_hbm, sum_a), (sum_b_hbm, sum_b)))
        for n in range(2)
    ]
    for load in loads:
        load.start()
    first = place[0] == 0
    frame_a = 2 * place[1]
    start_n, _ = clip_of(frame_a + 2, lengths, robots, clips)
    wide = start_n == frame_a
    quarter = above.shape[2]
    for n in range(2):
        loads[n].wait()
        loads[2 + n].wait()
        for group in range(2):
            second = above[2 + n].astype(F32)
            if group == 0:
                a = sum_a[n, 0] + jnp.where(wide, second, 0.0)
                b = sum_b[n, 0] + above[n].astype(F32)
            else:
                a = sum_a[n, 1] + below[n].astype(F32)
                b = sum_b[n, 1] + jnp.where(wide, 0.0, second)
            cols = slice(group * quarter, (group + 1) * quarter)
            mine[n, :, cols] = jnp.where(first, a, b).astype(BF16)
            theirs[n, :, cols] = jnp.where(first, b, a).astype(BF16)


def join(scalars, sum_a, sum_b, above, below):
    shape = (2, TOK, 2 * above.shape[2])
    return pl.pallas_call(
        functools.partial(join_kernel, scalars[1].shape[0]),
        in_specs=[smem()] * 3 + [hbm()] * 2 + [vmem()] * 2,
        out_specs=[vmem()] * 2,
        out_shape=[pltpu.VMEM(shape, BF16), pltpu.VMEM(shape, BF16)],
        scratch_shapes=[
            pltpu.VMEM(sum_a.shape, F32), pltpu.VMEM(sum_b.shape, F32), pltpu.SemaphoreType.DMA((4,))
        ],
        compiler_params=pltpu.CompilerParams(vmem_limit_bytes=8 * MIB),
        cost_estimate=pl.CostEstimate(flops=MIB, bytes_accessed=6 * MIB, transcendentals=0),
        name="join",
    )(*scalars, fixed(sum_a), fixed(sum_b), above, below)


def place_kernel(place, mine, other, key_grad, value_grad, sems):
    half = mine.shape[2]
    copies = []
    for n, out in enumerate((key_grad, value_grad)):
        for side, source in ((place[0], mine), (1 - place[0], other)):
            cols = pl.ds(pl.multiple_of(side * half, HEAD), half)
            copies.append(pltpu.make_async_copy(source.at[n], out.at[:, cols], sems.at[len(copies)]))
    for copy in copies:
        copy.start()
    for copy in copies:
        copy.wait()


def place_halves(place, mine, other):
    shape = (TOK, 2 * mine.shape[2])
    return pl.pallas_call(
        place_kernel,
        in_specs=[smem()] + [vmem()] * 2,
        out_specs=[hbm()] * 2,
        out_shape=[pltpu.HBM(shape, BF16), pltpu.HBM(shape, BF16)],
        scratch_shapes=[pltpu.SemaphoreType.DMA((4,))],
        compiler_params=pltpu.CompilerParams(vmem_limit_bytes=4 * MIB),
        cost_estimate=pl.CostEstimate(flops=0, bytes_accessed=4 * MIB, transcendentals=0),
        name="place_halves",
    )(place, mine, other)


def first_sum_kernel(nz, ny, pieces, out):
    for y in range(ny):
        total = functools.reduce(jnp.add, [pieces[z * ny + y].astype(F32) for z in range(nz)]).astype(BF16)
        for n in range(out.shape[0]):
            out[n, y] = total


def first_sum(pieces, nz, ny, peers):
    return pl.pallas_call(
        functools.partial(first_sum_kernel, nz, ny),
        in_specs=[vmem()],
        out_specs=vmem(),
        out_shape=pltpu.VMEM((peers, ny, ROWS, HEAD), BF16),
        compiler_params=pltpu.CompilerParams(vmem_limit_bytes=2 * MIB),
        name="first_sum",
    )(pieces)


def second_sum_kernel(nz, ny, up_rows, pieces, out):
    totals = [functools.reduce(jnp.add, [pieces[n, y].astype(F32) for n in range(pieces.shape[0])]) for y in range(ny)]
    everything = functools.reduce(jnp.add, totals)
    is_up = lax.broadcasted_iota(jnp.int32, (ROWS, HEAD), 0) < up_rows
    for y in range(ny):
        message = jnp.where(is_up, everything, totals[y]).astype(BF16)
        for z in range(nz):
            out[z * ny + y] = message


def second_sum(pieces, nz, ny, up_rows):
    return pl.pallas_call(
        functools.partial(second_sum_kernel, nz, ny, up_rows),
        in_specs=[vmem()],
        out_specs=vmem(),
        out_shape=pltpu.VMEM((nz * ny, ROWS, HEAD), BF16),
        compiler_params=pltpu.CompilerParams(vmem_limit_bytes=2 * MIB),
        name="second_sum",
    )(pieces)


def finish_kernel(heads, place, gathered, swapped, up_grad, adapter_grad, one, two):
    per_core = heads // 2
    one[...] = gathered[...].astype(F32)
    two[...] = swapped[...].astype(F32)
    for n, part in enumerate((one, two)):
        side = place[0] if n == 0 else 1 - place[0]
        for h in range(per_core):
            cols = pl.ds(pl.multiple_of((side * per_core + h) * HEAD, HEAD), HEAD)
            up_grad[:, cols] = part[:, h, :]
    for s in range(4):
        adapter_grad[s] = one[:, per_core + s, :] + two[:, per_core + s, :]


def finish(place, gathered, swapped, heads):
    return pl.pallas_call(
        functools.partial(finish_kernel, heads),
        in_specs=[smem(), vmem(), vmem()],
        out_specs=[vmem(), vmem()],
        out_shape=[
            jax.ShapeDtypeStruct((RANK, heads * HEAD), F32),
            jax.ShapeDtypeStruct((4, RANK, HEAD), F32),
        ],
        scratch_shapes=[pltpu.VMEM((RANK, ROWS, HEAD), F32), pltpu.VMEM((RANK, ROWS, HEAD), F32)],
        compiler_params=pltpu.CompilerParams(vmem_limit_bytes=6 * MIB),
        name="finish",
    )(place, gathered, swapped)


def local(
    query_tokens, key_tokens, value_tokens, out_grad, actions, clip_lengths, clip_robots, adapters, up_proj,
):
    q, k, v, g = (t[0, 0] for t in (query_tokens, key_tokens, value_tokens, out_grad))
    act = actions[0, 0]
    heads = q.shape[1] // HEAD
    core = lax.axis_index("core")
    nz, ny = lax.axis_size("z"), lax.axis_size("y")
    chips = lax.axis_size("x") * nz
    chip = lax.axis_index("x") * nz + lax.axis_index("z")
    chain = ("x", "z")
    swap = [(0, 1), (1, 0)]
    upward = [(c, c + 1) for c in range(chips - 1)]
    downward = [(c + 1, c) for c in range(chips - 1)]
    place = jnp.stack([core, chip]).astype(jnp.int32)
    scalars = (place, clip_lengths[0, 0], clip_robots[0, 0])
    own = (q, g, k, v)
    oth = lax.ppermute(take_half(place, own, act, True), "core", swap)
    near = take_half(place, own, act, False)
    up_msg, down_msg = pack(scalars, near, oth)
    below = lax.ppermute(up_msg, chain, upward)
    above = lax.ppermute(down_msg, chain, downward)
    table = jnp.swapaxes(adapters[0], 1, 2)
    payload, sum_a, sum_b, ret_down, ret_up = attend(scalars, table, near, oth, below, above, up_proj)
    ret_down, ret_up = hold(ret_down, ret_up)

    plane, line = ("z", "y"), ("dp", "x")
    peers = lax.axis_size("dp") * lax.axis_size("x")
    pieces = lax.all_to_all(payload, plane, 0, 0, tiled=True)
    pieces = lax.all_to_all(first_sum(pieces, nz, ny, peers), line, 0, 0, tiled=True)
    from_above = lax.ppermute(ret_down, chain, downward)
    from_below = lax.ppermute(ret_up, chain, upward)
    gathered = lax.all_to_all(second_sum(pieces, nz, ny, heads // 2), plane, 0, 0, tiled=True)
    swapped = lax.ppermute(gathered, "core", swap)
    up_total, adapter_total = finish(place, gathered, swapped, heads)
    adapter_total = jnp.swapaxes(adapter_total, 1, 2)
    mine, theirs = join(scalars, sum_a, sum_b, from_above, from_below)
    key_grad, value_grad = place_halves(place, mine, lax.ppermute(theirs, "core", swap))
    return key_grad[None, None], value_grad[None, None], adapter_total[None], up_total


def solution(mesh):
    sizes = dict(mesh.shape)
    wide = Mesh(
        mesh.devices.reshape(sizes["dp"], 2, sizes["context"] // 4, 2, sizes["embodime"]),
        ("dp", "x", "z", "core", "y"),
    )
    frames = P("dp", "y", ("x", "z", "core"), None)
    rows = P("dp", "y", None)
    return jax.shard_map(
        local,
        mesh=wide,
        in_specs=(frames,) * 5 + (rows, rows, P("y", None, None, None), P()),
        out_specs=(frames, frames, P("y", None, None, None), P()),
        check_vma=False,
    )
```

```python
import functools
import math

import jax
import jax.numpy as jnp
from jax import lax
from jax.experimental import pallas as pl
from jax.experimental.pallas import tpu as pltpu
from jax.sharding import Mesh, PartitionSpec as P

HEAD = 128
TOK = 128
RANK = 64
LOW = -1e30
SCALE = HEAD**-0.5
SCALE2 = SCALE * math.log2(math.e)
F32 = jnp.float32
BF16 = jnp.bfloat16
ROWS = 16
MIB = 1024 * 1024


def dot(a, b, ca, cb):
    return lax.dot_general(a, b, (((ca,), (cb,)), ((), ())), preferred_element_type=F32)


def clip_of(frame, lengths, robots, clips):
    begin = jnp.int32(0)
    start = jnp.int32(0)
    robot = jnp.int32(0)
    for i in range(clips):
        size = lengths[i]
        inside = jnp.logical_and(frame >= begin, frame < begin + size)
        start = jnp.where(inside, begin, start)
        robot = jnp.where(inside, robots[i], robot)
        begin = begin + size
    return start, robot


def smem():
    return pl.BlockSpec(memory_space=pltpu.SMEM)


def vmem():
    return pl.BlockSpec(memory_space=pltpu.VMEM)


def hbm():
    return pl.BlockSpec(memory_space=pl.ANY)


def fixed(x):
    return pltpu.with_memory_space_constraint(x, pltpu.HBM)


def take_kernel(far, place, q, g, k, v, act, out, sems):
    half = q.shape[1] // 2
    side = 1 - place[0] if far else place[0]
    copies = [
        pltpu.make_async_copy(
            x.at[:, pl.ds(pl.multiple_of(side * half, HEAD), half)], out.at[:, pl.ds(n * half, half)], sems.at[n]
        )
        for n, x in enumerate((q, g, k, v))
    ]
    copies.append(pltpu.make_async_copy(act, out.at[:, pl.ds(4 * half, HEAD)], sems.at[4]))
    for copy in copies:
        copy.start()
    for copy in copies:
        copy.wait()


def take_half(place, own, act, far):
    half = own[0].shape[1] // 2
    return pl.pallas_call(
        functools.partial(take_kernel, far),
        in_specs=[smem()] + [hbm()] * 5,
        out_specs=vmem(),
        out_shape=pltpu.VMEM((TOK, 4 * half + HEAD), BF16),
        scratch_shapes=[pltpu.SemaphoreType.DMA((5,))],
        compiler_params=pltpu.CompilerParams(vmem_limit_bytes=8 * MIB),
        cost_estimate=pl.CostEstimate(flops=0, bytes_accessed=4 * MIB, transcendentals=0),
        name="take_far" if far else "take_near",
    )(place, *(fixed(x) for x in own), fixed(act))


def pack_kernel(clips, place, lengths, robots, near, oth, up, down):
    half = near.shape[1] // 4 // HEAD * HEAD
    quarter = half // 2
    first = place[0] == 0
    frame_a = 2 * place[1]
    start_n, _ = clip_of(frame_a + 2, lengths, robots, clips)
    wide = start_n == frame_a

    def frame(is_a, array, group):
        at = array * half + group * quarter
        one, two = near[:, at:at + quarter], oth[:, at:at + quarter]
        return jnp.where(first, one, two) if is_a else jnp.where(first, two, one)

    for n, array in enumerate((2, 3)):
        up[:, n * quarter:(n + 1) * quarter] = frame(False, array, 0)
        up[:, (2 + n) * quarter:(3 + n) * quarter] = jnp.where(wide, frame(True, array, 0), frame(False, array, 1))
    for n in range(4):
        down[:, n * quarter:(n + 1) * quarter] = frame(True, n, 1)
    one, two = near[:, 4 * half:], oth[:, 4 * half:]
    down[:, 4 * quarter:] = jnp.where(first, one, two)


def pack(scalars, near, oth):
    quarter = near.shape[1] // 4 // HEAD * HEAD // 2
    return pl.pallas_call(
        functools.partial(pack_kernel, scalars[1].shape[0]),
        in_specs=[smem()] * 3 + [vmem()] * 2,
        out_specs=[vmem()] * 2,
        out_shape=[pltpu.VMEM((TOK, 4 * quarter), BF16), pltpu.VMEM((TOK, 4 * quarter + HEAD), BF16)],
        compiler_params=pltpu.CompilerParams(vmem_limit_bytes=8 * MIB),
        cost_estimate=pl.CostEstimate(flops=0, bytes_accessed=4 * MIB, transcendentals=0),
        name="pack",
    )(*scalars, near, oth)


class Views:
    def __init__(self, place, near, oth, below, above):
        self.first = place[0] == 0
        self.near, self.oth, self.below, self.above = near, oth, below, above
        self.half = near.shape[1] // 4 // HEAD * HEAD
        self.quarter = self.half // 2

    def pick(self, one, two):
        return jnp.where(self.first, one, two)

    def pair(self, one, two):
        return [self.pick(one, two), self.pick(two, one)]

    def both(self, n, group, j):
        at = n * self.half + group * self.quarter + j * HEAD
        return self.pair(self.near[:, at:at + HEAD], self.oth[:, at:at + HEAD])

    def lower(self, n, j):
        at = n * self.quarter + j * HEAD
        return self.below[:, at:at + HEAD]

    def upper(self, n, j):
        at = n * self.quarter + j * HEAD
        return self.above[:, at:at + HEAD]

    def actions(self):
        return self.pair(self.near[:, 4 * self.half:], self.oth[:, 4 * self.half:]) + [self.above[:, 4 * self.quarter:]]


def block(x, i, j):
    return x[i * TOK:(i + 1) * TOK, j * TOK:(j + 1) * TOK]


def column(blocks):
    return jnp.concatenate(blocks, 0)


def soften(raw, prods, biases, keep=None):
    tops = [jnp.max(r, 0, keepdims=True) + b for r, b in zip(raw, biases)]
    top = functools.reduce(jnp.maximum, tops)
    weights = [jnp.exp2(r * SCALE2 + (b - top) * SCALE2) for r, b in zip(raw, biases)]
    total = jnp.sum(functools.reduce(jnp.add, weights), 0, keepdims=True)
    mixed = [w * p for w, p in zip(weights, prods)]
    moment = jnp.sum(functools.reduce(jnp.add, mixed), 0, keepdims=True)
    inverse = 1.0 / total
    if keep is not None:
        inverse = inverse * keep
    delta = moment * inverse
    scaled = inverse * SCALE
    prob = [(w * inverse).astype(BF16) for w in weights]
    dscore = [((w * scaled) * (p - delta)).astype(BF16) for w, p in zip(weights, prods)]
    return prob, dscore


class Masks:
    def __init__(self, clips, place, lengths, robots):
        frame_a = 2 * place[1]
        start_a, robot_a = clip_of(frame_a, lengths, robots, clips)
        start_b, robot_b = clip_of(frame_a + 1, lengths, robots, clips)
        start_n, robot_n = clip_of(frame_a + 2, lengths, robots, clips)
        self.wide_below = start_a == frame_a - 2
        self.wide_above = start_n == frame_a
        self.robots = (robot_a, robot_b, robot_n)

        def bias(valid):
            return jnp.where(valid, jnp.float32(0), jnp.float32(LOW))

        zero = jnp.float32(0)
        self.a = (bias(self.wide_below), bias(start_a <= frame_a - 1), zero)
        self.b = (bias(start_b <= frame_a - 1), bias(start_b <= frame_a), zero)
        self.n = (zero, zero, zero)
        self.scale_a = jnp.where(self.wide_below, 0.0, 1.0).astype(F32)
        self.scale_n = jnp.where(self.wide_above, 1.0, 0.0).astype(F32)


def shifts(view, masks, adapters, adapted, adapted_t):
    for n, (act, robot) in enumerate(zip(view.actions(), masks.robots)):
        table = adapters[robot]
        adapted[n * TOK:(n + 1) * TOK, :] = dot(act, table, 1, 1).astype(BF16)
        if adapted_t is not None:
            adapted_t[:, n * TOK:(n + 1) * TOK] = dot(table, act, 1, 1).astype(BF16)


def narrow_head(view, masks, adapted, up_h, j):
    none = jnp.zeros((TOK, TOK), BF16)
    shift = dot(adapted[: 2 * TOK], up_h, 1, 0)
    query = (column(view.both(0, 0, j)).astype(F32) + shift).astype(BF16)
    grad = column(view.both(1, 0, j))
    keys = column([view.lower(2, j), view.lower(0, j)] + view.both(2, 0, j))
    values = column([view.lower(3, j), view.lower(1, j)] + view.both(3, 0, j))
    raw = dot(keys, query, 1, 1)
    prod = dot(values, grad, 1, 1)
    prob_a, dscore_a = soften([block(raw, i, 0) for i in range(3)], [block(prod, i, 0) for i in range(3)], masks.a)
    prob_b, dscore_b = soften([block(raw, i, 1) for i in range(1, 4)], [block(prod, i, 1) for i in range(1, 4)], masks.b)
    prob = jnp.concatenate([column(prob_a + [none]), column([none] + prob_b)], 1)
    dscore = jnp.concatenate([column(dscore_a + [none]), column([none] + dscore_b)], 1)
    return query, grad, keys, prob, dscore


def wide_head(view, masks, adapted, up_h, j):
    none = jnp.zeros((TOK, TOK), BF16)
    shift = dot(adapted[...], up_h, 1, 0)
    query = (column(view.both(0, 1, j) + [view.upper(0, j)]).astype(F32) + shift).astype(BF16)
    grad = column(view.both(1, 1, j) + [view.upper(1, j)])
    keys = column([view.lower(2, j)] + view.both(2, 1, j) + [view.upper(2, j)])
    values = column([view.lower(3, j)] + view.both(3, 1, j) + [view.upper(3, j)])
    raw = dot(keys[: 3 * TOK], query[: 2 * TOK], 1, 1)
    prod = dot(values[: 3 * TOK], grad[: 2 * TOK], 1, 1)
    raw_n = dot(keys[TOK:], query[2 * TOK:], 1, 1)
    prod_n = dot(values[TOK:], grad[2 * TOK:], 1, 1)
    prob_a, dscore_a = soften(
        [block(raw, i, 0) for i in range(2)], [block(prod, i, 0) for i in range(2)], masks.a[1:], masks.scale_a
    )
    prob_b, dscore_b = soften([block(raw, i, 1) for i in range(3)], [block(prod, i, 1) for i in range(3)], masks.b)
    prob_n, dscore_n = soften(
        [block(raw_n, i, 0) for i in range(3)], [block(prod_n, i, 0) for i in range(3)], masks.n, masks.scale_n
    )
    prob = jnp.concatenate([column(prob_a + [none, none]), column(prob_b + [none]), column([none] + prob_n)], 1)
    dscore = jnp.concatenate([column(dscore_a + [none, none]), column(dscore_b + [none]), column([none] + dscore_n)], 1)
    return query, grad, keys, prob, dscore


def attend_kernel(
    clips, place, lengths, robots, adapters, near, oth, below, above, up_hbm,
    payload, sum_a, sum_b, ret_down, ret_up,
    up, adapted, adapted_t, agrad_t, pay, keep_a, keep_b, keep_down, keep_up, sem_in, sem_out,
):
    view = Views(place, near, oth, below, above)
    half, quarter = view.half, view.quarter
    five = quarter // HEAD
    load = pltpu.make_async_copy(
        up_hbm.at[:, pl.ds(pl.multiple_of(place[0] * half, HEAD), half)], up, sem_in.at[0]
    )
    load.start()
    masks = Masks(clips, place, lengths, robots)
    shifts(view, masks, adapters, adapted, adapted_t)
    agrad_t[...] = jnp.zeros_like(agrad_t)
    pay[:, 2 * five:, :] = jnp.zeros((RANK, ROWS - 2 * five, HEAD), F32)
    load.wait()

    def sums(keys, dscore, up_h, rows, head):
        query_grad = dot(keys, dscore, 0, 0)
        high = query_grad.astype(BF16)
        low = (query_grad - high.astype(F32)).astype(BF16)
        agrad_t[:, :rows] += dot(up_h, high, 1, 0) + dot(up_h, low, 1, 0)
        term = dot(adapted_t[:, :rows], high, 1, 1) + dot(adapted_t[:, :rows], low, 1, 1)
        pay[:, head, :] = term

    stores = []
    for j in range(five):
        cols = slice(j * HEAD, (j + 1) * HEAD)
        up_h = up[:, cols]
        query, grad, keys, prob, dscore = narrow_head(view, masks, adapted, up_h, j)
        sums(keys, dscore, up_h, 2 * TOK, j)
        wide_parts = []
        for n, part in enumerate((dot(dscore, query, 1, 0), dot(prob, grad, 1, 0))):
            wide_parts.append(part[:TOK])
            keep_down[n, :, cols] = part[TOK:2 * TOK].astype(BF16)
            keep_a[n, 0, :, cols] = part[2 * TOK:3 * TOK]
            keep_b[n, 0, :, cols] = part[3 * TOK:]
        up_h = up[:, quarter + j * HEAD:quarter + (j + 1) * HEAD]
        query, grad, keys, prob, dscore = wide_head(view, masks, adapted, up_h, j)
        sums(keys, dscore, up_h, 3 * TOK, five + j)
        for n, part in enumerate((dot(dscore, query, 1, 0), dot(prob, grad, 1, 0))):
            keep_down[2 + n, :, cols] = jnp.where(masks.wide_below, wide_parts[n], part[:TOK]).astype(BF16)
            keep_a[n, 1, :, cols] = part[TOK:2 * TOK]
            keep_b[n, 1, :, cols] = part[2 * TOK:3 * TOK]
            keep_up[n, :, cols] = part[3 * TOK:].astype(BF16)
        span = pl.ds(j * HEAD, HEAD)
        for n, (x, y) in enumerate(((keep_down, ret_down), (keep_up, ret_up), (keep_a, sum_a), (keep_b, sum_b))):
            at = (slice(None),) * (len(x.shape) - 1) + (span,)
            stores.append(pltpu.make_async_copy(x.at[at], y.at[at], sem_out.at[j, n]))
            stores[-1].start()

    terms = []
    for n, act in enumerate(view.actions()):
        whole = agrad_t[:, n * TOK:(n + 1) * TOK]
        high = whole.astype(BF16)
        low = (whole - high.astype(F32)).astype(BF16)
        terms.append(dot(high, act, 1, 0) + dot(low, act, 1, 0))
    blank = jnp.zeros((RANK, HEAD), F32)
    for s in range(4):
        pay[:, 2 * five + s, :] = functools.reduce(
            jnp.add, [jnp.where(robot == s, term, blank) for robot, term in zip(masks.robots, terms)]
        )
    payload[...] = pay[...].astype(BF16)
    for store in stores:
        store.wait()


def attend(scalars, adapters, near, oth, below, above, up):
    half = up.shape[1] // 2
    quarter = half // 2
    five = quarter // HEAD
    shapes = [((4, TOK, quarter), BF16), ((2, TOK, quarter), BF16)]
    sums = ((2, 2, TOK, quarter), F32)
    return pl.pallas_call(
        functools.partial(attend_kernel, scalars[1].shape[0]),
        in_specs=[smem()] * 3 + [vmem()] * 5 + [hbm()],
        out_specs=[vmem()] + [hbm()] * 4,
        out_shape=[jax.ShapeDtypeStruct((RANK, ROWS, HEAD), BF16)] + [pltpu.HBM(*x) for x in (sums, sums, *shapes)],
        scratch_shapes=[
            pltpu.VMEM((RANK, half), BF16),
            pltpu.VMEM((3 * TOK, RANK), BF16),
            pltpu.VMEM((RANK, 3 * TOK), BF16),
            pltpu.VMEM((RANK, 3 * TOK), F32),
            pltpu.VMEM((RANK, ROWS, HEAD), F32),
            pltpu.VMEM(*sums),
            pltpu.VMEM(*sums),
            pltpu.VMEM(*shapes[0]),
            pltpu.VMEM(*shapes[1]),
            pltpu.SemaphoreType.DMA((1,)),
            pltpu.SemaphoreType.DMA((five, 4)),
        ],
        compiler_params=pltpu.CompilerParams(vmem_limit_bytes=24 * MIB),
        cost_estimate=pl.CostEstimate(
            flops=2 * five * 12 * 512 * 256 * 128, bytes_accessed=12 * MIB, transcendentals=five * 1024 * 256
        ),
        name="attend",
    )(*scalars, adapters, near, oth, below, above, fixed(up))


def hold_kernel(down_in, up_in, down_out, up_out):
    pass


def hold(ret_down, ret_up):
    return pl.pallas_call(
        hold_kernel,
        in_specs=[hbm()] * 2,
        out_specs=[hbm()] * 2,
        out_shape=[pltpu.HBM(x.shape, x.dtype) for x in (ret_down, ret_up)],
        input_output_aliases={0: 0, 1: 1},
        compiler_params=pltpu.CompilerParams(vmem_limit_bytes=MIB),
        cost_estimate=pl.CostEstimate(flops=MIB, bytes_accessed=MIB, transcendentals=0),
        name="hold",
    )(fixed(ret_down), fixed(ret_up))


def join_kernel(
    clips, place, lengths, robots, sum_a_hbm, sum_b_hbm, above, below, mine, theirs, sum_a, sum_b, sems
):
    loads = [
        pltpu.make_async_copy(x.at[n], y.at[n], sems.at[2 * m + n])
        for m, (x, y) in enumerate(((sum_a_hbm, sum_a), (sum_b_hbm, sum_b)))
        for n in range(2)
    ]
    for load in loads:
        load.start()
    first = place[0] == 0
    frame_a = 2 * place[1]
    start_n, _ = clip_of(frame_a + 2, lengths, robots, clips)
    wide = start_n == frame_a
    quarter = above.shape[2]
    for n in range(2):
        loads[n].wait()
        loads[2 + n].wait()
        for group in range(2):
            second = above[2 + n].astype(F32)
            if group == 0:
                a = sum_a[n, 0] + jnp.where(wide, second, 0.0)
                b = sum_b[n, 0] + above[n].astype(F32)
            else:
                a = sum_a[n, 1] + below[n].astype(F32)
                b = sum_b[n, 1] + jnp.where(wide, 0.0, second)
            cols = slice(group * quarter, (group + 1) * quarter)
            mine[n, :, cols] = jnp.where(first, a, b).astype(BF16)
            theirs[n, :, cols] = jnp.where(first, b, a).astype(BF16)


def join(scalars, sum_a, sum_b, above, below):
    shape = (2, TOK, 2 * above.shape[2])
    return pl.pallas_call(
        functools.partial(join_kernel, scalars[1].shape[0]),
        in_specs=[smem()] * 3 + [hbm()] * 2 + [vmem()] * 2,
        out_specs=[vmem()] * 2,
        out_shape=[pltpu.VMEM(shape, BF16), pltpu.VMEM(shape, BF16)],
        scratch_shapes=[
            pltpu.VMEM(sum_a.shape, F32), pltpu.VMEM(sum_b.shape, F32), pltpu.SemaphoreType.DMA((4,))
        ],
        compiler_params=pltpu.CompilerParams(vmem_limit_bytes=8 * MIB),
        cost_estimate=pl.CostEstimate(flops=MIB, bytes_accessed=6 * MIB, transcendentals=0),
        name="join",
    )(*scalars, fixed(sum_a), fixed(sum_b), above, below)


def place_kernel(place, mine, other, key_grad, value_grad, sems):
    half = mine.shape[2]
    copies = []
    for n, out in enumerate((key_grad, value_grad)):
        for side, source in ((place[0], mine), (1 - place[0], other)):
            cols = pl.ds(pl.multiple_of(side * half, HEAD), half)
            copies.append(pltpu.make_async_copy(source.at[n], out.at[:, cols], sems.at[len(copies)]))
    for copy in copies:
        copy.start()
    for copy in copies:
        copy.wait()


def place_halves(place, mine, other):
    shape = (TOK, 2 * mine.shape[2])
    return pl.pallas_call(
        place_kernel,
        in_specs=[smem()] + [vmem()] * 2,
        out_specs=[hbm()] * 2,
        out_shape=[pltpu.HBM(shape, BF16), pltpu.HBM(shape, BF16)],
        scratch_shapes=[pltpu.SemaphoreType.DMA((4,))],
        compiler_params=pltpu.CompilerParams(vmem_limit_bytes=4 * MIB),
        cost_estimate=pl.CostEstimate(flops=0, bytes_accessed=4 * MIB, transcendentals=0),
        name="place_halves",
    )(place, mine, other)


def first_sum_kernel(pieces, out):
    total = functools.reduce(jnp.add, [pieces[n].astype(F32) for n in range(pieces.shape[0])]).astype(BF16)
    for n in range(out.shape[0]):
        out[n] = total


def first_sum(pieces, peers):
    return pl.pallas_call(
        first_sum_kernel,
        in_specs=[vmem()],
        out_specs=vmem(),
        out_shape=pltpu.VMEM((peers,) + pieces.shape[1:], BF16),
        compiler_params=pltpu.CompilerParams(vmem_limit_bytes=2 * MIB),
        name="first_sum",
    )(pieces)


def second_sum_kernel(up_rows, where, pieces, out):
    everything = functools.reduce(jnp.add, [pieces[n].astype(F32) for n in range(pieces.shape[0])])
    is_up = lax.broadcasted_iota(jnp.int32, everything.shape, 0) % ROWS < up_rows
    message = jnp.where(is_up, everything, pieces[where[0]].astype(F32)).astype(BF16)
    for n in range(out.shape[0]):
        out[n] = message


def second_sum(where, pieces, peers, up_rows):
    return pl.pallas_call(
        functools.partial(second_sum_kernel, up_rows),
        in_specs=[smem(), vmem()],
        out_specs=vmem(),
        out_shape=pltpu.VMEM((peers,) + pieces.shape[1:], BF16),
        compiler_params=pltpu.CompilerParams(vmem_limit_bytes=2 * MIB),
        name="second_sum",
    )(where, pieces)


def finish_kernel(heads, place, gathered, swapped, up_grad, adapter_grad, one, two):
    per_core = heads // 2
    one[...] = gathered[...].astype(F32)
    two[...] = swapped[...].astype(F32)
    for n, part in enumerate((one, two)):
        side = place[0] if n == 0 else 1 - place[0]
        for h in range(per_core):
            cols = pl.ds(pl.multiple_of((side * per_core + h) * HEAD, HEAD), HEAD)
            up_grad[:, cols] = part[:, h, :]
    for s in range(4):
        adapter_grad[s] = one[:, per_core + s, :] + two[:, per_core + s, :]


def finish(place, gathered, swapped, heads):
    return pl.pallas_call(
        functools.partial(finish_kernel, heads),
        in_specs=[smem(), vmem(), vmem()],
        out_specs=[vmem(), vmem()],
        out_shape=[
            jax.ShapeDtypeStruct((RANK, heads * HEAD), F32),
            jax.ShapeDtypeStruct((4, RANK, HEAD), F32),
        ],
        scratch_shapes=[pltpu.VMEM((RANK, ROWS, HEAD), F32), pltpu.VMEM((RANK, ROWS, HEAD), F32)],
        compiler_params=pltpu.CompilerParams(vmem_limit_bytes=6 * MIB),
        name="finish",
    )(place, gathered, swapped)


def local(
    query_tokens, key_tokens, value_tokens, out_grad, actions, clip_lengths, clip_robots, adapters, up_proj,
):
    q, k, v, g = (t[0, 0] for t in (query_tokens, key_tokens, value_tokens, out_grad))
    act = actions[0, 0]
    heads = q.shape[1] // HEAD
    core = lax.axis_index("core")
    nz, ny = lax.axis_size("z"), lax.axis_size("y")
    chips = lax.axis_size("x") * nz
    chip = lax.axis_index("x") * nz + lax.axis_index("z")
    chain = ("x", "z")
    swap = [(0, 1), (1, 0)]
    upward = [(c, c + 1) for c in range(chips - 1)]
    downward = [(c + 1, c) for c in range(chips - 1)]
    place = jnp.stack([core, chip]).astype(jnp.int32)
    scalars = (place, clip_lengths[0, 0], clip_robots[0, 0])
    own = (q, g, k, v)
    oth = lax.ppermute(take_half(place, own, act, True), "core", swap)
    near = take_half(place, own, act, False)
    up_msg, down_msg = pack(scalars, near, oth)
    below = lax.ppermute(up_msg, chain, upward)
    above = lax.ppermute(down_msg, chain, downward)
    table = jnp.swapaxes(adapters[0], 1, 2)
    payload, sum_a, sum_b, ret_down, ret_up = attend(scalars, table, near, oth, below, above, up_proj)
    ret_down, ret_up = hold(ret_down, ret_up)

    plane = ("dp", "x", "z")
    peers = lax.axis_size(plane)
    share = (peers, RANK // peers * ROWS, HEAD)
    pieces = lax.all_to_all(payload.reshape(share), plane, 0, 0, tiled=True)
    pieces = lax.all_to_all(first_sum(pieces, ny), "y", 0, 0, tiled=True)
    row = lax.axis_index("y").astype(jnp.int32).reshape(1)
    message = second_sum(row, pieces, peers, heads // 2)
    gathered = lax.all_to_all(message, plane, 0, 0, tiled=True).reshape(RANK, ROWS, HEAD)
    swapped = lax.ppermute(gathered, "core", swap)
    from_above = lax.ppermute(ret_down, chain, downward)
    from_below = lax.ppermute(ret_up, chain, upward)
    up_total, adapter_total = finish(place, gathered, swapped, heads)
    adapter_total = jnp.swapaxes(adapter_total, 1, 2)
    mine, theirs = join(scalars, sum_a, sum_b, from_above, from_below)
    key_grad, value_grad = place_halves(place, mine, lax.ppermute(theirs, "core", swap))
    return key_grad[None, None], value_grad[None, None], adapter_total[None], up_total


def solution(mesh):
    sizes = dict(mesh.shape)
    wide = Mesh(
        mesh.devices.reshape(sizes["dp"], 2, sizes["context"] // 4, 2, sizes["embodime"]),
        ("dp", "x", "z", "core", "y"),
    )
    frames = P("dp", "y", ("x", "z", "core"), None)
    rows = P("dp", "y", None)
    return jax.shard_map(
        local,
        mesh=wide,
        in_specs=(frames,) * 5 + (rows, rows, P("y", None, None, None), P()),
        out_specs=(frames, frames, P("y", None, None, None), P()),
        check_vma=False,
    )
```

```python
import functools
import math

import jax
import jax.numpy as jnp
from jax import lax
from jax.experimental import pallas as pl
from jax.experimental.pallas import tpu as pltpu
from jax.sharding import Mesh, PartitionSpec as P

HEAD = 128
TOK = 128
RANK = 64
LOW = -1e30
SCALE = HEAD**-0.5
SCALE2 = SCALE * math.log2(math.e)
F32 = jnp.float32
BF16 = jnp.bfloat16
ROWS = 16
MIB = 1024 * 1024


def dot(a, b, ca, cb):
    return lax.dot_general(a, b, (((ca,), (cb,)), ((), ())), preferred_element_type=F32)


def clip_of(frame, lengths, robots, clips):
    begin = jnp.int32(0)
    start = jnp.int32(0)
    robot = jnp.int32(0)
    for i in range(clips):
        size = lengths[i]
        inside = jnp.logical_and(frame >= begin, frame < begin + size)
        start = jnp.where(inside, begin, start)
        robot = jnp.where(inside, robots[i], robot)
        begin = begin + size
    return start, robot


def smem():
    return pl.BlockSpec(memory_space=pltpu.SMEM)


def vmem():
    return pl.BlockSpec(memory_space=pltpu.VMEM)


def hbm():
    return pl.BlockSpec(memory_space=pl.ANY)


def fixed(x):
    return pltpu.with_memory_space_constraint(x, pltpu.HBM)


def take_kernel(far, place, q, g, k, v, act, out, sems):
    half = q.shape[1] // 2
    side = 1 - place[0] if far else place[0]
    copies = [
        pltpu.make_async_copy(
            x.at[:, pl.ds(pl.multiple_of(side * half, HEAD), half)], out.at[:, pl.ds(n * half, half)], sems.at[n]
        )
        for n, x in enumerate((q, g, k, v))
    ]
    copies.append(pltpu.make_async_copy(act, out.at[:, pl.ds(4 * half, HEAD)], sems.at[4]))
    for copy in copies:
        copy.start()
    for copy in copies:
        copy.wait()


def take_half(place, own, act, far):
    half = own[0].shape[1] // 2
    return pl.pallas_call(
        functools.partial(take_kernel, far),
        in_specs=[smem()] + [hbm()] * 5,
        out_specs=vmem(),
        out_shape=pltpu.VMEM((TOK, 4 * half + HEAD), BF16),
        scratch_shapes=[pltpu.SemaphoreType.DMA((5,))],
        compiler_params=pltpu.CompilerParams(vmem_limit_bytes=8 * MIB),
        cost_estimate=pl.CostEstimate(flops=0, bytes_accessed=4 * MIB, transcendentals=0),
        name="take_far" if far else "take_near",
    )(place, *(fixed(x) for x in own), fixed(act))


def pack_kernel(clips, place, lengths, robots, near, oth, up, down):
    half = near.shape[1] // 4 // HEAD * HEAD
    quarter = half // 2
    first = place[0] == 0
    frame_a = 2 * place[1]
    start_n, _ = clip_of(frame_a + 2, lengths, robots, clips)
    wide = start_n == frame_a

    def frame(is_a, array, group):
        at = array * half + group * quarter
        one, two = near[:, at:at + quarter], oth[:, at:at + quarter]
        return jnp.where(first, one, two) if is_a else jnp.where(first, two, one)

    for n, array in enumerate((2, 3)):
        up[:, n * quarter:(n + 1) * quarter] = frame(False, array, 0)
        up[:, (2 + n) * quarter:(3 + n) * quarter] = jnp.where(wide, frame(True, array, 0), frame(False, array, 1))
    for n in range(4):
        down[:, n * quarter:(n + 1) * quarter] = frame(True, n, 1)
    one, two = near[:, 4 * half:], oth[:, 4 * half:]
    down[:, 4 * quarter:] = jnp.where(first, one, two)


def pack(scalars, near, oth):
    quarter = near.shape[1] // 4 // HEAD * HEAD // 2
    return pl.pallas_call(
        functools.partial(pack_kernel, scalars[1].shape[0]),
        in_specs=[smem()] * 3 + [vmem()] * 2,
        out_specs=[vmem()] * 2,
        out_shape=[pltpu.VMEM((TOK, 4 * quarter), BF16), pltpu.VMEM((TOK, 4 * quarter + HEAD), BF16)],
        compiler_params=pltpu.CompilerParams(vmem_limit_bytes=8 * MIB),
        cost_estimate=pl.CostEstimate(flops=0, bytes_accessed=4 * MIB, transcendentals=0),
        name="pack",
    )(*scalars, near, oth)


class Views:
    def __init__(self, place, near, oth, below, above):
        self.first = place[0] == 0
        self.near, self.oth, self.below, self.above = near, oth, below, above
        self.half = near.shape[1] // 4 // HEAD * HEAD
        self.quarter = self.half // 2

    def pick(self, one, two):
        return jnp.where(self.first, one, two)

    def pair(self, one, two):
        return [self.pick(one, two), self.pick(two, one)]

    def both(self, n, group, j):
        at = n * self.half + group * self.quarter + j * HEAD
        return self.pair(self.near[:, at:at + HEAD], self.oth[:, at:at + HEAD])

    def lower(self, n, j):
        at = n * self.quarter + j * HEAD
        return self.below[:, at:at + HEAD]

    def upper(self, n, j):
        at = n * self.quarter + j * HEAD
        return self.above[:, at:at + HEAD]

    def actions(self):
        return self.pair(self.near[:, 4 * self.half:], self.oth[:, 4 * self.half:]) + [self.above[:, 4 * self.quarter:]]


def block(x, i, j):
    return x[i * TOK:(i + 1) * TOK, j * TOK:(j + 1) * TOK]


def column(blocks):
    return jnp.concatenate(blocks, 0)


def soften(raw, prods, biases, keep=None):
    tops = [jnp.max(r, 0, keepdims=True) + b for r, b in zip(raw, biases)]
    top = functools.reduce(jnp.maximum, tops)
    weights = [jnp.exp2(r * SCALE2 + (b - top) * SCALE2) for r, b in zip(raw, biases)]
    total = jnp.sum(functools.reduce(jnp.add, weights), 0, keepdims=True)
    mixed = [w * p for w, p in zip(weights, prods)]
    moment = jnp.sum(functools.reduce(jnp.add, mixed), 0, keepdims=True)
    inverse = 1.0 / total
    if keep is not None:
        inverse = inverse * keep
    delta = moment * inverse
    scaled = inverse * SCALE
    prob = [(w * inverse).astype(BF16) for w in weights]
    dscore = [((w * scaled) * (p - delta)).astype(BF16) for w, p in zip(weights, prods)]
    return prob, dscore


class Masks:
    def __init__(self, clips, place, lengths, robots):
        frame_a = 2 * place[1]
        start_a, robot_a = clip_of(frame_a, lengths, robots, clips)
        start_b, robot_b = clip_of(frame_a + 1, lengths, robots, clips)
        start_n, robot_n = clip_of(frame_a + 2, lengths, robots, clips)
        self.wide_below = start_a == frame_a - 2
        self.wide_above = start_n == frame_a
        self.robots = (robot_a, robot_b, robot_n)

        def bias(valid):
            return jnp.where(valid, jnp.float32(0), jnp.float32(LOW))

        zero = jnp.float32(0)
        self.a = (bias(self.wide_below), bias(start_a <= frame_a - 1), zero)
        self.b = (bias(start_b <= frame_a - 1), bias(start_b <= frame_a), zero)
        self.n = (zero, zero, zero)
        self.scale_a = jnp.where(self.wide_below, 0.0, 1.0).astype(F32)
        self.scale_n = jnp.where(self.wide_above, 1.0, 0.0).astype(F32)


def shift_of(act, robot, adapters, adapted, adapted_t, n):
    table = adapters[robot]
    adapted[n * TOK:(n + 1) * TOK, :] = dot(act, table, 1, 1).astype(BF16)
    adapted_t[:, n * TOK:(n + 1) * TOK] = dot(table, act, 1, 1).astype(BF16)


def own_kernel(
    clips, place, lengths, robots, adapters, near, oth, up_hbm,
    adapted, adapted_t, queries, raws, prods, up, sem,
):
    view = Views(place, near, oth, None, None)
    half, quarter = view.half, view.quarter
    load = pltpu.make_async_copy(
        up_hbm.at[:, pl.ds(pl.multiple_of(place[0] * half, HEAD), half)], up, sem.at[0]
    )
    load.start()
    masks = Masks(clips, place, lengths, robots)
    acts = view.pair(near[:, 4 * half:], oth[:, 4 * half:])
    for n in range(2):
        shift_of(acts[n], masks.robots[n], adapters, adapted, adapted_t, n)
    load.wait()
    for j in range(quarter // HEAD):
        for group in range(2):
            at = group * quarter + j * HEAD
            shift = dot(adapted[...], up[:, at:at + HEAD], 1, 0)
            query = (column(view.both(0, group, j)).astype(F32) + shift).astype(BF16)
            queries[j, group] = query
            grad = column(view.both(1, group, j))
            for out, pair, rows in ((raws, view.both(2, group, j), query), (prods, view.both(3, group, j), grad)):
                out[j, group, :, : 2 * TOK] = dot(pair[0], rows, 1, 1)
                out[j, group, :, 2 * TOK:] = dot(pair[1], rows[TOK:], 1, 1)


def own_scores(scalars, adapters, near, oth, up):
    half = up.shape[1] // 2
    five = half // 2 // HEAD
    return pl.pallas_call(
        functools.partial(own_kernel, scalars[1].shape[0]),
        in_specs=[smem()] * 3 + [vmem()] * 3 + [hbm()],
        out_specs=[vmem()] * 5,
        out_shape=[
            pltpu.VMEM((2 * TOK, RANK), BF16), pltpu.VMEM((RANK, 2 * TOK), BF16),
            pltpu.VMEM((five, 2, 2 * TOK, HEAD), BF16),
            pltpu.VMEM((five, 2, TOK, 3 * TOK), F32), pltpu.VMEM((five, 2, TOK, 3 * TOK), F32),
        ],
        scratch_shapes=[pltpu.VMEM((RANK, half), BF16), pltpu.SemaphoreType.DMA((1,))],
        compiler_params=pltpu.CompilerParams(vmem_limit_bytes=12 * MIB),
        cost_estimate=pl.CostEstimate(
            flops=2 * five * 6 * 512 * 256 * 128, bytes_accessed=4 * MIB, transcendentals=0
        ),
        name="own_scores",
    )(*scalars, adapters, near, oth, fixed(up))


def narrow_head(view, masks, queries, raws, prods, j):
    none = jnp.zeros((TOK, TOK), BF16)
    query = queries[j, 0]
    grad = column(view.both(1, 0, j))
    keys = column([view.lower(2, j), view.lower(0, j)] + view.both(2, 0, j))

    def blocks(p0, p1, rows, own):
        far = dot(p1, rows, 1, 1)
        near = own[j, 0]
        row_a = [dot(p0, rows[:TOK], 1, 1), far[:, :TOK], near[:, :TOK]]
        return row_a, [far[:, TOK:], near[:, TOK:2 * TOK], near[:, 2 * TOK:]]

    raw_a, raw_b = blocks(view.lower(2, j), view.lower(0, j), query, raws)
    prod_a, prod_b = blocks(view.lower(3, j), view.lower(1, j), grad, prods)
    prob_a, dscore_a = soften(raw_a, prod_a, masks.a)
    prob_b, dscore_b = soften(raw_b, prod_b, masks.b)
    prob = jnp.concatenate([column(prob_a + [none]), column([none] + prob_b)], 1)
    dscore = jnp.concatenate([column(dscore_a + [none]), column([none] + dscore_b)], 1)
    return query, grad, keys, prob, dscore


def wide_head(view, masks, queries, raws, prods, adapted_n, up_h, j):
    none = jnp.zeros((TOK, TOK), BF16)
    query = queries[j, 1]
    query_n = (view.upper(0, j).astype(F32) + dot(adapted_n, up_h, 1, 0)).astype(BF16)
    grad = column(view.both(1, 1, j))
    grad_n = view.upper(1, j)
    keys = column([view.lower(2, j)] + view.both(2, 1, j) + [view.upper(2, j)])
    values = column(view.both(3, 1, j) + [view.upper(3, j)])

    def blocks(p1, rows, own):
        far = dot(p1, rows, 1, 1)
        near = own[j, 1]
        return [far[:, :TOK], near[:, :TOK]], [far[:, TOK:], near[:, TOK:2 * TOK], near[:, 2 * TOK:]]

    raw_a, raw_b = blocks(view.lower(2, j), query, raws)
    prod_a, prod_b = blocks(view.lower(3, j), grad, prods)
    raw_n = dot(keys[TOK:], query_n, 1, 1)
    prod_n = dot(values, grad_n, 1, 1)
    prob_a, dscore_a = soften(raw_a, prod_a, masks.a[1:], masks.scale_a)
    prob_b, dscore_b = soften(raw_b, prod_b, masks.b)
    prob_n, dscore_n = soften(
        [block(raw_n, i, 0) for i in range(3)], [block(prod_n, i, 0) for i in range(3)], masks.n, masks.scale_n
    )
    prob = jnp.concatenate([column(prob_a + [none, none]), column(prob_b + [none]), column([none] + prob_n)], 1)
    dscore = jnp.concatenate([column(dscore_a + [none, none]), column(dscore_b + [none]), column([none] + dscore_n)], 1)
    return column([query, query_n]), column([grad, grad_n]), keys, prob, dscore


def attend_kernel(
    clips, place, lengths, robots, adapters, near, oth, below, above, adapted_own, adapted_own_t, queries, raws, prods,
    up_hbm, payload, sum_a, sum_b, ret_down, ret_up,
    up, adapted, adapted_t, agrad_t, pay, keep_a, keep_b, keep_down, keep_up, sem_in, sem_out,
):
    view = Views(place, near, oth, below, above)
    half, quarter = view.half, view.quarter
    five = quarter // HEAD
    load = pltpu.make_async_copy(
        up_hbm.at[:, pl.ds(pl.multiple_of(place[0] * half, HEAD), half)], up, sem_in.at[0]
    )
    load.start()
    masks = Masks(clips, place, lengths, robots)
    acts = view.actions()
    adapted_t[:, : 2 * TOK] = adapted_own_t[...]
    shift_of(acts[2], masks.robots[2], adapters, adapted, adapted_t, 2)
    agrad_t[...] = jnp.zeros_like(agrad_t)
    pay[:, 2 * five:, :] = jnp.zeros((RANK, ROWS - 2 * five, HEAD), F32)
    load.wait()

    def sums(keys, dscore, up_h, rows, head):
        query_grad = dot(keys, dscore, 0, 0)
        high = query_grad.astype(BF16)
        low = (query_grad - high.astype(F32)).astype(BF16)
        agrad_t[:, :rows] += dot(up_h, high, 1, 0) + dot(up_h, low, 1, 0)
        term = dot(adapted_t[:, :rows], high, 1, 1) + dot(adapted_t[:, :rows], low, 1, 1)
        pay[:, head, :] = term

    stores = []
    for j in range(five):
        cols = slice(j * HEAD, (j + 1) * HEAD)
        up_h = up[:, cols]
        query, grad, keys, prob, dscore = narrow_head(view, masks, queries, raws, prods, j)
        sums(keys, dscore, up_h, 2 * TOK, j)
        wide_parts = []
        for n, part in enumerate((dot(dscore, query, 1, 0), dot(prob, grad, 1, 0))):
            wide_parts.append(part[:TOK])
            keep_down[n, :, cols] = part[TOK:2 * TOK].astype(BF16)
            keep_a[n, 0, :, cols] = part[2 * TOK:3 * TOK]
            keep_b[n, 0, :, cols] = part[3 * TOK:]
        up_h = up[:, quarter + j * HEAD:quarter + (j + 1) * HEAD]
        query, grad, keys, prob, dscore = wide_head(view, masks, queries, raws, prods, adapted[2 * TOK:, :], up_h, j)
        sums(keys, dscore, up_h, 3 * TOK, five + j)
        for n, part in enumerate((dot(dscore, query, 1, 0), dot(prob, grad, 1, 0))):
            keep_down[2 + n, :, cols] = jnp.where(masks.wide_below, wide_parts[n], part[:TOK]).astype(BF16)
            keep_a[n, 1, :, cols] = part[TOK:2 * TOK]
            keep_b[n, 1, :, cols] = part[2 * TOK:3 * TOK]
            keep_up[n, :, cols] = part[3 * TOK:].astype(BF16)
        span = pl.ds(j * HEAD, HEAD)
        for n, (x, y) in enumerate(((keep_down, ret_down), (keep_up, ret_up), (keep_a, sum_a), (keep_b, sum_b))):
            at = (slice(None),) * (len(x.shape) - 1) + (span,)
            stores.append(pltpu.make_async_copy(x.at[at], y.at[at], sem_out.at[j, n]))
            stores[-1].start()

    terms = []
    for n, act in enumerate(acts):
        whole = agrad_t[:, n * TOK:(n + 1) * TOK]
        high = whole.astype(BF16)
        low = (whole - high.astype(F32)).astype(BF16)
        terms.append(dot(high, act, 1, 0) + dot(low, act, 1, 0))
    blank = jnp.zeros((RANK, HEAD), F32)
    for s in range(4):
        pay[:, 2 * five + s, :] = functools.reduce(
            jnp.add, [jnp.where(robot == s, term, blank) for robot, term in zip(masks.robots, terms)]
        )
    payload[...] = pay[...].astype(BF16)
    for store in stores:
        store.wait()


def attend(scalars, adapters, near, oth, below, above, stored, up):
    half = up.shape[1] // 2
    quarter = half // 2
    five = quarter // HEAD
    shapes = [((4, TOK, quarter), BF16), ((2, TOK, quarter), BF16)]
    sums = ((2, 2, TOK, quarter), F32)
    return pl.pallas_call(
        functools.partial(attend_kernel, scalars[1].shape[0]),
        in_specs=[smem()] * 3 + [vmem()] * 10 + [hbm()],
        out_specs=[vmem()] + [hbm()] * 4,
        out_shape=[jax.ShapeDtypeStruct((RANK, ROWS, HEAD), BF16)] + [pltpu.HBM(*x) for x in (sums, sums, *shapes)],
        scratch_shapes=[
            pltpu.VMEM((RANK, half), BF16),
            pltpu.VMEM((3 * TOK, RANK), BF16),
            pltpu.VMEM((RANK, 3 * TOK), BF16),
            pltpu.VMEM((RANK, 3 * TOK), F32),
            pltpu.VMEM((RANK, ROWS, HEAD), F32),
            pltpu.VMEM(*sums),
            pltpu.VMEM(*sums),
            pltpu.VMEM(*shapes[0]),
            pltpu.VMEM(*shapes[1]),
            pltpu.SemaphoreType.DMA((1,)),
            pltpu.SemaphoreType.DMA((five, 4)),
        ],
        compiler_params=pltpu.CompilerParams(vmem_limit_bytes=24 * MIB),
        cost_estimate=pl.CostEstimate(
            flops=2 * five * 12 * 512 * 256 * 128, bytes_accessed=12 * MIB, transcendentals=five * 1024 * 256
        ),
        name="attend",
    )(*scalars, adapters, near, oth, below, above, *stored, fixed(up))


def hold_kernel(down_in, up_in, down_out, up_out):
    pass


def hold(ret_down, ret_up):
    return pl.pallas_call(
        hold_kernel,
        in_specs=[hbm()] * 2,
        out_specs=[hbm()] * 2,
        out_shape=[pltpu.HBM(x.shape, x.dtype) for x in (ret_down, ret_up)],
        input_output_aliases={0: 0, 1: 1},
        compiler_params=pltpu.CompilerParams(vmem_limit_bytes=MIB),
        cost_estimate=pl.CostEstimate(flops=MIB, bytes_accessed=MIB, transcendentals=0),
        name="hold",
    )(fixed(ret_down), fixed(ret_up))


def join_kernel(
    clips, place, lengths, robots, sum_a_hbm, sum_b_hbm, above, below, mine, theirs, sum_a, sum_b, sems
):
    loads = [
        pltpu.make_async_copy(x.at[n], y.at[n], sems.at[2 * m + n])
        for m, (x, y) in enumerate(((sum_a_hbm, sum_a), (sum_b_hbm, sum_b)))
        for n in range(2)
    ]
    for load in loads:
        load.start()
    first = place[0] == 0
    frame_a = 2 * place[1]
    start_n, _ = clip_of(frame_a + 2, lengths, robots, clips)
    wide = start_n == frame_a
    quarter = above.shape[2]
    for n in range(2):
        loads[n].wait()
        loads[2 + n].wait()
        for group in range(2):
            second = above[2 + n].astype(F32)
            if group == 0:
                a = sum_a[n, 0] + jnp.where(wide, second, 0.0)
                b = sum_b[n, 0] + above[n].astype(F32)
            else:
                a = sum_a[n, 1] + below[n].astype(F32)
                b = sum_b[n, 1] + jnp.where(wide, 0.0, second)
            cols = slice(group * quarter, (group + 1) * quarter)
            mine[n, :, cols] = jnp.where(first, a, b).astype(BF16)
            theirs[n, :, cols] = jnp.where(first, b, a).astype(BF16)


def join(scalars, sum_a, sum_b, above, below):
    shape = (2, TOK, 2 * above.shape[2])
    return pl.pallas_call(
        functools.partial(join_kernel, scalars[1].shape[0]),
        in_specs=[smem()] * 3 + [hbm()] * 2 + [vmem()] * 2,
        out_specs=[vmem()] * 2,
        out_shape=[pltpu.VMEM(shape, BF16), pltpu.VMEM(shape, BF16)],
        scratch_shapes=[
            pltpu.VMEM(sum_a.shape, F32), pltpu.VMEM(sum_b.shape, F32), pltpu.SemaphoreType.DMA((4,))
        ],
        compiler_params=pltpu.CompilerParams(vmem_limit_bytes=8 * MIB),
        cost_estimate=pl.CostEstimate(flops=MIB, bytes_accessed=6 * MIB, transcendentals=0),
        name="join",
    )(*scalars, fixed(sum_a), fixed(sum_b), above, below)


def place_kernel(place, mine, other, key_grad, value_grad, sems):
    half = mine.shape[2]
    copies = []
    for n, out in enumerate((key_grad, value_grad)):
        for side, source in ((place[0], mine), (1 - place[0], other)):
            cols = pl.ds(pl.multiple_of(side * half, HEAD), half)
            copies.append(pltpu.make_async_copy(source.at[n], out.at[:, cols], sems.at[len(copies)]))
    for copy in copies:
        copy.start()
    for copy in copies:
        copy.wait()


def place_halves(place, mine, other):
    shape = (TOK, 2 * mine.shape[2])
    return pl.pallas_call(
        place_kernel,
        in_specs=[smem()] + [vmem()] * 2,
        out_specs=[hbm()] * 2,
        out_shape=[pltpu.HBM(shape, BF16), pltpu.HBM(shape, BF16)],
        scratch_shapes=[pltpu.SemaphoreType.DMA((4,))],
        compiler_params=pltpu.CompilerParams(vmem_limit_bytes=4 * MIB),
        cost_estimate=pl.CostEstimate(flops=0, bytes_accessed=4 * MIB, transcendentals=0),
        name="place_halves",
    )(place, mine, other)


def first_sum_kernel(pieces, out):
    total = functools.reduce(jnp.add, [pieces[n].astype(F32) for n in range(pieces.shape[0])]).astype(BF16)
    for n in range(out.shape[0]):
        out[n] = total


def first_sum(pieces, peers):
    return pl.pallas_call(
        first_sum_kernel,
        in_specs=[vmem()],
        out_specs=vmem(),
        out_shape=pltpu.VMEM((peers,) + pieces.shape[1:], BF16),
        compiler_params=pltpu.CompilerParams(vmem_limit_bytes=2 * MIB),
        name="first_sum",
    )(pieces)


def second_sum_kernel(up_rows, where, pieces, out):
    everything = functools.reduce(jnp.add, [pieces[n].astype(F32) for n in range(pieces.shape[0])])
    is_up = lax.broadcasted_iota(jnp.int32, everything.shape, 0) % ROWS < up_rows
    message = jnp.where(is_up, everything, pieces[where[0]].astype(F32)).astype(BF16)
    for n in range(out.shape[0]):
        out[n] = message


def second_sum(where, pieces, peers, up_rows):
    return pl.pallas_call(
        functools.partial(second_sum_kernel, up_rows),
        in_specs=[smem(), vmem()],
        out_specs=vmem(),
        out_shape=pltpu.VMEM((peers,) + pieces.shape[1:], BF16),
        compiler_params=pltpu.CompilerParams(vmem_limit_bytes=2 * MIB),
        name="second_sum",
    )(where, pieces)


def finish_kernel(heads, place, gathered, swapped, up_grad, adapter_grad, one, two):
    per_core = heads // 2
    one[...] = gathered[...].astype(F32)
    two[...] = swapped[...].astype(F32)
    for n, part in enumerate((one, two)):
        side = place[0] if n == 0 else 1 - place[0]
        for h in range(per_core):
            cols = pl.ds(pl.multiple_of((side * per_core + h) * HEAD, HEAD), HEAD)
            up_grad[:, cols] = part[:, h, :]
    for s in range(4):
        adapter_grad[s] = one[:, per_core + s, :] + two[:, per_core + s, :]


def finish(place, gathered, swapped, heads):
    return pl.pallas_call(
        functools.partial(finish_kernel, heads),
        in_specs=[smem(), vmem(), vmem()],
        out_specs=[vmem(), vmem()],
        out_shape=[
            jax.ShapeDtypeStruct((RANK, heads * HEAD), F32),
            jax.ShapeDtypeStruct((4, RANK, HEAD), F32),
        ],
        scratch_shapes=[pltpu.VMEM((RANK, ROWS, HEAD), F32), pltpu.VMEM((RANK, ROWS, HEAD), F32)],
        compiler_params=pltpu.CompilerParams(vmem_limit_bytes=6 * MIB),
        name="finish",
    )(place, gathered, swapped)


def local(
    query_tokens, key_tokens, value_tokens, out_grad, actions, clip_lengths, clip_robots, adapters, up_proj,
):
    q, k, v, g = (t[0, 0] for t in (query_tokens, key_tokens, value_tokens, out_grad))
    act = actions[0, 0]
    heads = q.shape[1] // HEAD
    core = lax.axis_index("core")
    nz, ny = lax.axis_size("z"), lax.axis_size("y")
    chips = lax.axis_size("x") * nz
    chip = lax.axis_index("x") * nz + lax.axis_index("z")
    chain = ("x", "z")
    swap = [(0, 1), (1, 0)]
    upward = [(c, c + 1) for c in range(chips - 1)]
    downward = [(c + 1, c) for c in range(chips - 1)]
    place = jnp.stack([core, chip]).astype(jnp.int32)
    scalars = (place, clip_lengths[0, 0], clip_robots[0, 0])
    own = (q, g, k, v)
    oth = lax.ppermute(take_half(place, own, act, True), "core", swap)
    near = take_half(place, own, act, False)
    up_msg, down_msg = pack(scalars, near, oth)
    below = lax.ppermute(up_msg, chain, upward)
    above = lax.ppermute(down_msg, chain, downward)
    table = jnp.swapaxes(adapters[0], 1, 2)
    stored = own_scores(scalars, table, near, oth, up_proj)
    payload, sum_a, sum_b, ret_down, ret_up = attend(
        scalars, table, near, oth, below, above, stored, up_proj
    )
    ret_down, ret_up = hold(ret_down, ret_up)

    plane = ("dp", "x", "z")
    peers = lax.axis_size(plane)
    share = (peers, RANK // peers * ROWS, HEAD)
    pieces = lax.all_to_all(payload.reshape(share), plane, 0, 0, tiled=True)
    pieces = lax.all_to_all(first_sum(pieces, ny), "y", 0, 0, tiled=True)
    row = lax.axis_index("y").astype(jnp.int32).reshape(1)
    message = second_sum(row, pieces, peers, heads // 2)
    gathered = lax.all_to_all(message, plane, 0, 0, tiled=True).reshape(RANK, ROWS, HEAD)
    swapped = lax.ppermute(gathered, "core", swap)
    from_above = lax.ppermute(ret_down, chain, downward)
    from_below = lax.ppermute(ret_up, chain, upward)
    up_total, adapter_total = finish(place, gathered, swapped, heads)
    adapter_total = jnp.swapaxes(adapter_total, 1, 2)
    mine, theirs = join(scalars, sum_a, sum_b, from_above, from_below)
    key_grad, value_grad = place_halves(place, mine, lax.ppermute(theirs, "core", swap))
    return key_grad[None, None], value_grad[None, None], adapter_total[None], up_total


def solution(mesh):
    sizes = dict(mesh.shape)
    wide = Mesh(
        mesh.devices.reshape(sizes["dp"], 2, sizes["context"] // 4, 2, sizes["embodime"]),
        ("dp", "x", "z", "core", "y"),
    )
    frames = P("dp", "y", ("x", "z", "core"), None)
    rows = P("dp", "y", None)
    return jax.shard_map(
        local,
        mesh=wide,
        in_specs=(frames,) * 5 + (rows, rows, P("y", None, None, None), P()),
        out_specs=(frames, frames, P("y", None, None, None), P()),
        check_vma=False,
    )
```

```python
import functools
import math

import jax
import jax.numpy as jnp
from jax import lax
from jax.experimental import pallas as pl
from jax.experimental.pallas import tpu as pltpu
from jax.sharding import Mesh, PartitionSpec as P

HEAD = 128
TOK = 128
RANK = 64
LOW = -1e30
SCALE = HEAD**-0.5
SCALE2 = SCALE * math.log2(math.e)
F32 = jnp.float32
BF16 = jnp.bfloat16
ROWS = 16
MIB = 1024 * 1024


def dot(a, b, ca, cb):
    return lax.dot_general(a, b, (((ca,), (cb,)), ((), ())), preferred_element_type=F32)


def clip_of(frame, lengths, robots, clips):
    begin = jnp.int32(0)
    start = jnp.int32(0)
    robot = jnp.int32(0)
    for i in range(clips):
        size = lengths[i]
        inside = jnp.logical_and(frame >= begin, frame < begin + size)
        start = jnp.where(inside, begin, start)
        robot = jnp.where(inside, robots[i], robot)
        begin = begin + size
    return start, robot


def smem():
    return pl.BlockSpec(memory_space=pltpu.SMEM)


def vmem():
    return pl.BlockSpec(memory_space=pltpu.VMEM)


def hbm():
    return pl.BlockSpec(memory_space=pl.ANY)


def fixed(x):
    return pltpu.with_memory_space_constraint(x, pltpu.HBM)


def take_kernel(far, place, q, g, k, v, act, out, sems):
    half = q.shape[1] // 2
    side = 1 - place[0] if far else place[0]
    copies = [
        pltpu.make_async_copy(
            x.at[:, pl.ds(pl.multiple_of(side * half, HEAD), half)], out.at[:, pl.ds(n * half, half)], sems.at[n]
        )
        for n, x in enumerate((q, g, k, v))
    ]
    copies.append(pltpu.make_async_copy(act, out.at[:, pl.ds(4 * half, HEAD)], sems.at[4]))
    for copy in copies:
        copy.start()
    for copy in copies:
        copy.wait()


def take_half(place, own, act, far):
    half = own[0].shape[1] // 2
    return pl.pallas_call(
        functools.partial(take_kernel, far),
        in_specs=[smem()] + [hbm()] * 5,
        out_specs=vmem(),
        out_shape=pltpu.VMEM((TOK, 4 * half + HEAD), BF16),
        scratch_shapes=[pltpu.SemaphoreType.DMA((5,))],
        compiler_params=pltpu.CompilerParams(vmem_limit_bytes=8 * MIB),
        cost_estimate=pl.CostEstimate(flops=0, bytes_accessed=4 * MIB, transcendentals=0),
        name="take_far" if far else "take_near",
    )(place, *(fixed(x) for x in own), fixed(act))


def pack_kernel(clips, place, lengths, robots, near, oth, up, down):
    half = near.shape[1] // 4 // HEAD * HEAD
    quarter = half // 2
    first = place[0] == 0
    frame_a = 2 * place[1]
    start_n, _ = clip_of(frame_a + 2, lengths, robots, clips)
    wide = start_n == frame_a

    def frame(is_a, array, group):
        at = array * half + group * quarter
        one, two = near[:, at:at + quarter], oth[:, at:at + quarter]
        return jnp.where(first, one, two) if is_a else jnp.where(first, two, one)

    for n, array in enumerate((2, 3)):
        up[:, n * quarter:(n + 1) * quarter] = frame(False, array, 0)
        up[:, (2 + n) * quarter:(3 + n) * quarter] = jnp.where(wide, frame(True, array, 0), frame(False, array, 1))
    for n in range(4):
        down[:, n * quarter:(n + 1) * quarter] = frame(True, n, 1)
    one, two = near[:, 4 * half:], oth[:, 4 * half:]
    down[:, 4 * quarter:] = jnp.where(first, one, two)


def pack(scalars, near, oth):
    quarter = near.shape[1] // 4 // HEAD * HEAD // 2
    return pl.pallas_call(
        functools.partial(pack_kernel, scalars[1].shape[0]),
        in_specs=[smem()] * 3 + [vmem()] * 2,
        out_specs=[vmem()] * 2,
        out_shape=[pltpu.VMEM((TOK, 4 * quarter), BF16), pltpu.VMEM((TOK, 4 * quarter + HEAD), BF16)],
        compiler_params=pltpu.CompilerParams(vmem_limit_bytes=8 * MIB),
        cost_estimate=pl.CostEstimate(flops=0, bytes_accessed=4 * MIB, transcendentals=0),
        name="pack",
    )(*scalars, near, oth)


class Views:
    def __init__(self, place, near, oth, below, above):
        self.first = place[0] == 0
        self.near, self.oth, self.below, self.above = near, oth, below, above
        self.half = near.shape[1] // 4 // HEAD * HEAD
        self.quarter = self.half // 2

    def pick(self, one, two):
        return jnp.where(self.first, one, two)

    def pair(self, one, two):
        return [self.pick(one, two), self.pick(two, one)]

    def both(self, n, group, j):
        at = n * self.half + group * self.quarter + j * HEAD
        return self.pair(self.near[:, at:at + HEAD], self.oth[:, at:at + HEAD])

    def lower(self, n, j):
        at = n * self.quarter + j * HEAD
        return self.below[:, at:at + HEAD]

    def upper(self, n, j):
        at = n * self.quarter + j * HEAD
        return self.above[:, at:at + HEAD]

    def actions(self):
        return self.pair(self.near[:, 4 * self.half:], self.oth[:, 4 * self.half:]) + [self.above[:, 4 * self.quarter:]]


def block(x, i, j):
    return x[i * TOK:(i + 1) * TOK, j * TOK:(j + 1) * TOK]


def column(blocks):
    return jnp.concatenate(blocks, 0)


def soften(raw, prods, biases, own=None, keep=None):
    tops = [jnp.max(r, 0, keepdims=True) + b for r, b in zip(raw, biases)]
    if own is not None:
        own_weights, own_prods, (own_top, own_total, own_moment) = own
        tops.append(own_top)
    top = functools.reduce(jnp.maximum, tops)
    weights = [jnp.exp2(r * SCALE2 + (b - top) * SCALE2) for r, b in zip(raw, biases)]
    total = jnp.sum(functools.reduce(jnp.add, weights), 0, keepdims=True)
    mixed = [w * p for w, p in zip(weights, prods)]
    moment = jnp.sum(functools.reduce(jnp.add, mixed), 0, keepdims=True)
    factors = [None] * len(weights)
    if own is not None:
        factor = jnp.exp2((own_top - top) * SCALE2)
        total = total + own_total * factor
        moment = moment + own_moment * factor
        weights = weights + own_weights
        prods = prods + own_prods
        factors += [factor] * len(own_weights)
    inverse = 1.0 / total
    if keep is not None:
        inverse = inverse * keep
    delta = moment * inverse
    prob, dscore = [], []
    for w, p, factor in zip(weights, prods, factors):
        share = inverse if factor is None else inverse * factor
        prob.append((w * share).astype(BF16))
        dscore.append(((w * (share * SCALE)) * (p - delta)).astype(BF16))
    return prob, dscore


def weigh(raw, prods, biases):
    tops = [jnp.max(r, 0, keepdims=True) + b for r, b in zip(raw, biases)]
    top = functools.reduce(jnp.maximum, tops)
    weights = [jnp.exp2(r * SCALE2 + (b - top) * SCALE2) for r, b in zip(raw, biases)]
    total = jnp.sum(functools.reduce(jnp.add, weights), 0, keepdims=True)
    moment = jnp.sum(functools.reduce(jnp.add, [w * p for w, p in zip(weights, prods)]), 0, keepdims=True)
    return weights, (top, total, moment)


def own_row(weights, prods, stats, row):
    cuts = ((0,), (1, 2))[row]
    return (
        [weights[:, i * TOK:(i + 1) * TOK] for i in cuts],
        [prods[:, i * TOK:(i + 1) * TOK] for i in cuts],
        tuple(stats[3 * row + i:3 * row + i + 1] for i in range(3)),
    )


class Masks:
    def __init__(self, clips, place, lengths, robots):
        frame_a = 2 * place[1]
        start_a, robot_a = clip_of(frame_a, lengths, robots, clips)
        start_b, robot_b = clip_of(frame_a + 1, lengths, robots, clips)
        start_n, robot_n = clip_of(frame_a + 2, lengths, robots, clips)
        self.wide_below = start_a == frame_a - 2
        self.wide_above = start_n == frame_a
        self.robots = (robot_a, robot_b, robot_n)

        def bias(valid):
            return jnp.where(valid, jnp.float32(0), jnp.float32(LOW))

        zero = jnp.float32(0)
        self.a = (bias(self.wide_below), bias(start_a <= frame_a - 1), zero)
        self.b = (bias(start_b <= frame_a - 1), bias(start_b <= frame_a), zero)
        self.n = (zero, zero, zero)
        self.scale_a = jnp.where(self.wide_below, 0.0, 1.0).astype(F32)
        self.scale_n = jnp.where(self.wide_above, 1.0, 0.0).astype(F32)


def shift_of(act, robot, adapters, adapted, adapted_t, n):
    table = adapters[robot]
    adapted[n * TOK:(n + 1) * TOK, :] = dot(act, table, 1, 1).astype(BF16)
    adapted_t[:, n * TOK:(n + 1) * TOK] = dot(table, act, 1, 1).astype(BF16)


def own_kernel(
    clips, place, lengths, robots, adapters, near, oth, up_hbm,
    adapted, adapted_t, queries, weights, prods, stats, up, sem,
):
    view = Views(place, near, oth, None, None)
    half, quarter = view.half, view.quarter
    load = pltpu.make_async_copy(
        up_hbm.at[:, pl.ds(pl.multiple_of(place[0] * half, HEAD), half)], up, sem.at[0]
    )
    load.start()
    masks = Masks(clips, place, lengths, robots)
    acts = view.pair(near[:, 4 * half:], oth[:, 4 * half:])
    for n in range(2):
        shift_of(acts[n], masks.robots[n], adapters, adapted, adapted_t, n)
    load.wait()
    for j in range(quarter // HEAD):
        for group in range(2):
            at = group * quarter + j * HEAD
            shift = dot(adapted[...], up[:, at:at + HEAD], 1, 0)
            query = (column(view.both(0, group, j)).astype(F32) + shift).astype(BF16)
            queries[j, group] = query
            grad = column(view.both(1, group, j))
            raw, prod = [], []
            for out, pair, rows in ((raw, view.both(2, group, j), query), (prod, view.both(3, group, j), grad)):
                first = dot(pair[0], rows, 1, 1)
                out += [first[:, :TOK], first[:, TOK:], dot(pair[1], rows[TOK:], 1, 1)]
            row_a, stats_a = weigh(raw[:1], prod[:1], masks.a[2:])
            row_b, stats_b = weigh(raw[1:], prod[1:], masks.b[1:])
            for i, (w, p) in enumerate(zip(row_a + row_b, prod)):
                weights[j, group, :, i * TOK:(i + 1) * TOK] = w
                prods[j, group, :, i * TOK:(i + 1) * TOK] = p
            for i, stat in enumerate(stats_a + stats_b):
                stats[j, group, i:i + 1, :] = stat


def own_scores(scalars, adapters, near, oth, up):
    half = up.shape[1] // 2
    five = half // 2 // HEAD
    return pl.pallas_call(
        functools.partial(own_kernel, scalars[1].shape[0]),
        in_specs=[smem()] * 3 + [vmem()] * 3 + [hbm()],
        out_specs=[vmem()] * 6,
        out_shape=[
            pltpu.VMEM((2 * TOK, RANK), BF16), pltpu.VMEM((RANK, 2 * TOK), BF16),
            pltpu.VMEM((five, 2, 2 * TOK, HEAD), BF16),
            pltpu.VMEM((five, 2, TOK, 3 * TOK), F32), pltpu.VMEM((five, 2, TOK, 3 * TOK), F32),
            pltpu.VMEM((five, 2, 8, TOK), F32),
        ],
        scratch_shapes=[pltpu.VMEM((RANK, half), BF16), pltpu.SemaphoreType.DMA((1,))],
        compiler_params=pltpu.CompilerParams(vmem_limit_bytes=12 * MIB),
        cost_estimate=pl.CostEstimate(
            flops=2 * five * 6 * 512 * 256 * 128, bytes_accessed=4 * MIB, transcendentals=0
        ),
        name="own_scores",
    )(*scalars, adapters, near, oth, fixed(up))


def narrow_head(view, masks, queries, weights, prods, stats, j):
    none = jnp.zeros((TOK, TOK), BF16)
    query = queries[j, 0]
    grad = column(view.both(1, 0, j))
    keys = column([view.lower(2, j), view.lower(0, j)] + view.both(2, 0, j))

    def blocks(p0, p1, rows):
        far = dot(p1, rows, 1, 1)
        return [dot(p0, rows[:TOK], 1, 1), far[:, :TOK]], [far[:, TOK:]]

    raw_a, raw_b = blocks(view.lower(2, j), view.lower(0, j), query)
    prod_a, prod_b = blocks(view.lower(3, j), view.lower(1, j), grad)
    own = [own_row(weights[j, 0], prods[j, 0], stats[j, 0], row) for row in range(2)]
    prob_a, dscore_a = soften(raw_a, prod_a, masks.a[:2], own[0])
    prob_b, dscore_b = soften(raw_b, prod_b, masks.b[:1], own[1])
    prob = jnp.concatenate([column(prob_a + [none]), column([none] + prob_b)], 1)
    dscore = jnp.concatenate([column(dscore_a + [none]), column([none] + dscore_b)], 1)
    return query, grad, keys, prob, dscore


def wide_head(view, masks, queries, weights, prods, stats, adapted_n, up_h, j):
    none = jnp.zeros((TOK, TOK), BF16)
    query = queries[j, 1]
    query_n = (view.upper(0, j).astype(F32) + dot(adapted_n, up_h, 1, 0)).astype(BF16)
    grad = column(view.both(1, 1, j))
    grad_n = view.upper(1, j)
    keys = column([view.lower(2, j)] + view.both(2, 1, j) + [view.upper(2, j)])
    values = column(view.both(3, 1, j) + [view.upper(3, j)])
    raw = dot(view.lower(2, j), query, 1, 1)
    prod = dot(view.lower(3, j), grad, 1, 1)
    raw_n = dot(keys[TOK:], query_n, 1, 1)
    prod_n = dot(values, grad_n, 1, 1)
    own = [own_row(weights[j, 1], prods[j, 1], stats[j, 1], row) for row in range(2)]
    prob_a, dscore_a = soften([raw[:, :TOK]], [prod[:, :TOK]], masks.a[1:2], own[0], masks.scale_a)
    prob_b, dscore_b = soften([raw[:, TOK:]], [prod[:, TOK:]], masks.b[:1], own[1])
    prob_n, dscore_n = soften(
        [block(raw_n, i, 0) for i in range(3)], [block(prod_n, i, 0) for i in range(3)], masks.n, None, masks.scale_n
    )
    prob = jnp.concatenate([column(prob_a + [none, none]), column(prob_b + [none]), column([none] + prob_n)], 1)
    dscore = jnp.concatenate([column(dscore_a + [none, none]), column(dscore_b + [none]), column([none] + dscore_n)], 1)
    return column([query, query_n]), column([grad, grad_n]), keys, prob, dscore


def attend_kernel(
    clips, place, lengths, robots, adapters, near, oth, below, above, adapted_own, adapted_own_t, queries, weights, prods,
    stats, up_hbm, payload, sum_a, sum_b, ret_down, ret_up,
    up, adapted, adapted_t, agrad_t, pay, keep_a, keep_b, keep_down, keep_up, sem_in, sem_out,
):
    view = Views(place, near, oth, below, above)
    half, quarter = view.half, view.quarter
    five = quarter // HEAD
    load = pltpu.make_async_copy(
        up_hbm.at[:, pl.ds(pl.multiple_of(place[0] * half, HEAD), half)], up, sem_in.at[0]
    )
    load.start()
    masks = Masks(clips, place, lengths, robots)
    acts = view.actions()
    adapted_t[:, : 2 * TOK] = adapted_own_t[...]
    shift_of(acts[2], masks.robots[2], adapters, adapted, adapted_t, 2)
    agrad_t[...] = jnp.zeros_like(agrad_t)
    pay[:, 2 * five:, :] = jnp.zeros((RANK, ROWS - 2 * five, HEAD), F32)
    load.wait()

    def sums(keys, dscore, up_h, rows, head):
        query_grad = dot(keys, dscore, 0, 0)
        high = query_grad.astype(BF16)
        low = (query_grad - high.astype(F32)).astype(BF16)
        agrad_t[:, :rows] += dot(up_h, high, 1, 0) + dot(up_h, low, 1, 0)
        term = dot(adapted_t[:, :rows], high, 1, 1) + dot(adapted_t[:, :rows], low, 1, 1)
        pay[:, head, :] = term

    stores = []

    def ahead(h):
        j, group = h // 2, h % 2
        up_h = up[:, group * quarter + j * HEAD:group * quarter + (j + 1) * HEAD]
        if group == 0:
            return up_h, narrow_head(view, masks, queries, weights, prods, stats, j)
        return up_h, wide_head(view, masks, queries, weights, prods, stats, adapted[2 * TOK:, :], up_h, j)

    def behind(h, made, wide_parts):
        j, group = h // 2, h % 2
        cols = slice(j * HEAD, (j + 1) * HEAD)
        up_h, (query, grad, keys, prob, dscore) = made
        sums(keys, dscore, up_h, (2 + group) * TOK, group * five + j)
        parts = (dot(dscore, query, 1, 0), dot(prob, grad, 1, 0))
        for n, part in enumerate(parts):
            if group == 0:
                keep_down[n, :, cols] = part[TOK:2 * TOK].astype(BF16)
                keep_a[n, 0, :, cols] = part[2 * TOK:3 * TOK]
                keep_b[n, 0, :, cols] = part[3 * TOK:]
            else:
                keep_down[2 + n, :, cols] = jnp.where(masks.wide_below, wide_parts[n], part[:TOK]).astype(BF16)
                keep_a[n, 1, :, cols] = part[TOK:2 * TOK]
                keep_b[n, 1, :, cols] = part[2 * TOK:3 * TOK]
                keep_up[n, :, cols] = part[3 * TOK:].astype(BF16)
        if group == 0:
            return [part[:TOK] for part in parts]
        span = pl.ds(j * HEAD, HEAD)
        for n, (x, y) in enumerate(((keep_down, ret_down), (keep_up, ret_up), (keep_a, sum_a), (keep_b, sum_b))):
            at = (slice(None),) * (len(x.shape) - 1) + (span,)
            stores.append(pltpu.make_async_copy(x.at[at], y.at[at], sem_out.at[j, n]))
            stores[-1].start()
        return None

    made, kept = ahead(0), None
    for h in range(2 * five):
        following = ahead(h + 1) if h + 1 < 2 * five else None
        kept = behind(h, made, kept)
        made = following

    terms = []
    for n, act in enumerate(acts):
        whole = agrad_t[:, n * TOK:(n + 1) * TOK]
        high = whole.astype(BF16)
        low = (whole - high.astype(F32)).astype(BF16)
        terms.append(dot(high, act, 1, 0) + dot(low, act, 1, 0))
    blank = jnp.zeros((RANK, HEAD), F32)
    for s in range(4):
        pay[:, 2 * five + s, :] = functools.reduce(
            jnp.add, [jnp.where(robot == s, term, blank) for robot, term in zip(masks.robots, terms)]
        )
    payload[...] = pay[...].astype(BF16)
    for store in stores:
        store.wait()


def attend(scalars, adapters, near, oth, below, above, stored, up):
    half = up.shape[1] // 2
    quarter = half // 2
    five = quarter // HEAD
    shapes = [((4, TOK, quarter), BF16), ((2, TOK, quarter), BF16)]
    sums = ((2, 2, TOK, quarter), F32)
    return pl.pallas_call(
        functools.partial(attend_kernel, scalars[1].shape[0]),
        in_specs=[smem()] * 3 + [vmem()] * 11 + [hbm()],
        out_specs=[vmem()] + [hbm()] * 4,
        out_shape=[jax.ShapeDtypeStruct((RANK, ROWS, HEAD), BF16)] + [pltpu.HBM(*x) for x in (sums, sums, *shapes)],
        scratch_shapes=[
            pltpu.VMEM((RANK, half), BF16),
            pltpu.VMEM((3 * TOK, RANK), BF16),
            pltpu.VMEM((RANK, 3 * TOK), BF16),
            pltpu.VMEM((RANK, 3 * TOK), F32),
            pltpu.VMEM((RANK, ROWS, HEAD), F32),
            pltpu.VMEM(*sums),
            pltpu.VMEM(*sums),
            pltpu.VMEM(*shapes[0]),
            pltpu.VMEM(*shapes[1]),
            pltpu.SemaphoreType.DMA((1,)),
            pltpu.SemaphoreType.DMA((five, 4)),
        ],
        compiler_params=pltpu.CompilerParams(vmem_limit_bytes=24 * MIB),
        cost_estimate=pl.CostEstimate(
            flops=2 * five * 12 * 512 * 256 * 128, bytes_accessed=12 * MIB, transcendentals=five * 1024 * 256
        ),
        name="attend",
    )(*scalars, adapters, near, oth, below, above, *stored, fixed(up))


def hold_kernel(held_in, after, held_out):
    pass


def hold(held, after):
    return pl.pallas_call(
        hold_kernel,
        in_specs=[hbm()] * 2,
        out_specs=hbm(),
        out_shape=pltpu.HBM(held.shape, held.dtype),
        input_output_aliases={0: 0},
        compiler_params=pltpu.CompilerParams(vmem_limit_bytes=MIB),
        cost_estimate=pl.CostEstimate(flops=MIB, bytes_accessed=MIB, transcendentals=0),
        name="hold",
    )(fixed(held), after)


def join_kernel(
    clips, place, lengths, robots, sum_a_hbm, sum_b_hbm, above, below, mine, theirs, sum_a, sum_b, sems
):
    loads = [
        pltpu.make_async_copy(x.at[n], y.at[n], sems.at[2 * m + n])
        for m, (x, y) in enumerate(((sum_a_hbm, sum_a), (sum_b_hbm, sum_b)))
        for n in range(2)
    ]
    for load in loads:
        load.start()
    first = place[0] == 0
    frame_a = 2 * place[1]
    start_n, _ = clip_of(frame_a + 2, lengths, robots, clips)
    wide = start_n == frame_a
    quarter = above.shape[2]
    for n in range(2):
        loads[n].wait()
        loads[2 + n].wait()
        for group in range(2):
            second = above[2 + n].astype(F32)
            if group == 0:
                a = sum_a[n, 0] + jnp.where(wide, second, 0.0)
                b = sum_b[n, 0] + above[n].astype(F32)
            else:
                a = sum_a[n, 1] + below[n].astype(F32)
                b = sum_b[n, 1] + jnp.where(wide, 0.0, second)
            cols = slice(group * quarter, (group + 1) * quarter)
            mine[n, :, cols] = jnp.where(first, a, b).astype(BF16)
            theirs[n, :, cols] = jnp.where(first, b, a).astype(BF16)


def join(scalars, sum_a, sum_b, above, below):
    shape = (2, TOK, 2 * above.shape[2])
    return pl.pallas_call(
        functools.partial(join_kernel, scalars[1].shape[0]),
        in_specs=[smem()] * 3 + [hbm()] * 2 + [vmem()] * 2,
        out_specs=[vmem()] * 2,
        out_shape=[pltpu.VMEM(shape, BF16), pltpu.VMEM(shape, BF16)],
        scratch_shapes=[
            pltpu.VMEM(sum_a.shape, F32), pltpu.VMEM(sum_b.shape, F32), pltpu.SemaphoreType.DMA((4,))
        ],
        compiler_params=pltpu.CompilerParams(vmem_limit_bytes=8 * MIB),
        cost_estimate=pl.CostEstimate(flops=MIB, bytes_accessed=6 * MIB, transcendentals=0),
        name="join",
    )(*scalars, fixed(sum_a), fixed(sum_b), above, below)


def place_kernel(place, mine, other, key_grad, value_grad, sems):
    half = mine.shape[2]
    copies = []
    for n, out in enumerate((key_grad, value_grad)):
        for side, source in ((place[0], mine), (1 - place[0], other)):
            cols = pl.ds(pl.multiple_of(side * half, HEAD), half)
            copies.append(pltpu.make_async_copy(source.at[n], out.at[:, cols], sems.at[len(copies)]))
    for copy in copies:
        copy.start()
    for copy in copies:
        copy.wait()


def place_halves(place, mine, other):
    shape = (TOK, 2 * mine.shape[2])
    return pl.pallas_call(
        place_kernel,
        in_specs=[smem()] + [vmem()] * 2,
        out_specs=[hbm()] * 2,
        out_shape=[pltpu.HBM(shape, BF16), pltpu.HBM(shape, BF16)],
        scratch_shapes=[pltpu.SemaphoreType.DMA((4,))],
        compiler_params=pltpu.CompilerParams(vmem_limit_bytes=4 * MIB),
        cost_estimate=pl.CostEstimate(flops=0, bytes_accessed=4 * MIB, transcendentals=0),
        name="place_halves",
    )(place, mine, other)


def first_sum_kernel(pieces, out):
    total = functools.reduce(jnp.add, [pieces[n].astype(F32) for n in range(pieces.shape[0])]).astype(BF16)
    for n in range(out.shape[0]):
        out[n] = total


def first_sum(pieces, peers):
    return pl.pallas_call(
        first_sum_kernel,
        in_specs=[vmem()],
        out_specs=vmem(),
        out_shape=pltpu.VMEM((peers,) + pieces.shape[1:], BF16),
        compiler_params=pltpu.CompilerParams(vmem_limit_bytes=2 * MIB),
        name="first_sum",
    )(pieces)


def second_sum_kernel(up_rows, where, pieces, out):
    everything = functools.reduce(jnp.add, [pieces[n].astype(F32) for n in range(pieces.shape[0])])
    is_up = lax.broadcasted_iota(jnp.int32, everything.shape, 0) % ROWS < up_rows
    message = jnp.where(is_up, everything, pieces[where[0]].astype(F32)).astype(BF16)
    for n in range(out.shape[0]):
        out[n] = message


def second_sum(where, pieces, peers, up_rows):
    return pl.pallas_call(
        functools.partial(second_sum_kernel, up_rows),
        in_specs=[smem(), vmem()],
        out_specs=vmem(),
        out_shape=pltpu.VMEM((peers,) + pieces.shape[1:], BF16),
        compiler_params=pltpu.CompilerParams(vmem_limit_bytes=2 * MIB),
        name="second_sum",
    )(where, pieces)


def finish_kernel(heads, place, gathered, swapped, up_grad, adapter_grad, one, two):
    per_core = heads // 2
    one[...] = gathered[...].astype(F32)
    two[...] = swapped[...].astype(F32)
    for n, part in enumerate((one, two)):
        side = place[0] if n == 0 else 1 - place[0]
        for h in range(per_core):
            cols = pl.ds(pl.multiple_of((side * per_core + h) * HEAD, HEAD), HEAD)
            up_grad[:, cols] = part[:, h, :]
    for s in range(4):
        adapter_grad[s] = one[:, per_core + s, :] + two[:, per_core + s, :]


def finish(place, gathered, swapped, heads):
    return pl.pallas_call(
        functools.partial(finish_kernel, heads),
        in_specs=[smem(), vmem(), vmem()],
        out_specs=[vmem(), vmem()],
        out_shape=[
            jax.ShapeDtypeStruct((RANK, heads * HEAD), F32),
            jax.ShapeDtypeStruct((4, RANK, HEAD), F32),
        ],
        scratch_shapes=[pltpu.VMEM((RANK, ROWS, HEAD), F32), pltpu.VMEM((RANK, ROWS, HEAD), F32)],
        compiler_params=pltpu.CompilerParams(vmem_limit_bytes=6 * MIB),
        name="finish",
    )(place, gathered, swapped)


def local(
    query_tokens, key_tokens, value_tokens, out_grad, actions, clip_lengths, clip_robots, adapters, up_proj,
):
    q, k, v, g = (t[0, 0] for t in (query_tokens, key_tokens, value_tokens, out_grad))
    act = actions[0, 0]
    heads = q.shape[1] // HEAD
    core = lax.axis_index("core")
    nz, ny = lax.axis_size("z"), lax.axis_size("y")
    chips = lax.axis_size("x") * nz
    chip = lax.axis_index("x") * nz + lax.axis_index("z")
    chain = ("x", "z")
    swap = [(0, 1), (1, 0)]
    upward = [(c, c + 1) for c in range(chips - 1)]
    downward = [(c + 1, c) for c in range(chips - 1)]
    place = jnp.stack([core, chip]).astype(jnp.int32)
    scalars = (place, clip_lengths[0, 0], clip_robots[0, 0])
    own = (q, g, k, v)
    oth = lax.ppermute(take_half(place, own, act, True), "core", swap)
    near = take_half(place, own, act, False)
    up_msg, down_msg = pack(scalars, near, oth)
    below = lax.ppermute(up_msg, chain, upward)
    above = lax.ppermute(down_msg, chain, downward)
    table = jnp.swapaxes(adapters[0], 1, 2)
    stored = own_scores(scalars, table, near, oth, up_proj)
    payload, sum_a, sum_b, ret_down, ret_up = attend(
        scalars, table, near, oth, below, above, stored, up_proj
    )
    ret_down, ret_up = hold(ret_down, payload), hold(ret_up, payload)

    plane = ("dp", "x", "z")
    peers = lax.axis_size(plane)
    share = (peers, RANK // peers * ROWS, HEAD)
    pieces = lax.all_to_all(payload.reshape(share), plane, 0, 0, tiled=True)
    message = first_sum(pieces, ny)
    pieces = lax.all_to_all(message, "y", 0, 0, tiled=True)
    row = lax.axis_index("y").astype(jnp.int32).reshape(1)
    message = second_sum(row, pieces, peers, heads // 2)
    gathered = lax.all_to_all(message, plane, 0, 0, tiled=True).reshape(RANK, ROWS, HEAD)
    swapped = lax.ppermute(gathered, "core", swap)
    from_above = lax.ppermute(ret_down, chain, downward)
    from_below = lax.ppermute(ret_up, chain, upward)
    up_total, adapter_total = finish(place, gathered, swapped, heads)
    adapter_total = jnp.swapaxes(adapter_total, 1, 2)
    mine, theirs = join(scalars, sum_a, sum_b, from_above, from_below)
    key_grad, value_grad = place_halves(place, mine, lax.ppermute(theirs, "core", swap))
    return key_grad[None, None], value_grad[None, None], adapter_total[None], up_total


def solution(mesh):
    sizes = dict(mesh.shape)
    wide = Mesh(
        mesh.devices.reshape(sizes["dp"], 2, sizes["context"] // 4, 2, sizes["embodime"]),
        ("dp", "x", "z", "core", "y"),
    )
    frames = P("dp", "y", ("x", "z", "core"), None)
    rows = P("dp", "y", None)
    return jax.shard_map(
        local,
        mesh=wide,
        in_specs=(frames,) * 5 + (rows, rows, P("y", None, None, None), P()),
        out_specs=(frames, frames, P("y", None, None, None), P()),
        check_vma=False,
    )
```

```python
import functools
import math

import jax
import jax.numpy as jnp
from jax import lax
from jax.experimental import pallas as pl
from jax.experimental.pallas import tpu as pltpu
from jax.sharding import Mesh, PartitionSpec as P

HEAD = 128
TOK = 128
RANK = 64
LOW = -1e30
SCALE = HEAD**-0.5
SCALE2 = SCALE * math.log2(math.e)
F32 = jnp.float32
BF16 = jnp.bfloat16
ROWS = 16
MIB = 1024 * 1024


def dot(a, b, ca, cb):
    return lax.dot_general(a, b, (((ca,), (cb,)), ((), ())), preferred_element_type=F32)


def clip_of(frame, lengths, robots, clips):
    begin = jnp.int32(0)
    start = jnp.int32(0)
    robot = jnp.int32(0)
    for i in range(clips):
        size = lengths[i]
        inside = jnp.logical_and(frame >= begin, frame < begin + size)
        start = jnp.where(inside, begin, start)
        robot = jnp.where(inside, robots[i], robot)
        begin = begin + size
    return start, robot


def smem():
    return pl.BlockSpec(memory_space=pltpu.SMEM)


def vmem():
    return pl.BlockSpec(memory_space=pltpu.VMEM)


def hbm():
    return pl.BlockSpec(memory_space=pl.ANY)


def fixed(x):
    return pltpu.with_memory_space_constraint(x, pltpu.HBM)


def take_kernel(far, place, q, g, k, v, act, out, sems):
    half = q.shape[1] // 2
    side = 1 - place[0] if far else place[0]
    copies = [
        pltpu.make_async_copy(
            x.at[:, pl.ds(pl.multiple_of(side * half, HEAD), half)], out.at[:, pl.ds(n * half, half)], sems.at[n]
        )
        for n, x in enumerate((q, g, k, v))
    ]
    copies.append(pltpu.make_async_copy(act, out.at[:, pl.ds(4 * half, HEAD)], sems.at[4]))
    for copy in copies:
        copy.start()
    for copy in copies:
        copy.wait()


def take_half(place, own, act, far):
    half = own[0].shape[1] // 2
    return pl.pallas_call(
        functools.partial(take_kernel, far),
        in_specs=[smem()] + [hbm()] * 5,
        out_specs=vmem(),
        out_shape=pltpu.VMEM((TOK, 4 * half + HEAD), BF16),
        scratch_shapes=[pltpu.SemaphoreType.DMA((5,))],
        compiler_params=pltpu.CompilerParams(vmem_limit_bytes=8 * MIB),
        cost_estimate=pl.CostEstimate(flops=0, bytes_accessed=4 * MIB, transcendentals=0),
        name="take_far" if far else "take_near",
    )(place, *(fixed(x) for x in own), fixed(act))


def pack_kernel(clips, place, lengths, robots, near, oth, up, down):
    half = near.shape[1] // 4 // HEAD * HEAD
    quarter = half // 2
    first = place[0] == 0
    frame_a = 2 * place[1]
    start_n, _ = clip_of(frame_a + 2, lengths, robots, clips)
    wide = start_n == frame_a

    def frame(is_a, array, group):
        at = array * half + group * quarter
        one, two = near[:, at:at + quarter], oth[:, at:at + quarter]
        return jnp.where(first, one, two) if is_a else jnp.where(first, two, one)

    for n, array in enumerate((2, 3)):
        up[:, n * quarter:(n + 1) * quarter] = frame(False, array, 0)
        up[:, (2 + n) * quarter:(3 + n) * quarter] = jnp.where(wide, frame(True, array, 0), frame(False, array, 1))
    for n in range(4):
        down[:, n * quarter:(n + 1) * quarter] = frame(True, n, 1)
    one, two = near[:, 4 * half:], oth[:, 4 * half:]
    down[:, 4 * quarter:] = jnp.where(first, one, two)


def pack(scalars, near, oth):
    quarter = near.shape[1] // 4 // HEAD * HEAD // 2
    return pl.pallas_call(
        functools.partial(pack_kernel, scalars[1].shape[0]),
        in_specs=[smem()] * 3 + [vmem()] * 2,
        out_specs=[vmem()] * 2,
        out_shape=[pltpu.VMEM((TOK, 4 * quarter), BF16), pltpu.VMEM((TOK, 4 * quarter + HEAD), BF16)],
        compiler_params=pltpu.CompilerParams(vmem_limit_bytes=8 * MIB),
        cost_estimate=pl.CostEstimate(flops=0, bytes_accessed=4 * MIB, transcendentals=0),
        name="pack",
    )(*scalars, near, oth)


class Views:
    def __init__(self, place, near, oth, below, above):
        self.first = place[0] == 0
        self.near, self.oth, self.below, self.above = near, oth, below, above
        self.half = near.shape[1] // 4 // HEAD * HEAD
        self.quarter = self.half // 2

    def pick(self, one, two):
        return jnp.where(self.first, one, two)

    def pair(self, one, two):
        return [self.pick(one, two), self.pick(two, one)]

    def both(self, n, group, j):
        at = n * self.half + group * self.quarter + j * HEAD
        return self.pair(self.near[:, at:at + HEAD], self.oth[:, at:at + HEAD])

    def lower(self, n, j):
        at = n * self.quarter + j * HEAD
        return self.below[:, at:at + HEAD]

    def upper(self, n, j):
        at = n * self.quarter + j * HEAD
        return self.above[:, at:at + HEAD]

    def actions(self):
        return self.pair(self.near[:, 4 * self.half:], self.oth[:, 4 * self.half:]) + [self.above[:, 4 * self.quarter:]]


def block(x, i, j):
    return x[i * TOK:(i + 1) * TOK, j * TOK:(j + 1) * TOK]


def column(blocks):
    return jnp.concatenate(blocks, 0)


def soften(raw, prods, biases, own=None, keep=None):
    tops = [jnp.max(r, 0, keepdims=True) + b for r, b in zip(raw, biases)]
    if own is not None:
        own_weights, own_prods, (own_top, own_total, own_moment) = own
        tops.append(own_top)
    top = functools.reduce(jnp.maximum, tops)
    weights = [jnp.exp2(r * SCALE2 + (b - top) * SCALE2) for r, b in zip(raw, biases)]
    total = jnp.sum(functools.reduce(jnp.add, weights), 0, keepdims=True)
    mixed = [w * p for w, p in zip(weights, prods)]
    moment = jnp.sum(functools.reduce(jnp.add, mixed), 0, keepdims=True)
    factors = [None] * len(weights)
    if own is not None:
        factor = jnp.exp2((own_top - top) * SCALE2)
        total = total + own_total * factor
        moment = moment + own_moment * factor
        weights = weights + own_weights
        prods = prods + own_prods
        factors += [factor] * len(own_weights)
    inverse = 1.0 / total
    if keep is not None:
        inverse = inverse * keep
    delta = moment * inverse
    prob, dscore = [], []
    for w, p, factor in zip(weights, prods, factors):
        share = inverse if factor is None else inverse * factor
        prob.append((w * share).astype(BF16))
        dscore.append(((w * (share * SCALE)) * (p - delta)).astype(BF16))
    return prob, dscore


def weigh(raw, prods, biases):
    tops = [jnp.max(r, 0, keepdims=True) + b for r, b in zip(raw, biases)]
    top = functools.reduce(jnp.maximum, tops)
    weights = [jnp.exp2(r * SCALE2 + (b - top) * SCALE2) for r, b in zip(raw, biases)]
    total = jnp.sum(functools.reduce(jnp.add, weights), 0, keepdims=True)
    moment = jnp.sum(functools.reduce(jnp.add, [w * p for w, p in zip(weights, prods)]), 0, keepdims=True)
    return weights, (top, total, moment)


def own_row(weights, prods, stats, row):
    cuts = ((0,), (1, 2))[row]
    return (
        [weights[:, i * TOK:(i + 1) * TOK] for i in cuts],
        [prods[:, i * TOK:(i + 1) * TOK] for i in cuts],
        tuple(stats[3 * row + i:3 * row + i + 1] for i in range(3)),
    )


class Masks:
    def __init__(self, clips, place, lengths, robots):
        frame_a = 2 * place[1]
        start_a, robot_a = clip_of(frame_a, lengths, robots, clips)
        start_b, robot_b = clip_of(frame_a + 1, lengths, robots, clips)
        start_n, robot_n = clip_of(frame_a + 2, lengths, robots, clips)
        self.wide_below = start_a == frame_a - 2
        self.wide_above = start_n == frame_a
        self.robots = (robot_a, robot_b, robot_n)

        def bias(valid):
            return jnp.where(valid, jnp.float32(0), jnp.float32(LOW))

        zero = jnp.float32(0)
        self.a = (bias(self.wide_below), bias(start_a <= frame_a - 1), zero)
        self.b = (bias(start_b <= frame_a - 1), bias(start_b <= frame_a), zero)
        self.n = (zero, zero, zero)
        self.scale_a = jnp.where(self.wide_below, 0.0, 1.0).astype(F32)
        self.scale_n = jnp.where(self.wide_above, 1.0, 0.0).astype(F32)


def shift_of(act, robot, adapters, adapted, adapted_t, n):
    table = adapters[robot]
    adapted[n * TOK:(n + 1) * TOK, :] = dot(act, table, 1, 1).astype(BF16)
    adapted_t[:, n * TOK:(n + 1) * TOK] = dot(table, act, 1, 1).astype(BF16)


def own_kernel(
    clips, place, lengths, robots, adapters, near, oth, up_hbm,
    adapted, adapted_t, queries, weights, prods, stats, up, sem,
):
    view = Views(place, near, oth, None, None)
    half, quarter = view.half, view.quarter
    load = pltpu.make_async_copy(
        up_hbm.at[:, pl.ds(pl.multiple_of(place[0] * half, HEAD), half)], up, sem.at[0]
    )
    load.start()
    masks = Masks(clips, place, lengths, robots)
    acts = view.pair(near[:, 4 * half:], oth[:, 4 * half:])
    for n in range(2):
        shift_of(acts[n], masks.robots[n], adapters, adapted, adapted_t, n)
    load.wait()
    for j in range(quarter // HEAD):
        for group in range(2):
            at = group * quarter + j * HEAD
            shift = dot(adapted[...], up[:, at:at + HEAD], 1, 0)
            query = (column(view.both(0, group, j)).astype(F32) + shift).astype(BF16)
            queries[j, group] = query
            grad = column(view.both(1, group, j))
            raw, prod = [], []
            for out, pair, rows in ((raw, view.both(2, group, j), query), (prod, view.both(3, group, j), grad)):
                first = dot(pair[0], rows, 1, 1)
                out += [first[:, :TOK], first[:, TOK:], dot(pair[1], rows[TOK:], 1, 1)]
            row_a, stats_a = weigh(raw[:1], prod[:1], masks.a[2:])
            row_b, stats_b = weigh(raw[1:], prod[1:], masks.b[1:])
            for i, (w, p) in enumerate(zip(row_a + row_b, prod)):
                weights[j, group, :, i * TOK:(i + 1) * TOK] = w
                prods[j, group, :, i * TOK:(i + 1) * TOK] = p
            for i, stat in enumerate(stats_a + stats_b):
                stats[j, group, i:i + 1, :] = stat


def own_scores(scalars, adapters, near, oth, up):
    half = up.shape[1] // 2
    five = half // 2 // HEAD
    return pl.pallas_call(
        functools.partial(own_kernel, scalars[1].shape[0]),
        in_specs=[smem()] * 3 + [vmem()] * 3 + [hbm()],
        out_specs=[vmem()] * 6,
        out_shape=[
            pltpu.VMEM((2 * TOK, RANK), BF16), pltpu.VMEM((RANK, 2 * TOK), BF16),
            pltpu.VMEM((five, 2, 2 * TOK, HEAD), BF16),
            pltpu.VMEM((five, 2, TOK, 3 * TOK), F32), pltpu.VMEM((five, 2, TOK, 3 * TOK), F32),
            pltpu.VMEM((five, 2, 8, TOK), F32),
        ],
        scratch_shapes=[pltpu.VMEM((RANK, half), BF16), pltpu.SemaphoreType.DMA((1,))],
        compiler_params=pltpu.CompilerParams(vmem_limit_bytes=12 * MIB),
        cost_estimate=pl.CostEstimate(
            flops=2 * five * 6 * 512 * 256 * 128, bytes_accessed=4 * MIB, transcendentals=0
        ),
        name="own_scores",
    )(*scalars, adapters, near, oth, fixed(up))


def narrow_head(view, masks, queries, weights, prods, stats, j):
    none = jnp.zeros((TOK, TOK), BF16)
    query = queries[j, 0]
    grad = column(view.both(1, 0, j))
    keys = column([view.lower(2, j), view.lower(0, j)] + view.both(2, 0, j))

    def blocks(p0, p1, rows):
        far = dot(p1, rows, 1, 1)
        return [dot(p0, rows[:TOK], 1, 1), far[:, :TOK]], [far[:, TOK:]]

    raw_a, raw_b = blocks(view.lower(2, j), view.lower(0, j), query)
    prod_a, prod_b = blocks(view.lower(3, j), view.lower(1, j), grad)

    def rest():
        own = [own_row(weights[j, 0], prods[j, 0], stats[j, 0], row) for row in range(2)]
        prob_a, dscore_a = soften(raw_a, prod_a, masks.a[:2], own[0])
        prob_b, dscore_b = soften(raw_b, prod_b, masks.b[:1], own[1])
        prob = jnp.concatenate([column(prob_a + [none]), column([none] + prob_b)], 1)
        dscore = jnp.concatenate([column(dscore_a + [none]), column([none] + dscore_b)], 1)
        return query, grad, keys, prob, dscore

    return rest


def wide_head(view, masks, queries, weights, prods, stats, adapted_n, up_h, j):
    none = jnp.zeros((TOK, TOK), BF16)
    query = queries[j, 1]
    query_n = (view.upper(0, j).astype(F32) + dot(adapted_n, up_h, 1, 0)).astype(BF16)
    grad = column(view.both(1, 1, j))
    grad_n = view.upper(1, j)
    keys = column([view.lower(2, j)] + view.both(2, 1, j) + [view.upper(2, j)])
    values = column(view.both(3, 1, j) + [view.upper(3, j)])
    raw = dot(view.lower(2, j), query, 1, 1)
    prod = dot(view.lower(3, j), grad, 1, 1)
    raw_n = dot(keys[TOK:], query_n, 1, 1)
    prod_n = dot(values, grad_n, 1, 1)

    def rest():
        own = [own_row(weights[j, 1], prods[j, 1], stats[j, 1], row) for row in range(2)]
        prob_a, dscore_a = soften([raw[:, :TOK]], [prod[:, :TOK]], masks.a[1:2], own[0], masks.scale_a)
        prob_b, dscore_b = soften([raw[:, TOK:]], [prod[:, TOK:]], masks.b[:1], own[1])
        prob_n, dscore_n = soften(
            [block(raw_n, i, 0) for i in range(3)], [block(prod_n, i, 0) for i in range(3)], masks.n, None, masks.scale_n
        )
        probs = [column(prob_a + [none, none]), column(prob_b + [none]), column([none] + prob_n)]
        dscores = [column(dscore_a + [none, none]), column(dscore_b + [none]), column([none] + dscore_n)]
        both_rows = column([query, query_n]), column([grad, grad_n])
        return *both_rows, keys, jnp.concatenate(probs, 1), jnp.concatenate(dscores, 1)

    return rest


def attend_kernel(
    clips, place, lengths, robots, adapters, near, oth, below, above, adapted_own, adapted_own_t, queries, weights, prods,
    stats, up_hbm, payload, sum_a, sum_b, ret_down, ret_up,
    up, adapted, adapted_t, agrad_t, pay, keep_a, keep_b, keep_down, keep_up, sem_in, sem_out,
):
    view = Views(place, near, oth, below, above)
    half, quarter = view.half, view.quarter
    five = quarter // HEAD
    load = pltpu.make_async_copy(
        up_hbm.at[:, pl.ds(pl.multiple_of(place[0] * half, HEAD), half)], up, sem_in.at[0]
    )
    load.start()
    masks = Masks(clips, place, lengths, robots)
    acts = view.actions()
    adapted_t[:, : 2 * TOK] = adapted_own_t[...]
    shift_of(acts[2], masks.robots[2], adapters, adapted, adapted_t, 2)
    agrad_t[...] = jnp.zeros_like(agrad_t)
    pay[:, 2 * five:, :] = jnp.zeros((RANK, ROWS - 2 * five, HEAD), F32)
    load.wait()

    def sums(keys, dscore, up_h, rows, head):
        query_grad = dot(keys, dscore, 0, 0).astype(BF16)
        agrad_t[:, :rows] += dot(up_h, query_grad, 1, 0)
        term = dot(adapted_t[:, :rows], query_grad, 1, 1)
        pay[:, head, :] = term

    stores = []

    def ahead(h):
        j, group = h // 2, h % 2
        up_h = up[:, group * quarter + j * HEAD:group * quarter + (j + 1) * HEAD]
        if group == 0:
            return up_h, narrow_head(view, masks, queries, weights, prods, stats, j)
        return up_h, wide_head(view, masks, queries, weights, prods, stats, adapted[2 * TOK:, :], up_h, j)

    def behind(h, made, wide_parts):
        j, group = h // 2, h % 2
        cols = slice(j * HEAD, (j + 1) * HEAD)
        up_h, (query, grad, keys, prob, dscore) = made
        sums(keys, dscore, up_h, (2 + group) * TOK, group * five + j)
        parts = (dot(dscore, query, 1, 0), dot(prob, grad, 1, 0))
        for n, part in enumerate(parts):
            if group == 0:
                keep_down[n, :, cols] = part[TOK:2 * TOK].astype(BF16)
                keep_a[n, 0, :, cols] = part[2 * TOK:3 * TOK]
                keep_b[n, 0, :, cols] = part[3 * TOK:]
            else:
                keep_down[2 + n, :, cols] = jnp.where(masks.wide_below, wide_parts[n], part[:TOK]).astype(BF16)
                keep_a[n, 1, :, cols] = part[TOK:2 * TOK]
                keep_b[n, 1, :, cols] = part[2 * TOK:3 * TOK]
                keep_up[n, :, cols] = part[3 * TOK:].astype(BF16)
        if group == 0:
            return [part[:TOK] for part in parts]
        span = pl.ds(j * HEAD, HEAD)
        for n, (x, y) in enumerate(((keep_down, ret_down), (keep_up, ret_up), (keep_a, sum_a), (keep_b, sum_b))):
            at = (slice(None),) * (len(x.shape) - 1) + (span,)
            stores.append(pltpu.make_async_copy(x.at[at], y.at[at], sem_out.at[j, n]))
            stores[-1].start()
        return None

    raw, made, kept = {}, {}, None
    for h in range(2 * five + 2):
        if h < 2 * five:
            raw[h] = ahead(h)
        if 0 < h <= 2 * five:
            up_h, rest = raw.pop(h - 1)
            made[h - 1] = up_h, rest()
        if h > 1:
            kept = behind(h - 2, made.pop(h - 2), kept)

    terms = []
    for n, act in enumerate(acts):
        whole = agrad_t[:, n * TOK:(n + 1) * TOK]
        high = whole.astype(BF16)
        low = (whole - high.astype(F32)).astype(BF16)
        terms.append(dot(high, act, 1, 0) + dot(low, act, 1, 0))
    blank = jnp.zeros((RANK, HEAD), F32)
    for s in range(4):
        pay[:, 2 * five + s, :] = functools.reduce(
            jnp.add, [jnp.where(robot == s, term, blank) for robot, term in zip(masks.robots, terms)]
        )
    payload[...] = pay[...].astype(BF16)
    for store in stores:
        store.wait()


def attend(scalars, adapters, near, oth, below, above, stored, up):
    half = up.shape[1] // 2
    quarter = half // 2
    five = quarter // HEAD
    shapes = [((4, TOK, quarter), BF16), ((2, TOK, quarter), BF16)]
    sums = ((2, 2, TOK, quarter), F32)
    return pl.pallas_call(
        functools.partial(attend_kernel, scalars[1].shape[0]),
        in_specs=[smem()] * 3 + [vmem()] * 11 + [hbm()],
        out_specs=[vmem()] + [hbm()] * 4,
        out_shape=[jax.ShapeDtypeStruct((RANK, ROWS, HEAD), BF16)] + [pltpu.HBM(*x) for x in (sums, sums, *shapes)],
        scratch_shapes=[
            pltpu.VMEM((RANK, half), BF16),
            pltpu.VMEM((3 * TOK, RANK), BF16),
            pltpu.VMEM((RANK, 3 * TOK), BF16),
            pltpu.VMEM((RANK, 3 * TOK), F32),
            pltpu.VMEM((RANK, ROWS, HEAD), F32),
            pltpu.VMEM(*sums),
            pltpu.VMEM(*sums),
            pltpu.VMEM(*shapes[0]),
            pltpu.VMEM(*shapes[1]),
            pltpu.SemaphoreType.DMA((1,)),
            pltpu.SemaphoreType.DMA((five, 4)),
        ],
        compiler_params=pltpu.CompilerParams(vmem_limit_bytes=24 * MIB),
        cost_estimate=pl.CostEstimate(
            flops=2 * five * 12 * 512 * 256 * 128, bytes_accessed=12 * MIB, transcendentals=five * 1024 * 256
        ),
        name="attend",
    )(*scalars, adapters, near, oth, below, above, *stored, fixed(up))


def hold_kernel(held_in, after, held_out):
    pass


def hold(held, after):
    return pl.pallas_call(
        hold_kernel,
        in_specs=[hbm()] * 2,
        out_specs=hbm(),
        out_shape=pltpu.HBM(held.shape, held.dtype),
        input_output_aliases={0: 0},
        compiler_params=pltpu.CompilerParams(vmem_limit_bytes=MIB),
        cost_estimate=pl.CostEstimate(flops=MIB, bytes_accessed=MIB, transcendentals=0),
        name="hold",
    )(fixed(held), after)


def join_kernel(
    clips, place, lengths, robots, sum_a_hbm, sum_b_hbm, above, below, mine, theirs, sum_a, sum_b, sems
):
    loads = [
        pltpu.make_async_copy(x.at[n], y.at[n], sems.at[2 * m + n])
        for m, (x, y) in enumerate(((sum_a_hbm, sum_a), (sum_b_hbm, sum_b)))
        for n in range(2)
    ]
    for load in loads:
        load.start()
    first = place[0] == 0
    frame_a = 2 * place[1]
    start_n, _ = clip_of(frame_a + 2, lengths, robots, clips)
    wide = start_n == frame_a
    quarter = above.shape[2]
    for n in range(2):
        loads[n].wait()
        loads[2 + n].wait()
        for group in range(2):
            second = above[2 + n].astype(F32)
            if group == 0:
                a = sum_a[n, 0] + jnp.where(wide, second, 0.0)
                b = sum_b[n, 0] + above[n].astype(F32)
            else:
                a = sum_a[n, 1] + below[n].astype(F32)
                b = sum_b[n, 1] + jnp.where(wide, 0.0, second)
            cols = slice(group * quarter, (group + 1) * quarter)
            mine[n, :, cols] = jnp.where(first, a, b).astype(BF16)
            theirs[n, :, cols] = jnp.where(first, b, a).astype(BF16)


def join(scalars, sum_a, sum_b, above, below):
    shape = (2, TOK, 2 * above.shape[2])
    return pl.pallas_call(
        functools.partial(join_kernel, scalars[1].shape[0]),
        in_specs=[smem()] * 3 + [hbm()] * 2 + [vmem()] * 2,
        out_specs=[vmem()] * 2,
        out_shape=[pltpu.VMEM(shape, BF16), pltpu.VMEM(shape, BF16)],
        scratch_shapes=[
            pltpu.VMEM(sum_a.shape, F32), pltpu.VMEM(sum_b.shape, F32), pltpu.SemaphoreType.DMA((4,))
        ],
        compiler_params=pltpu.CompilerParams(vmem_limit_bytes=8 * MIB),
        cost_estimate=pl.CostEstimate(flops=MIB, bytes_accessed=6 * MIB, transcendentals=0),
        name="join",
    )(*scalars, fixed(sum_a), fixed(sum_b), above, below)


def place_kernel(place, mine, other, key_grad, value_grad, sems):
    half = mine.shape[2]
    copies = []
    for n, out in enumerate((key_grad, value_grad)):
        for side, source in ((place[0], mine), (1 - place[0], other)):
            cols = pl.ds(pl.multiple_of(side * half, HEAD), half)
            copies.append(pltpu.make_async_copy(source.at[n], out.at[:, cols], sems.at[len(copies)]))
    for copy in copies:
        copy.start()
    for copy in copies:
        copy.wait()


def place_halves(place, mine, other):
    shape = (TOK, 2 * mine.shape[2])
    return pl.pallas_call(
        place_kernel,
        in_specs=[smem()] + [vmem()] * 2,
        out_specs=[hbm()] * 2,
        out_shape=[pltpu.HBM(shape, BF16), pltpu.HBM(shape, BF16)],
        scratch_shapes=[pltpu.SemaphoreType.DMA((4,))],
        compiler_params=pltpu.CompilerParams(vmem_limit_bytes=4 * MIB),
        cost_estimate=pl.CostEstimate(flops=0, bytes_accessed=4 * MIB, transcendentals=0),
        name="place_halves",
    )(place, mine, other)


def first_sum_kernel(pieces, out):
    total = functools.reduce(jnp.add, [pieces[n].astype(F32) for n in range(pieces.shape[0])]).astype(BF16)
    for n in range(out.shape[0]):
        out[n] = total


def first_sum(pieces, peers):
    return pl.pallas_call(
        first_sum_kernel,
        in_specs=[vmem()],
        out_specs=vmem(),
        out_shape=pltpu.VMEM((peers,) + pieces.shape[1:], BF16),
        compiler_params=pltpu.CompilerParams(vmem_limit_bytes=2 * MIB),
        name="first_sum",
    )(pieces)


def second_sum_kernel(up_rows, where, pieces, out):
    everything = functools.reduce(jnp.add, [pieces[n].astype(F32) for n in range(pieces.shape[0])])
    is_up = lax.broadcasted_iota(jnp.int32, everything.shape, 0) % ROWS < up_rows
    message = jnp.where(is_up, everything, pieces[where[0]].astype(F32)).astype(BF16)
    for n in range(out.shape[0]):
        out[n] = message


def second_sum(where, pieces, peers, up_rows):
    return pl.pallas_call(
        functools.partial(second_sum_kernel, up_rows),
        in_specs=[smem(), vmem()],
        out_specs=vmem(),
        out_shape=pltpu.VMEM((peers,) + pieces.shape[1:], BF16),
        compiler_params=pltpu.CompilerParams(vmem_limit_bytes=2 * MIB),
        name="second_sum",
    )(where, pieces)


def finish_kernel(heads, place, gathered, swapped, up_grad, adapter_grad, one, two):
    per_core = heads // 2
    one[...] = gathered[...].astype(F32)
    two[...] = swapped[...].astype(F32)
    for n, part in enumerate((one, two)):
        side = place[0] if n == 0 else 1 - place[0]
        for h in range(per_core):
            cols = pl.ds(pl.multiple_of((side * per_core + h) * HEAD, HEAD), HEAD)
            up_grad[:, cols] = part[:, h, :]
    for s in range(4):
        adapter_grad[s] = one[:, per_core + s, :] + two[:, per_core + s, :]


def finish(place, gathered, swapped, heads):
    return pl.pallas_call(
        functools.partial(finish_kernel, heads),
        in_specs=[smem(), vmem(), vmem()],
        out_specs=[vmem(), vmem()],
        out_shape=[
            jax.ShapeDtypeStruct((RANK, heads * HEAD), F32),
            jax.ShapeDtypeStruct((4, RANK, HEAD), F32),
        ],
        scratch_shapes=[pltpu.VMEM((RANK, ROWS, HEAD), F32), pltpu.VMEM((RANK, ROWS, HEAD), F32)],
        compiler_params=pltpu.CompilerParams(vmem_limit_bytes=6 * MIB),
        name="finish",
    )(place, gathered, swapped)


def local(
    query_tokens, key_tokens, value_tokens, out_grad, actions, clip_lengths, clip_robots, adapters, up_proj,
):
    q, k, v, g = (t[0, 0] for t in (query_tokens, key_tokens, value_tokens, out_grad))
    act = actions[0, 0]
    heads = q.shape[1] // HEAD
    core = lax.axis_index("core")
    nz, ny = lax.axis_size("z"), lax.axis_size("y")
    chips = lax.axis_size("x") * nz
    chip = lax.axis_index("x") * nz + lax.axis_index("z")
    chain = ("x", "z")
    swap = [(0, 1), (1, 0)]
    upward = [(c, c + 1) for c in range(chips - 1)]
    downward = [(c + 1, c) for c in range(chips - 1)]
    place = jnp.stack([core, chip]).astype(jnp.int32)
    scalars = (place, clip_lengths[0, 0], clip_robots[0, 0])
    own = (q, g, k, v)
    oth = lax.ppermute(take_half(place, own, act, True), "core", swap)
    near = take_half(place, own, act, False)
    up_msg, down_msg = pack(scalars, near, oth)
    below = lax.ppermute(up_msg, chain, upward)
    above = lax.ppermute(down_msg, chain, downward)
    table = jnp.swapaxes(adapters[0], 1, 2)
    stored = own_scores(scalars, table, near, oth, up_proj)
    payload, sum_a, sum_b, ret_down, ret_up = attend(
        scalars, table, near, oth, below, above, stored, up_proj
    )
    ret_down, ret_up = hold(ret_down, payload), hold(ret_up, payload)

    plane = ("dp", "x", "z")
    peers = lax.axis_size(plane)
    share = (peers, RANK // peers * ROWS, HEAD)
    pieces = lax.all_to_all(payload.reshape(share), plane, 0, 0, tiled=True)
    message = first_sum(pieces, ny)
    pieces = lax.all_to_all(message, "y", 0, 0, tiled=True)
    row = lax.axis_index("y").astype(jnp.int32).reshape(1)
    message = second_sum(row, pieces, peers, heads // 2)
    gathered = lax.all_to_all(message, plane, 0, 0, tiled=True).reshape(RANK, ROWS, HEAD)
    swapped = lax.ppermute(gathered, "core", swap)
    from_above = lax.ppermute(ret_down, chain, downward)
    from_below = lax.ppermute(ret_up, chain, upward)
    up_total, adapter_total = finish(place, gathered, swapped, heads)
    adapter_total = jnp.swapaxes(adapter_total, 1, 2)
    mine, theirs = join(scalars, sum_a, sum_b, from_above, from_below)
    key_grad, value_grad = place_halves(place, mine, lax.ppermute(theirs, "core", swap))
    return key_grad[None, None], value_grad[None, None], adapter_total[None], up_total


def solution(mesh):
    sizes = dict(mesh.shape)
    wide = Mesh(
        mesh.devices.reshape(sizes["dp"], 2, sizes["context"] // 4, 2, sizes["embodime"]),
        ("dp", "x", "z", "core", "y"),
    )
    frames = P("dp", "y", ("x", "z", "core"), None)
    rows = P("dp", "y", None)
    return jax.shard_map(
        local,
        mesh=wide,
        in_specs=(frames,) * 5 + (rows, rows, P("y", None, None, None), P()),
        out_specs=(frames, frames, P("y", None, None, None), P()),
        check_vma=False,
    )
```
